32 devices in a mesh: dp: 16 (over z, y, x), mp: 2 (over core).
Axes of the slice: x: 2, y: 2, z: 4, core: 2. Of those that a mesh axis runs over, the one named last changes fastest.
Arguments:
- tokens: bfloat16 [64, 144, 512], P(('dp', 'mp')), may hold values from -6 to 6
- cotangent: bfloat16 [64, 144, 512], P(('dp', 'mp')), may hold values from -6 to 6
- region_ids: int32 [64, 144], P(('dp', 'mp')), may hold values from 0 to 3
- rel_bucket: int32 [144, 144], replicated, may hold values from 0 to 758
- norm_gain: float32 [512], replicated, may hold values from 0.5 to 1.5
- in_weight: bfloat16 [512, 1536], P('mp'), may hold values from -0.25 to 0.25
- out_weight: bfloat16 [512, 512], P('mp'), may hold values from -0.25 to 0.25
- bias_table: float32 [8, 759], replicated, may hold values from -3 to 250
- in_error: float32 [16, 512, 1536], P('dp', 'mp'), may hold values from -12 to 12
- out_error: float32 [16, 512, 512], P('dp', 'mp'), may hold values from -6 to 6
- in_basis: float32 [2, 1536, 32], P('mp'), may hold values from -6 to 6
- out_basis: float32 [2, 512, 32], P('mp'), may hold values from -6 to 6
Outputs:
- token_grad: bfloat16 [64, 144, 512], P(('dp', 'mp'))
- gain_grad: float32 [512], replicated
- table_grad: float32 [8, 759], replicated
- in_update: float32 [512, 1536], P('mp')
- out_update: float32 [512, 512], P('mp')
- in_new_error: float32 [16, 512, 1536], P('dp', 'mp')
- out_new_error: float32 [16, 512, 512], P('dp', 'mp')
- in_new_basis: float32 [2, 1536, 32], P('mp')
- out_new_basis: float32 [2, 512, 32], P('mp')
The draws below stay inside these ranges and needn't reach their ends.
All inputs are finite; a program needn't handle non-finite values.
Results may differ from the reference program's by a relative error of at most 0.024.
Values may be sent and summed in bfloat16 or wider, within the bound.
No kernel may reach another device: no remote copies, remote signals or barrier semaphores. Data moves between devices by JAX's collectives and lax.ppermute only.
A program may use at most 64 MiB of HBM per device.

```python
import jax
import jax.numpy as jnp
from jax import lax

D = 512
HEADS = 8
RANK = 32
WIN_DEV = 2
WT = 144
BUCKETS = 759
WINDOWS = 64
N_DP = 16
N_MP = 2


def draw_bias_table(key, part):
    key = jax.random.fold_in(key, 7)
    base_key = jax.random.fold_in(key, 0)
    values = jnp.clip(jax.random.normal(base_key, (HEADS, BUCKETS), jnp.float32), -3.0, 3.0)
    return values


def place_ends(entries, key, smallest, largest):
    longest = entries.shape.index(max(entries.shape))
    spots = []
    for shift in (0, 1):
        where = [jax.random.randint(jax.random.fold_in(key, axis), (), 0, length) for axis, length in enumerate(entries.shape)]
        where[longest] = (where[longest] + shift) % entries.shape[longest]
        spots.append(tuple(where))
    return entries.at[spots[0]].set(smallest).at[spots[1]].set(largest)


def block_scale(rng, shape, cuts, smallest, high):
    level, own = 1.0, jax.random.fold_in(rng, 6)
    for axis_at, blocks in cuts:
        heights = jnp.exp(jax.random.uniform(jax.random.fold_in(own, axis_at), (blocks,), jnp.float32, smallest / len(cuts), high / len(cuts)))
        level = level * jnp.repeat(heights, shape[axis_at] // blocks).reshape([-1 if axis == axis_at else 1 for axis in range(len(shape))])
    return level


def gaussian(stream_key, shape, spread, reach, shards=(), held_as=jnp.bfloat16):
    drawn = spread * jax.random.normal(stream_key, shape, jnp.float32)
    if shards:
        drawn = drawn * block_scale(stream_key, shape, shards, -0.22, 0.18)
    return jnp.clip(drawn, -reach, reach).astype(held_as)


def setup_inputs(seed: int = 0) -> dict:
    key_list = jax.random.split(jax.random.key(seed), 13)
    return {
        "tokens": gaussian(key_list[0], (WINDOWS, WT, D), 1.0, 6.0, ((0, 32),)),
        "cotangent": gaussian(key_list[1], (WINDOWS, WT, D), 1.0, 6.0, ((0, 32),)),
        "region_ids": place_ends(jax.random.randint(key_list[2], (WINDOWS, WT), 0, 4), jax.random.fold_in(key_list[2], 1), 0, 3).astype(jnp.int32),
        "rel_bucket": place_ends(jax.random.randint(key_list[3], (WT, WT), 0, BUCKETS), jax.random.fold_in(key_list[3], 1), 0, BUCKETS - 1).astype(jnp.int32),
        "norm_gain": jnp.clip(1.0 + 0.1 * jax.random.normal(key_list[4], (D,), jnp.float32), 0.5, 1.5),
        "in_weight": gaussian(key_list[5], (D, 3 * D), D ** -0.5, 0.25, ((0, 2),)),
        "out_weight": gaussian(key_list[6], (D, D), D ** -0.5, 0.25, ((0, 2),)),
        "bias_table": draw_bias_table(jax.random.fold_in(key_list[12], 71), 0),
        "in_error": gaussian(key_list[8], (N_DP, D, 3 * D), 2.0, 12.0, ((0, 16), (1, 2)), jnp.float32),
        "out_error": gaussian(key_list[9], (N_DP, D, D), 1.0, 6.0, ((0, 16), (1, 2)), jnp.float32),
        "in_basis": gaussian(key_list[10], (N_MP, 3 * D, RANK), 1.0, 6.0, ((0, 2),), jnp.float32),
        "out_basis": gaussian(key_list[11], (N_MP, D, RANK), 1.0, 6.0, ((0, 2),), jnp.float32),
    }


NORM_EPS = 1e-05
BASIS_EPS = 1e-06
MASKED = -1e+30
HIGH = lax.Precision.HIGHEST

def norm_forward(token_rows):
    tokens_wide = token_rows.astype(jnp.float32)
    mean_x = lax.optimization_barrier(jnp.mean(tokens_wide, axis=-1, keepdims=True))
    centered = tokens_wide - mean_x
    variance = lax.optimization_barrier(jnp.mean(centered * centered, axis=-1, keepdims=True))
    inv_sigma = lax.rsqrt(variance + NORM_EPS)
    return (centered * inv_sigma, inv_sigma)

def orthonormal(left_factor):

    def next_column(j, finished):
        j = j.astype(jnp.int32)
        column = lax.dynamic_slice_in_dim(left_factor, j, 1, 1)
        for repeat in range(2):
            column = column - jnp.dot(finished, jnp.dot(finished.T, column, precision=HIGH), precision=HIGH)
        column = column * lax.rsqrt(jnp.sum(column * column) + BASIS_EPS)
        return lax.dynamic_update_slice_in_dim(finished, column, j, 1)
    return lax.fori_loop(0, left_factor.shape[1], next_column, jnp.zeros_like(left_factor))

def layer_grads(tokens, cotangent, region_ids, rel_bucket, norm_gain, in_weight, out_weight, bias_table):
    window_count, win_span, feature_count = tokens.shape
    head_count = bias_table.shape[0]
    head_size = feature_count // head_count
    row_count = window_count * win_span
    score_scale = head_size ** (-0.5)
    f32 = jnp.float32
    x_hat, inv_sigma = norm_forward(tokens.reshape(row_count, feature_count))
    normed = (x_hat * norm_gain).astype(jnp.bfloat16)
    projected = jnp.dot(normed, in_weight, preferred_element_type=f32).astype(jnp.bfloat16)
    projected = projected.reshape(window_count, win_span, 3, head_count, head_size)
    queries = projected[:, :, 0].astype(f32)
    key_rows = projected[:, :, 1].astype(f32)
    value_rows = projected[:, :, 2].astype(f32)
    pos_bias = jnp.take(bias_table, rel_bucket, axis=1)
    allowed = region_ids[:, :, None] == region_ids[:, None, :]
    scores = jnp.einsum('wihd,wjhd->whij', queries, key_rows) * score_scale + pos_bias[None]
    scores = jnp.where(allowed[:, None], scores, MASKED)
    row_top = lax.optimization_barrier(jnp.max(scores, axis=-1, keepdims=True))
    exp_scores = jnp.exp(scores - row_top)
    attn_prob = exp_scores / lax.optimization_barrier(jnp.sum(exp_scores, axis=-1, keepdims=True))
    prob_b = attn_prob.astype(jnp.bfloat16)
    mixed_out = jnp.einsum('whij,wjhd->wihd', prob_b.astype(f32), value_rows).astype(jnp.bfloat16)
    mixed_out = mixed_out.reshape(row_count, feature_count)
    cot_rows = cotangent.reshape(row_count, feature_count)
    out_term = jnp.dot(mixed_out.T, cot_rows, preferred_element_type=f32)
    mixed_grad = jnp.dot(cot_rows, out_weight.T, preferred_element_type=f32).astype(jnp.bfloat16)
    mixed_grad = mixed_grad.reshape(window_count, win_span, head_count, head_size).astype(f32)
    prob_grad = jnp.einsum('wihd,wjhd->whij', mixed_grad, value_rows)
    value_grad = jnp.einsum('whij,wihd->wjhd', prob_b.astype(f32), mixed_grad)
    score_grad = attn_prob * (prob_grad - lax.optimization_barrier(jnp.sum(attn_prob * prob_grad, axis=-1, keepdims=True)))
    score_sum = lax.optimization_barrier(jnp.sum(score_grad, axis=0)).reshape(head_count, win_span * win_span)
    table_term = jax.ops.segment_sum(score_sum.T, rel_bucket.reshape(-1), num_segments=bias_table.shape[1]).T
    score_b = score_grad.astype(jnp.bfloat16).astype(f32)
    query_grad = jnp.einsum('whij,wjhd->wihd', score_b, key_rows) * score_scale
    key_grad = jnp.einsum('whij,wihd->wjhd', score_b, queries) * score_scale
    packed_grad = jnp.stack([query_grad, key_grad, value_grad], axis=2).astype(jnp.bfloat16)
    packed_grad = packed_grad.reshape(row_count, 3 * feature_count)
    in_term = jnp.dot(normed.T, packed_grad, preferred_element_type=f32)
    normed_grad = jnp.dot(packed_grad, in_weight.T, preferred_element_type=f32)
    gain_term = lax.optimization_barrier(jnp.sum(normed_grad * x_hat, axis=0))
    hat_grad = normed_grad * norm_gain
    token_delta = inv_sigma * (hat_grad - lax.optimization_barrier(jnp.mean(hat_grad, axis=-1, keepdims=True)) - x_hat * lax.optimization_barrier(jnp.mean(hat_grad * x_hat, axis=-1, keepdims=True)))
    token_grad = (cot_rows.astype(f32) + token_delta).astype(jnp.bfloat16).reshape(tokens.shape)
    return (token_grad, in_term, out_term, gain_term, table_term)

def compress(group_grad, error, basis):
    row_block = group_grad.shape[1] // N_MP
    merged = (group_grad + error).reshape(N_DP, N_MP, row_block, group_grad.shape[2])
    left_factor = jnp.einsum('amrc,mck->mrk', merged, basis, precision=HIGH) / N_DP
    left_basis = jax.vmap(orthonormal)(left_factor)
    right_factor = jnp.einsum('amrc,mrk->mck', merged, left_basis, precision=HIGH) / N_DP
    update = jnp.einsum('mrk,mck->mrc', left_basis, right_factor, precision=HIGH)
    new_error = merged - update[None]
    return (update.reshape(group_grad.shape[1], group_grad.shape[2]), new_error.reshape(group_grad.shape), right_factor)

def reference(tokens, cotangent, region_ids, rel_bucket, norm_gain, in_weight, out_weight, bias_table, in_error, out_error, in_basis, out_basis):

    def blocks_of(array):
        return array.reshape((N_DP, N_MP, WIN_DEV) + array.shape[1:])

    def per_device(block):
        token_grad, in_term, out_term, gain_term, table_term = layer_grads(block[0], block[1], block[2], rel_bucket, norm_gain, in_weight, out_weight, bias_table)
        return (token_grad, in_term.astype(jnp.bfloat16), out_term.astype(jnp.bfloat16), gain_term, table_term)

    def worker(block):
        token_grad, in_terms, out_terms, gain_terms, table_terms = lax.map(per_device, block)
        in_terms = lax.optimization_barrier(in_terms)
        out_terms = lax.optimization_barrier(out_terms)
        in_group = lax.optimization_barrier(jnp.sum(in_terms.astype(jnp.float32), axis=0)) / N_MP
        out_group = lax.optimization_barrier(jnp.sum(out_terms.astype(jnp.float32), axis=0)) / N_MP
        return (token_grad, in_group, out_group, lax.optimization_barrier(jnp.sum(gain_terms, axis=0)), lax.optimization_barrier(jnp.sum(table_terms, axis=0)))
    token_grad, in_group, out_group, gain_parts, table_parts = lax.map(worker, (blocks_of(tokens), blocks_of(cotangent), blocks_of(region_ids)))
    devices = N_DP * N_MP
    gain_grad = lax.optimization_barrier(jnp.sum(gain_parts, axis=0)) / devices
    table_grad = lax.optimization_barrier(jnp.sum(table_parts, axis=0)) / devices
    in_update, in_new_error, in_new_basis = compress(in_group, in_error, in_basis)
    out_update, out_new_error, out_new_basis = compress(out_group, out_error, out_basis)
    return (token_grad.reshape(tokens.shape), gain_grad, table_grad, in_update, out_update, in_new_error, out_new_error, in_new_basis, out_new_basis)
```

```python
import functools

import jax
import jax.numpy as jnp
from jax import lax
from jax.experimental import pallas as pl
from jax.experimental.pallas import tpu as pltpu
from jax.sharding import PartitionSpec as P

NORM_EPS = 1e-05
BASIS_EPS = 1e-06
MASKED = -1e30
LANES = 128
SUBLANES = 8
READY_HEADS = 2
F32 = jnp.float32
BF16 = jnp.bfloat16

VMEM = pl.BlockSpec(memory_space=pltpu.VMEM)
SMEM = pl.BlockSpec(memory_space=pltpu.SMEM)
HBM = pl.BlockSpec(memory_space=pltpu.HBM)
ANY = pl.BlockSpec(memory_space=pl.ANY)


def nn(a, b):
    return lax.dot_general(
        a, b, (((1,), (0,)), ((), ())), preferred_element_type=F32
    )


def nt(a, b):
    return lax.dot_general(
        a, b, (((1,), (1,)), ((), ())), preferred_element_type=F32
    )


def tn(a, b):
    return lax.dot_general(
        a, b, (((0,), (0,)), ((), ())), preferred_element_type=F32
    )


def block_columns(me, step, blocks, width):
    if blocks == 1:
        return pl.ds(0, width)
    index = me if step == 0 else 1 - me
    return pl.ds(pl.multiple_of(index * width, width), width)


def norm_forward(token_rows):
    tokens_wide = token_rows.astype(F32)
    mean_x = jnp.mean(tokens_wide, axis=-1, keepdims=True)
    centered = tokens_wide - mean_x
    variance = jnp.mean(centered * centered, axis=-1, keepdims=True)
    inv_sigma = lax.rsqrt(variance + NORM_EPS)
    return (centered * inv_sigma, inv_sigma)


def fetch(pairs, sems):
    copies = [
        pltpu.make_async_copy(source, target, sems.at[at])
        for at, (source, target) in enumerate(pairs)
    ]
    for copy in copies:
        copy.start()
    return copies


def halves(value):
    coarse = value.astype(BF16)
    return coarse, (value - coarse.astype(F32)).astype(BF16)


def stacked(value):
    return jnp.concatenate(halves(value), axis=0)


def folded(value):
    half = value.shape[0] // 2
    return value[:half] + value[half:]


def gather_bias(bias, heads, table_pad, index_t, index):
    span = index.shape[0]
    padded = table_pad.shape[1]
    even = span // LANES * LANES
    lookups = [(index_t[:, :even], False)] if even else []
    if even < span:
        lookups.append((index[even:, :], True))
    for places, flipped in lookups:
        rows, columns = places.shape
        for start in range(0, columns, LANES):
            stop = min(columns, start + LANES)
            part = places[:, start:stop]
            if stop - start < LANES:
                filler = jnp.zeros((rows, LANES - (stop - start)), jnp.int32)
                part = jnp.concatenate([part, filler], axis=1)
            high, low = part // LANES, part % LANES
            for head in heads:
                found = jnp.zeros((rows, LANES), F32)
                for level in range(padded // LANES):
                    row = table_pad[head : head + 1, level * LANES : (level + 1) * LANES]
                    row = jnp.broadcast_to(row, (rows, LANES))
                    picked = jnp.take_along_axis(row, low, axis=1, mode="promise_in_bounds")
                    found = jnp.where(high == level, picked, found)
                if flipped:
                    bias[head, start:stop, even:] = found[:, : stop - start].T
                else:
                    bias[head, :, start:stop] = found[:, : stop - start]


def prepare_kernel(blocks, ready, me_ref, *refs):
    sources, rest = refs[:12], refs[12:]
    normed, part, bias, index_t, table_pad, bucket, *kept = rest[:16]
    table, sems = rest[16:]
    copies = fetch(list(zip(sources, [bucket, table] + kept)), sems)
    tokens, gain, w_own = kept[:3]
    me = me_ref[0]
    width = w_own.shape[0]
    span = bucket.shape[0]
    head_count, padded = table_pad.shape
    for copy in copies[:2]:
        copy.wait()
    table_pad[...] = jnp.zeros_like(table_pad)
    table_pad[:, : table.shape[1]] = table[...]
    index_t[...] = bucket[...].T
    gather_bias(bias, range(ready), table_pad, index_t, bucket)
    for copy in copies[2:5]:
        copy.wait()
    x_hat, _ = norm_forward(tokens[...])
    normed[...] = (x_hat * gain[...]).astype(BF16)
    part[...] = nn(normed[:, block_columns(me, 0, blocks, width)], w_own[...])
    for copy in copies[5:]:
        copy.wait()


def attend_kernel(blocks, share, *refs):
    me_ref, normed, part, bias_ready, index_t, table_pad, bucket, gain, cot, region = refs[:10]
    own, arrived = refs[10:14], refs[14 : 10 + 4 * blocks]
    rest = refs[10 + 4 * blocks :]
    terms, lefts, rest = rest[:blocks], rest[blocks : 2 * blocks], rest[2 * blocks :]
    score_parts, (packed, gain_term), rest = rest[:blocks], rest[blocks : blocks + 2], rest[blocks + 2 :]
    proj, mixed_grad, mixed, score_sum, gain_row, bias = rest
    w_in, w_out, in_basis, out_basis = (
        [own[at]] + list(arrived[at : at + blocks - 1]) for at in range(4)
    )
    me = me_ref[0]
    window_count, span = region.shape
    features = normed.shape[1]
    ready, head_count = bias_ready.shape[0], bias.shape[0]
    head_size = features // head_count
    scale = head_size ** (-0.5)
    width = features // blocks
    if blocks == 1:
        proj[...] = part[...].astype(BF16)
    else:
        other = nn(normed[:, block_columns(me, 1, blocks, width)], w_in[1][...])
        proj[...] = (part[...] + other).astype(BF16)
    for step in range(blocks):
        mixed_grad[:, block_columns(me, step, blocks, width)] = nt(
            cot[...], w_out[step][...]
        ).astype(BF16)
    lane = lax.broadcasted_iota(jnp.int32, (span, LANES), 1)
    per_group = LANES // head_size
    for window in range(window_count):
        rows = pl.ds(window * span, span)
        ids_row = jnp.broadcast_to(region[window : window + 1, :], (span, span))
        allowed = ids_row == ids_row.T
        for group in range(features // LANES):
            start = group * LANES
            heads = slice(group * per_group, (group + 1) * per_group)
            if heads.stop <= ready:
                pair_bias = bias_ready[heads]
            else:
                if window == 0:
                    gather_bias(bias, range(heads.start, heads.stop), table_pad, index_t, bucket)
                pair_bias = bias[heads]
            q = proj[rows, start : start + LANES]
            k = proj[rows, features + start : features + start + LANES]
            v = proj[rows, 2 * features + start : 2 * features + start + LANES]
            g = mixed_grad[rows, start : start + LANES]
            pick = [lane // head_size == sub for sub in range(per_group)]
            k_split = jnp.concatenate([jnp.where(own, k, jnp.zeros_like(k)) for own in pick], 0)
            v_split = jnp.concatenate([jnp.where(own, v, jnp.zeros_like(v)) for own in pick], 0)
            scores = nt(k_split, q).reshape(per_group, span, span) * scale + pair_bias
            scores = jnp.where(allowed[None], scores, MASKED)
            top = jnp.max(scores, axis=1, keepdims=True)
            raised = jnp.exp(scores - top)
            prob = raised * (1.0 / jnp.sum(raised, axis=1, keepdims=True))
            prob_b = prob.astype(BF16)
            prob_grad = nt(v_split, g).reshape(per_group, span, span)
            inner = jnp.sum(prob * prob_grad, axis=1, keepdims=True)
            score_grad = prob * (prob_grad - inner)
            score_b = score_grad.astype(BF16)
            if window == 0:
                score_sum[heads] = score_grad
            else:
                score_sum[heads] += score_grad
            k_grads = nn(score_b.reshape(per_group * span, span), q)
            v_grads = nn(prob_b.reshape(per_group * span, span), g)

            def joined(parts):
                total = parts[0]
                for sub in range(1, per_group):
                    total = jnp.where(pick[sub], parts[sub], total)
                return total

            k_grad = joined([k_grads[at * span : (at + 1) * span] for at in range(per_group)])
            v_grad = joined([v_grads[at * span : (at + 1) * span] for at in range(per_group)])
            out = joined([tn(prob_b[at], v) for at in range(per_group)])
            q_grad = joined([tn(score_b[at], k) for at in range(per_group)])
            mixed[rows, start : start + LANES] = out.astype(BF16)
            packed[rows, start : start + LANES] = (q_grad * scale).astype(BF16)
            packed[rows, features + start : features + start + LANES] = (k_grad * scale).astype(
                BF16
            )
            packed[rows, 2 * features + start : 2 * features + start + LANES] = v_grad.astype(BF16)
    wide = 3 * features
    for step in range(blocks):
        columns = block_columns(me, step, blocks, width)
        product = tn(normed[:, columns], packed[...])
        terms[step][:, :wide] = product.astype(BF16)
        terms[step][:, wide:] = tn(mixed[:, columns], cot[...]).astype(BF16)
        weighted = product * w_in[step][...].astype(F32)
        folds = tree_add(
            [weighted[:, start : start + LANES] for start in range(0, wide, LANES)]
        )
        gain_row[:, columns] = jnp.sum(folds.T, axis=0, keepdims=True) / gain[:, columns]
        rank = in_basis[step].shape[0]
        for basis, at, place in (
            (in_basis[step], slice(None, wide), 0),
            (out_basis[step], slice(wide, None), rank),
        ):
            left = folded(nt(stacked(basis[...]), terms[step][:, at])) * share
            lefts[step][place : place + rank, :] = left
    gain_term[...] = jnp.zeros_like(gain_term)
    for piece in range(features // LANES):
        gain_term[piece : piece + 1, :] = gain_row[:, piece * LANES : (piece + 1) * LANES]
    rows = span // blocks
    for step in range(blocks):
        score_parts[step][...] = score_sum[:, block_columns(me, step, blocks, rows), :]


def token_kernel(blocks, me_ref, packed, *refs):
    w_in, (tokens, cot, gain, _, result, flag, normed_grad, token_grad, sems) = (
        refs[:blocks],
        refs[blocks:],
    )
    me = me_ref[0]
    width = tokens.shape[1] // blocks
    for step in range(blocks):
        normed_grad[:, block_columns(me, step, blocks, width)] = nt(packed[...], w_in[step][...])
    x_hat, inv_sigma = norm_forward(tokens[...])
    hat_grad = normed_grad[...] * gain[...]
    token_delta = inv_sigma * (
        hat_grad
        - jnp.mean(hat_grad, axis=-1, keepdims=True)
        - x_hat * jnp.mean(hat_grad * x_hat, axis=-1, keepdims=True)
    )
    token_grad[...] = (cot[...].astype(F32) + token_delta).astype(BF16)
    flag[...] = jnp.zeros_like(flag)
    for copy in fetch([(token_grad, result)], sems):
        copy.wait()


def table_kernel(blocks, me_ref, *refs):
    score_parts, (gain_term, index_t, stats) = refs[:blocks], refs[blocks:]
    head_count, rows, span = score_parts[0].shape
    padded = stats.shape[1] - 2 * LANES
    levels = padded // LANES
    indices = index_t[block_columns(me_ref[0], 0, blocks, rows), :]
    scores = tree_add([part[...] for part in score_parts])
    sublane = lax.broadcasted_iota(jnp.int32, (LANES, span), 0)
    total = jnp.zeros((2 * levels * head_count, LANES), F32)
    for row in range(rows):
        index = indices[row : row + 1, :]
        high = jnp.broadcast_to(index // LANES, (head_count, span))
        low = jnp.broadcast_to(index % LANES, (LANES, span))
        one_hot = jnp.where(low == sublane, 1.0, 0.0).astype(BF16)
        values = scores[:, row, :]
        coarse = values.astype(BF16).astype(F32)
        fine = values - coarse
        picked = [
            jnp.where(high == level, piece, 0.0)
            for piece in (coarse, fine)
            for level in range(levels)
        ]
        total += nt(jnp.concatenate(picked, axis=0).astype(BF16), one_hot)
    total = folded(total)
    for level in range(levels):
        stats[:, level * LANES : (level + 1) * LANES] = total[
            level * head_count : (level + 1) * head_count
        ]
    stats[:, padded : padded + LANES] = gain_term[...]
    stats[:, padded + LANES :] = jnp.zeros((head_count, LANES), F32)


def shard_kernel(share, shard, in_basis, out_basis, left):
    rank, split = in_basis.shape
    left[:rank, :] = folded(nt(stacked(in_basis[...]), shard[:, :split])) * share
    left[rank:, :] = folded(nt(stacked(out_basis[...]), shard[:, split:])) * share


def error_kernel(term_left, in_error, out_error, in_basis, out_basis, left):
    rank = in_basis.shape[0]
    for error, basis, at in ((in_error, in_basis, 0), (out_error, out_basis, rank)):
        coarse, fine = halves(error[...])
        pair = stacked(basis[...])
        left[at : at + rank, :] = term_left[at : at + rank, :] + folded(
            nt(pair, coarse) + nt(pair, fine)
        )


def merge_kernel(share, parts, *refs):
    shards, (in_error, out_error, merged) = refs[:parts], refs[parts:]
    split = in_error.shape[1]
    for columns, error in ((slice(None, split), in_error), (slice(split, None), out_error)):
        total = tree_add([shard[:, columns].astype(F32) for shard in shards])
        merged[:, columns] = total * share + error[...]


def tree_sum(values):
    while len(values) > 1:
        values = [values[at] + values[at + 1] for at in range(0, len(values), 2)]
    return values[0]


def tree_add(values):
    while len(values) > 1:
        odd = values[len(values) // 2 * 2 :]
        values = [values[at] + values[at + 1] for at in range(0, len(values) - 1, 2)] + odd
    return values[0]


def join_kernel(left_own, left_other, *refs):
    left = refs[len(refs) // 2]
    left[...] = left_own[...] + left_other[...]


def add_kernel(parts, *refs):
    refs[-1][...] = tree_sum([ref[...] for ref in refs[:parts]])


def stats_pieces(pair):
    pieces = []
    for at in range(2):
        tile = pair[:, at * LANES : (at + 1) * LANES]
        coarse, fine = halves(tile)
        pieces += [coarse.astype(F32), fine.astype(F32)]
    return jnp.concatenate(pieces, axis=0).astype(BF16)


def stats_pair(pieces):
    rows = pieces.shape[0] // 4
    return jnp.concatenate(
        [
            pieces[2 * at * rows : (2 * at + 1) * rows]
            + pieces[(2 * at + 1) * rows : (2 * at + 2) * rows]
            for at in range(2)
        ],
        axis=1,
    )


def orthonormal(problems):
    rank, rows = problems[0].shape
    tiles = rank // SUBLANES
    spread_shape = (SUBLANES, rows)
    place = lax.broadcasted_iota(jnp.int32, spread_shape, 0)

    def dots(rows_of, vector):
        return jnp.sum(rows_of * vector, axis=1, keepdims=True)

    def spread(tiled, row):
        tile, at = divmod(row, SUBLANES)
        return jnp.broadcast_to(tiled[tile][at : at + 1], spread_shape)

    states = []
    for first in problems:
        original = [first[at * SUBLANES : (at + 1) * SUBLANES] for at in range(tiles)]
        states.append((original, list(original), [jnp.zeros(spread_shape, F32)] * tiles))
    def project(finished, found):
        weighted = tree_add([found[q] * finished[q] for q in found])
        return jnp.sum(weighted, axis=0, keepdims=True)

    currents = [spread(original, 0) for original, _, _ in states]
    known = [None for _ in states]
    for column in range(rank):
        tile, at = divmod(column, SUBLANES)
        before = range((column - 1) // SUBLANES + 1)
        for which, (original, residual, finished) in enumerate(states):
            current = currents[which]
            square = dots(current, current)
            inverse = lax.rsqrt(square + BASIS_EPS)
            unit = current * inverse
            if column + 1 < rank:
                ahead = spread(residual, column + 1)
                step = dots(spread(original, column + 1), current) * inverse
                own = dots(ahead, current) * inverse
                following = ahead - unit * (step + own - step * (square * inverse * inverse))
                if column:
                    cross = project(finished, {q: dots(finished[q], current) for q in before})
                    following = following - known[which] + (step * inverse) * cross
            finished[tile] = jnp.where(place == at, unit, finished[tile])
            if column + 1 < rank:
                for q in range((column + 1) // SUBLANES, tiles):
                    residual[q] = residual[q] - (dots(original[q], current) * inverse) * unit
                currents[which] = following
            if column + 2 < rank:
                far = spread(residual, column + 2)
                known[which] = project(
                    finished, {q: dots(finished[q], far) for q in range(tile + 1)}
                )
    return [jnp.concatenate(finished, axis=0) for _, _, finished in states]


def ortho_kernel(share, parts, stat_parts, me_ref, *refs):
    lefts, stats = refs[:parts], refs[parts : parts + stat_parts]
    merged, ortho, *pieces, sums = refs[parts + stat_parts :]
    digit = me_ref[1]
    rank = ortho.shape[0] // 2
    quarter = merged.shape[1] // len(pieces)
    sums[...] = tree_sum([stat[...] for stat in stats])
    total = tree_sum([left[...] for left in lefts]) * share
    finished = orthonormal([total[:rank], total[rank:]])
    ortho[:rank, :], ortho[rank:, :] = finished
    for step, piece in enumerate(pieces):
        block = jnp.bitwise_xor(digit, step)
        columns = pl.ds(pl.multiple_of(block * quarter, quarter), quarter)
        pair = stacked(jnp.where(block < len(pieces) - 1, finished[0], finished[1]))
        coarse, fine = halves(merged[:, columns])
        piece[:, :quarter] = folded(nn(pair, coarse) + nn(pair, fine)).astype(BF16)
        stat_columns = pl.ds(pl.multiple_of(block * 2 * LANES, 2 * LANES), 2 * LANES)
        piece[:, quarter:] = stats_pieces(sums[:, stat_columns])


def reduce_kernel(*refs):
    pieces, total = refs[:-2], refs[-1]
    quarter = total.shape[1] - LANES
    summed = tree_sum([piece[...].astype(F32) for piece in pieces])
    total[:, :quarter] = summed[:, :quarter].astype(BF16)
    total[:, quarter:] = stats_pieces(stats_pair(summed[:, quarter:]))


def update_kernel(share, stat_share, parts, me_ref, *refs):
    pieces = refs[:parts]
    ortho, merged = refs[parts : parts + 2]
    in_update, out_update, in_new_error, out_new_error = refs[parts + 2 : parts + 6]
    small_results = refs[parts + 6 : parts + 10]
    rights, updates, errors, sems = refs[parts + 10 : parts + 14]
    small = refs[parts + 14 : parts + 18]
    in_basis, out_basis, table, gain = small
    digit = me_ref[1]
    rank = ortho.shape[0] // 2
    quarter = rights.shape[2] - LANES
    for step, piece in enumerate(pieces):
        rights[step] = piece[...].astype(F32)
    copies = []
    tiles = []
    for block in range(parts):
        here = rights[jnp.bitwise_xor(digit, block)]
        right = here[:, :quarter] * share
        tiles.append(stats_pair(here[:, quarter:]) * stat_share)
        is_in = block < parts - 1
        columns = slice(block * quarter, (block + 1) * quarter)
        own = ortho[:rank, :] if is_in else ortho[rank:, :]
        own_coarse, own_fine = halves(own)
        coarse, fine = halves(right)
        update = tn(
            jnp.concatenate([own_coarse, own_coarse, own_fine], axis=0),
            jnp.concatenate([coarse, fine, coarse], axis=0),
        )
        updates[block] = update
        errors[block] = merged[:, columns] - update
        if is_in:
            in_basis[:, columns] = right
            update_to, error_to = in_update.at[:, columns], in_new_error.at[:, columns]
        else:
            out_basis[...] = right
            update_to, error_to = out_update, out_new_error
        copies += fetch(
            [(updates.at[block], update_to), (errors.at[block], error_to)], sems.at[block]
        )
    stats = jnp.concatenate(tiles, axis=1)
    table[...] = stats[:, : table.shape[1]]
    padded = stats.shape[1] - 2 * LANES
    for at in range(gain.shape[1] // LANES):
        gain[:, at * LANES : (at + 1) * LANES] = stats[at : at + 1, padded : padded + LANES]
    copies += fetch(list(zip(small, small_results)), refs[parts + 18])
    for copy in copies:
        copy.wait()


def call(kernel, outs, scratch=(), flops=0, moved=0, vmem=16, **options):
    return pl.pallas_call(
        kernel,
        out_shape=outs,
        scratch_shapes=list(scratch),
        cost_estimate=pl.CostEstimate(flops=flops, bytes_accessed=moved, transcendentals=0),
        compiler_params=pltpu.CompilerParams(vmem_limit_bytes=vmem << 20),
        **options,
    )


def buffers(*arrays):
    return [pltpu.VMEM(array.shape, array.dtype) for array in arrays] + [
        pltpu.SemaphoreType.DMA((len(arrays),))
    ]


def in_hbm(*arrays):
    return [pltpu.with_memory_space_constraint(array, pltpu.HBM) for array in arrays]


def shape(dims, dtype):
    return jax.ShapeDtypeStruct(dims, dtype)


def exchange(value, axis, count, distance):
    return lax.ppermute(value, axis, [(at, at ^ distance) for at in range(count)])


def digits(count):
    groups, stride = [], 1
    while stride < count:
        size = 4 if count // stride % 4 == 0 else 2
        groups.append((stride, size))
        stride *= size
    return groups


def partners(value, axis, count, stride, size):
    return [value] + [exchange(value, axis, count, step * stride) for step in range(1, size)]


def sum_over(value, axis, count):
    for stride, size in digits(count):
        value = tree_sum(partners(value, axis, count, stride, size))
    return value


def shards(
    tokens,
    cotangent,
    region_ids,
    rel_bucket,
    norm_gain,
    in_weight,
    out_weight,
    bias_table,
    in_error,
    out_error,
    in_basis,
    out_basis,
):
    n_dp = lax.axis_size("dp")
    n_mp = lax.axis_size("mp")
    window_count, span, features = tokens.shape
    head_count, buckets = bias_table.shape
    rank = in_basis.shape[2]
    row_count = window_count * span
    row_block = in_weight.shape[0]
    wide = in_weight.shape[1]
    both = wide + features
    padded = -(-buckets // LANES) * LANES
    blocks = 2 if n_mp == 2 else 1
    me = jnp.stack([lax.axis_index("mp"), lax.axis_index("dp") & 3]).astype(jnp.int32)
    token_rows = tokens.reshape(row_count, features)
    cot_rows = cotangent.reshape(row_count, features)
    gain = norm_gain.reshape(1, features)

    in_basis_t = jnp.swapaxes(in_basis[0], 0, 1)
    out_basis_t = jnp.swapaxes(out_basis[0], 0, 1)
    if blocks == 2:
        own = (in_weight, out_weight, in_basis_t, out_basis_t)
        arrived = [exchange(array, "mp", n_mp, 1) for array in own]
    else:
        own = (
            lax.all_gather(in_weight, "mp", axis=0, tiled=True),
            lax.all_gather(out_weight, "mp", axis=0, tiled=True),
            in_basis_t,
            out_basis_t,
        )
        arrived = []
    width = features // blocks

    operands = (
        rel_bucket,
        bias_table,
        token_rows,
        gain,
        own[0],
        cot_rows,
        region_ids,
        *own[1:],
        in_error[0],
        out_error[0],
    )
    normed, part, bias, index_t, table_pad, bucket, *kept = call(
        functools.partial(prepare_kernel, blocks, READY_HEADS),
        (
            shape((row_count, features), BF16),
            shape((row_count, wide), F32),
            shape((READY_HEADS, span, span), F32),
            shape((span, span), jnp.int32),
            shape((head_count, padded), F32),
            shape((span, span), jnp.int32),
        )
        + tuple(shape(array.shape, array.dtype) for array in operands[2:]),
        [pltpu.VMEM(bias_table.shape, F32), pltpu.SemaphoreType.DMA((12,))],
        flops=2 * row_count * width * wide,
        moved=4 << 20,
        in_specs=[SMEM] + [HBM] * 12,
        out_specs=[VMEM] * 16,
    )(me, *in_hbm(*operands))
    token_rows, gain, w_in_own, cot_rows, region, *own, in_errors, out_errors = kept
    in_basis_t, out_basis_t = own[1:]

    left_shape = shape((2 * rank, width), F32)
    outputs = call(
        functools.partial(attend_kernel, blocks, 1.0 / n_mp),
        (shape((width, both), BF16),) * blocks
        + (left_shape,) * blocks
        + (shape((head_count, span // blocks, span), F32),) * blocks
        + (shape((row_count, wide), BF16), shape((SUBLANES, LANES), F32)),
        [
            pltpu.VMEM((row_count, wide), BF16),
            pltpu.VMEM((row_count, features), BF16),
            pltpu.VMEM((row_count, features), BF16),
            pltpu.VMEM((head_count, span, span), F32),
            pltpu.VMEM((1, features), F32),
            pltpu.VMEM((head_count, span, span), F32),
        ],
        flops=4 * row_count * features * both,
        moved=8 << 20,
        in_specs=[SMEM] + [VMEM] * (13 + len(arrived)),
        out_specs=[VMEM] * (3 * blocks + 2),
    )(me, normed, part, bias, index_t, table_pad, bucket, gain, cot_rows, region, w_in_own, *own, *arrived)
    terms, lefts, score_parts = (
        outputs[at * blocks : (at + 1) * blocks] for at in range(3)
    )
    packed, gain_term = outputs[3 * blocks :]

    if blocks == 2:
        left_other = exchange(lefts[1], "mp", n_mp, 1)
        left = lefts[0]
    else:
        term_parts = [lax.psum_scatter(terms[0], "mp", scatter_dimension=0, tiled=True)]
        left = call(
            functools.partial(shard_kernel, 1.0 / n_mp),
            shape((2 * rank, row_block), F32),
            in_specs=[VMEM] * 3,
            out_specs=VMEM,
        )(term_parts[0], in_basis_t, out_basis_t)

    left = call(
        error_kernel,
        shape((2 * rank, row_block), F32),
        flops=8 * row_block * both * rank,
        moved=3 << 20,
        in_specs=[VMEM] * 5,
        out_specs=VMEM,
    )(left, in_errors, out_errors, in_basis_t, out_basis_t)
    if blocks == 2:
        left, term_sent, score_sent = call(
            join_kernel,
            tuple(shape(array.shape, array.dtype) for array in (left, terms[1], score_parts[1])),
            in_specs=[VMEM] * 2 + [ANY] * 2,
            out_specs=[VMEM] + [ANY] * 2,
            input_output_aliases={2: 1, 3: 2},
        )(left, left_other, terms[1], score_parts[1])
        score_parts = [score_parts[0], exchange(score_sent, "mp", n_mp, 1)]
        term_parts = [terms[0], exchange(term_sent, "mp", n_mp, 1)]

    stats = call(
        functools.partial(table_kernel, blocks),
        shape((head_count, padded + 2 * LANES), F32),
        flops=2 * row_count * features * wide,
        moved=4 << 20,
        in_specs=[SMEM] + [VMEM] * (blocks + 2),
        out_specs=VMEM,
    )(me, *score_parts, gain_term, index_t)

    if blocks == 2:
        stats = [stats, exchange(stats, "mp", n_mp, 1)]
    else:
        stats = [sum_over(stats, "mp", n_mp)]

    groups = digits(n_dp)
    for group in groups[:0:-1]:
        left = call(
            functools.partial(add_kernel, group[1]),
            shape(left.shape, F32),
            in_specs=[VMEM] * (group[1] + 1),
            out_specs=VMEM,
        )(*partners(left, "dp", n_dp, *group), stats[-1])
    stride, parts = groups[0]
    lefts = partners(left, "dp", n_dp, stride, parts)
    merged = call(
        functools.partial(merge_kernel, 1.0 / n_mp, len(term_parts)),
        shape((row_block, both), F32),
        flops=4 * row_block * both,
        moved=6 << 20,
        in_specs=[VMEM] * (len(term_parts) + 2),
        out_specs=VMEM,
    )(*term_parts, in_errors, out_errors)

    quarter = both // parts
    piece = shape((rank, quarter + LANES), BF16)
    ortho, *pieces = call(
        functools.partial(ortho_kernel, 1.0 / n_dp, len(lefts), len(stats)),
        (shape((2 * rank, row_block), F32),) + (piece,) * parts,
        [pltpu.VMEM((head_count, padded + 2 * LANES), F32)],
        flops=12 * row_block * both * rank,
        moved=3 << 20,
        in_specs=[SMEM] + [VMEM] * (len(lefts) + len(stats) + 1),
        out_specs=[VMEM] * (1 + parts),
    )(me, *lefts, *stats, merged)

    token_grad, flag = call(
        functools.partial(token_kernel, blocks),
        (shape((row_count, features), BF16), shape((SUBLANES, LANES), F32)),
        [
            pltpu.VMEM((row_count, features), F32),
            pltpu.VMEM((row_count, features), BF16),
            pltpu.SemaphoreType.DMA((1,)),
        ],
        flops=2 * row_count * features * wide,
        moved=4 << 20,
        in_specs=[SMEM] + [VMEM] * (blocks + 5),
        out_specs=[HBM, VMEM],
    )(me, packed, w_in_own, *arrived[:1], token_rows, cot_rows, gain, ortho)

    def reduced(values):
        return call(
            reduce_kernel,
            piece,
            in_specs=[VMEM] * (len(values) + 1),
            out_specs=VMEM,
            moved=1 << 18,
        )(*values, flag)

    held = reduced(
        [pieces[0]]
        + [exchange(pieces[step], "dp", n_dp, step * stride) for step in range(1, parts)]
    )
    for group in groups[1:]:
        held = reduced(partners(held, "dp", n_dp, *group))
    pieces = partners(held, "dp", n_dp, stride, parts)

    small = (
        shape((rank, wide), F32),
        shape((rank, features), F32),
        shape((head_count, buckets), F32),
        shape((1, features), F32),
    )
    in_update, out_update, in_new_error, out_new_error, in_right, out_right, table, gain = call(
        functools.partial(update_kernel, 1.0 / n_dp, 1.0 / (n_dp * n_mp), parts),
        (
            shape((row_block, wide), F32),
            shape((row_block, features), F32),
            shape((row_block, wide), F32),
            shape((row_block, features), F32),
            *small,
        ),
        [
            pltpu.VMEM((parts, rank, quarter + LANES), F32),
            pltpu.VMEM((parts, row_block, quarter), F32),
            pltpu.VMEM((parts, row_block, quarter), F32),
            pltpu.SemaphoreType.DMA((parts, 2)),
        ]
        + buffers(*small),
        flops=12 * row_block * both * rank,
        moved=8 << 20,
        in_specs=[SMEM] + [VMEM] * (parts + 2),
        out_specs=[HBM] * 8,
    )(me, *pieces, ortho, merged)

    return (
        token_grad.reshape(tokens.shape),
        gain.reshape(features),
        table,
        in_update,
        out_update,
        in_new_error[None],
        out_new_error[None],
        jnp.swapaxes(in_right, 0, 1)[None],
        jnp.swapaxes(out_right, 0, 1)[None],
    )


def solution(mesh):
    placed = (
        P(("dp", "mp"), None, None),
        P(("dp", "mp"), None, None),
        P(("dp", "mp"), None),
        P(),
        P(),
        P("mp", None),
        P("mp", None),
        P(),
        P("dp", "mp", None),
        P("dp", "mp", None),
        P("mp", None, None),
        P("mp", None, None),
    )
    return jax.shard_map(
        shards,
        mesh=mesh,
        in_specs=placed,
        out_specs=(
            P(("dp", "mp"), None, None),
            P(),
            P(),
            P("mp", None),
            P("mp", None),
            P("dp", "mp", None),
            P("dp", "mp", None),
            P("mp", None, None),
            P("mp", None, None),
        ),
        check_vma=False,
    )
```

```python
import functools

import jax
import jax.numpy as jnp
from jax import lax
from jax.experimental import pallas as pl
from jax.experimental.pallas import tpu as pltpu
from jax.sharding import PartitionSpec as P

NORM_EPS = 1e-05
BASIS_EPS = 1e-06
MASKED = -1e30
LANES = 128
SUBLANES = 8
READY_HEADS = 2
F32 = jnp.float32
BF16 = jnp.bfloat16

VMEM = pl.BlockSpec(memory_space=pltpu.VMEM)
HBM = pl.BlockSpec(memory_space=pltpu.HBM)
ANY = pl.BlockSpec(memory_space=pl.ANY)


def nn(a, b):
    return lax.dot_general(
        a, b, (((1,), (0,)), ((), ())), preferred_element_type=F32
    )


def nt(a, b):
    return lax.dot_general(
        a, b, (((1,), (1,)), ((), ())), preferred_element_type=F32
    )


def tn(a, b):
    return lax.dot_general(
        a, b, (((0,), (0,)), ((), ())), preferred_element_type=F32
    )


def block_columns(me, step, blocks, width):
    if blocks == 1:
        return pl.ds(0, width)
    index = me if step == 0 else 1 - me
    return pl.ds(pl.multiple_of(index * width, width), width)


def norm_forward(token_rows):
    tokens_wide = token_rows.astype(F32)
    mean_x = jnp.mean(tokens_wide, axis=-1, keepdims=True)
    centered = tokens_wide - mean_x
    variance = jnp.mean(centered * centered, axis=-1, keepdims=True)
    inv_sigma = lax.rsqrt(variance + NORM_EPS)
    return (centered * inv_sigma, inv_sigma)


def fetch(pairs, sems):
    copies = [
        pltpu.make_async_copy(source, target, sems.at[at])
        for at, (source, target) in enumerate(pairs)
    ]
    for copy in copies:
        copy.start()
    return copies


def halves(value):
    coarse = value.astype(BF16)
    return coarse, (value - coarse.astype(F32)).astype(BF16)


def stacked(value):
    return jnp.concatenate(halves(value), axis=0)


def folded(value):
    half = value.shape[0] // 2
    return value[:half] + value[half:]


def gather_bias(bias, heads, table_pad, index_t, index):
    span = index.shape[0]
    padded = table_pad.shape[1]
    even = span // LANES * LANES
    lookups = [(index_t[:, :even], False)] if even else []
    if even < span:
        lookups.append((index[even:, :], True))
    for places, flipped in lookups:
        rows, columns = places.shape
        for start in range(0, columns, LANES):
            stop = min(columns, start + LANES)
            part = places[:, start:stop]
            if stop - start < LANES:
                filler = jnp.zeros((rows, LANES - (stop - start)), jnp.int32)
                part = jnp.concatenate([part, filler], axis=1)
            high, low = part // LANES, part % LANES
            for head in heads:
                found = jnp.zeros((rows, LANES), F32)
                for level in range(padded // LANES):
                    row = table_pad[head : head + 1, level * LANES : (level + 1) * LANES]
                    row = jnp.broadcast_to(row, (rows, LANES))
                    picked = jnp.take_along_axis(row, low, axis=1, mode="promise_in_bounds")
                    found = jnp.where(high == level, picked, found)
                if flipped:
                    bias[head, start:stop, even:] = found[:, : stop - start].T
                else:
                    bias[head, :, start:stop] = found[:, : stop - start]


def prepare_kernel(blocks, ready, *refs):
    sources, rest = refs[:12], refs[12:]
    normed, part, bias, index_t, table_pad, bucket, *kept = rest[:16]
    table, sems = rest[16:]
    copies = fetch(list(zip(sources, [bucket, table] + kept)), sems)
    tokens, gain, w_own = kept[:3]
    me = lax.axis_index("mp")
    width = w_own.shape[0]
    span = bucket.shape[0]
    head_count, padded = table_pad.shape
    for copy in copies[:2]:
        copy.wait()
    table_pad[...] = jnp.zeros_like(table_pad)
    table_pad[:, : table.shape[1]] = table[...]
    index_t[...] = bucket[...].T
    gather_bias(bias, range(ready), table_pad, index_t, bucket)
    for copy in copies[2:5]:
        copy.wait()
    x_hat, _ = norm_forward(tokens[...])
    normed[...] = (x_hat * gain[...]).astype(BF16)
    part[...] = nn(normed[:, block_columns(me, 0, blocks, width)], w_own[...])
    for copy in copies[5:]:
        copy.wait()


def attend_kernel(blocks, share, *refs):
    normed, part, bias_ready, index_t, table_pad, bucket, gain, cot, region = refs[:9]
    own, arrived = refs[9:13], refs[13 : 9 + 4 * blocks]
    rest = refs[9 + 4 * blocks :]
    terms, lefts, rest = rest[:blocks], rest[blocks : 2 * blocks], rest[2 * blocks :]
    score_parts, (packed, gain_term), rest = rest[:blocks], rest[blocks : blocks + 2], rest[blocks + 2 :]
    proj, mixed_grad, mixed, score_sum, gain_row, bias = rest
    w_in, w_out, in_basis, out_basis = (
        [own[at]] + list(arrived[at : at + blocks - 1]) for at in range(4)
    )
    me = lax.axis_index("mp")
    window_count, span = region.shape
    features = normed.shape[1]
    ready, head_count = bias_ready.shape[0], bias.shape[0]
    head_size = features // head_count
    scale = head_size ** (-0.5)
    width = features // blocks
    if blocks == 1:
        proj[...] = part[...].astype(BF16)
    else:
        other = nn(normed[:, block_columns(me, 1, blocks, width)], w_in[1][...])
        proj[...] = (part[...] + other).astype(BF16)
    for step in range(blocks):
        mixed_grad[:, block_columns(me, step, blocks, width)] = nt(
            cot[...], w_out[step][...]
        ).astype(BF16)
    lane = lax.broadcasted_iota(jnp.int32, (span, LANES), 1)
    per_group = LANES // head_size
    for window in range(window_count):
        rows = pl.ds(window * span, span)
        ids_row = jnp.broadcast_to(region[window : window + 1, :], (span, span))
        allowed = ids_row == ids_row.T
        for group in range(features // LANES):
            start = group * LANES
            heads = slice(group * per_group, (group + 1) * per_group)
            if heads.stop <= ready:
                pair_bias = bias_ready[heads]
            else:
                if window == 0:
                    gather_bias(bias, range(heads.start, heads.stop), table_pad, index_t, bucket)
                pair_bias = bias[heads]
            q = proj[rows, start : start + LANES]
            k = proj[rows, features + start : features + start + LANES]
            v = proj[rows, 2 * features + start : 2 * features + start + LANES]
            g = mixed_grad[rows, start : start + LANES]
            pick = [lane // head_size == sub for sub in range(per_group)]
            k_split = jnp.concatenate([jnp.where(own, k, jnp.zeros_like(k)) for own in pick], 0)
            v_split = jnp.concatenate([jnp.where(own, v, jnp.zeros_like(v)) for own in pick], 0)
            scores = nt(k_split, q).reshape(per_group, span, span) * scale + pair_bias
            scores = jnp.where(allowed[None], scores, MASKED)
            top = jnp.max(scores, axis=1, keepdims=True)
            raised = jnp.exp(scores - top)
            prob = raised * (1.0 / jnp.sum(raised, axis=1, keepdims=True))
            prob_b = prob.astype(BF16)
            prob_grad = nt(v_split, g).reshape(per_group, span, span)
            inner = jnp.sum(prob * prob_grad, axis=1, keepdims=True)
            score_grad = prob * (prob_grad - inner)
            score_b = score_grad.astype(BF16)
            if window == 0:
                score_sum[heads] = score_grad
            else:
                score_sum[heads] += score_grad
            k_grads = nn(score_b.reshape(per_group * span, span), q)
            v_grads = nn(prob_b.reshape(per_group * span, span), g)

            def joined(parts):
                total = parts[0]
                for sub in range(1, per_group):
                    total = jnp.where(pick[sub], parts[sub], total)
                return total

            k_grad = joined([k_grads[at * span : (at + 1) * span] for at in range(per_group)])
            v_grad = joined([v_grads[at * span : (at + 1) * span] for at in range(per_group)])
            out = joined([tn(prob_b[at], v) for at in range(per_group)])
            q_grad = joined([tn(score_b[at], k) for at in range(per_group)])
            mixed[rows, start : start + LANES] = out.astype(BF16)
            packed[rows, start : start + LANES] = (q_grad * scale).astype(BF16)
            packed[rows, features + start : features + start + LANES] = (k_grad * scale).astype(
                BF16
            )
            packed[rows, 2 * features + start : 2 * features + start + LANES] = v_grad.astype(BF16)
    wide = 3 * features
    for step in range(blocks):
        columns = block_columns(me, step, blocks, width)
        product = tn(normed[:, columns], packed[...])
        terms[step][:, :wide] = product.astype(BF16)
        terms[step][:, wide:] = tn(mixed[:, columns], cot[...]).astype(BF16)
        weighted = product * w_in[step][...].astype(F32)
        folds = tree_add(
            [weighted[:, start : start + LANES] for start in range(0, wide, LANES)]
        )
        gain_row[:, columns] = jnp.sum(folds.T, axis=0, keepdims=True) / gain[:, columns]
        rank = in_basis[step].shape[0]
        for basis, at, place in (
            (in_basis[step], slice(None, wide), 0),
            (out_basis[step], slice(wide, None), rank),
        ):
            left = folded(nt(stacked(basis[...]), terms[step][:, at])) * share
            lefts[step][place : place + rank, :] = left
    gain_term[...] = jnp.zeros_like(gain_term)
    for piece in range(features // LANES):
        gain_term[piece : piece + 1, :] = gain_row[:, piece * LANES : (piece + 1) * LANES]
    rows = span // blocks
    for step in range(blocks):
        score_parts[step][...] = score_sum[:, block_columns(me, step, blocks, rows), :]


def token_kernel(blocks, packed, *refs):
    w_in, (tokens, cot, gain, _, result, flag, normed_grad, token_grad, sems) = (
        refs[:blocks],
        refs[blocks:],
    )
    me = lax.axis_index("mp")
    width = tokens.shape[1] // blocks
    for step in range(blocks):
        normed_grad[:, block_columns(me, step, blocks, width)] = nt(packed[...], w_in[step][...])
    x_hat, inv_sigma = norm_forward(tokens[...])
    hat_grad = normed_grad[...] * gain[...]
    token_delta = inv_sigma * (
        hat_grad
        - jnp.mean(hat_grad, axis=-1, keepdims=True)
        - x_hat * jnp.mean(hat_grad * x_hat, axis=-1, keepdims=True)
    )
    token_grad[...] = (cot[...].astype(F32) + token_delta).astype(BF16)
    flag[...] = jnp.zeros_like(flag)
    for copy in fetch([(token_grad, result)], sems):
        copy.wait()


def table_kernel(blocks, *refs):
    score_parts, (gain_term, index_t, stats) = refs[:blocks], refs[blocks:]
    head_count, rows, span = score_parts[0].shape
    padded = stats.shape[1] - 2 * LANES
    levels = padded // LANES
    indices = index_t[block_columns(lax.axis_index("mp"), 0, blocks, rows), :]
    scores = tree_add([part[...] for part in score_parts])
    sublane = lax.broadcasted_iota(jnp.int32, (LANES, span), 0)
    total = jnp.zeros((2 * levels * head_count, LANES), F32)
    for row in range(rows):
        index = indices[row : row + 1, :]
        high = jnp.broadcast_to(index // LANES, (head_count, span))
        low = jnp.broadcast_to(index % LANES, (LANES, span))
        one_hot = jnp.where(low == sublane, 1.0, 0.0).astype(BF16)
        values = scores[:, row, :]
        coarse = values.astype(BF16).astype(F32)
        fine = values - coarse
        picked = [
            jnp.where(high == level, piece, 0.0)
            for piece in (coarse, fine)
            for level in range(levels)
        ]
        total += nt(jnp.concatenate(picked, axis=0).astype(BF16), one_hot)
    total = folded(total)
    for level in range(levels):
        stats[:, level * LANES : (level + 1) * LANES] = total[
            level * head_count : (level + 1) * head_count
        ]
    stats[:, padded : padded + LANES] = gain_term[...]
    stats[:, padded + LANES :] = jnp.zeros((head_count, LANES), F32)


def shard_kernel(share, shard, in_basis, out_basis, left):
    rank, split = in_basis.shape
    left[:rank, :] = folded(nt(stacked(in_basis[...]), shard[:, :split])) * share
    left[rank:, :] = folded(nt(stacked(out_basis[...]), shard[:, split:])) * share


def error_kernel(term_left, in_error, out_error, in_basis, out_basis, left):
    rank = in_basis.shape[0]
    for error, basis, at in ((in_error, in_basis, 0), (out_error, out_basis, rank)):
        coarse, fine = halves(error[...])
        pair = stacked(basis[...])
        left[at : at + rank, :] = term_left[at : at + rank, :] + folded(
            nt(pair, coarse) + nt(pair, fine)
        )


def merge_kernel(share, parts, *refs):
    shards, (in_error, out_error, merged) = refs[:parts], refs[parts:]
    split = in_error.shape[1]
    for columns, error in ((slice(None, split), in_error), (slice(split, None), out_error)):
        total = tree_add([shard[:, columns].astype(F32) for shard in shards])
        merged[:, columns] = total * share + error[...]


def tree_sum(values):
    while len(values) > 1:
        values = [values[at] + values[at + 1] for at in range(0, len(values), 2)]
    return values[0]


def tree_add(values):
    while len(values) > 1:
        odd = values[len(values) // 2 * 2 :]
        values = [values[at] + values[at + 1] for at in range(0, len(values) - 1, 2)] + odd
    return values[0]


def join_kernel(left_own, left_other, *refs):
    left = refs[len(refs) // 2]
    left[...] = left_own[...] + left_other[...]


def add_kernel(parts, *refs):
    refs[-1][...] = tree_sum([ref[...] for ref in refs[:parts]])


def stats_pieces(pair):
    pieces = []
    for at in range(2):
        tile = pair[:, at * LANES : (at + 1) * LANES]
        coarse, fine = halves(tile)
        pieces += [coarse.astype(F32), fine.astype(F32)]
    return jnp.concatenate(pieces, axis=0).astype(BF16)


def stats_pair(pieces):
    rows = pieces.shape[0] // 4
    return jnp.concatenate(
        [
            pieces[2 * at * rows : (2 * at + 1) * rows]
            + pieces[(2 * at + 1) * rows : (2 * at + 2) * rows]
            for at in range(2)
        ],
        axis=1,
    )


def orthonormal(problems):
    rank, rows = problems[0].shape
    tiles = rank // SUBLANES
    spread_shape = (SUBLANES, rows)
    place = lax.broadcasted_iota(jnp.int32, spread_shape, 0)

    def dots(rows_of, vector):
        return jnp.sum(rows_of * vector, axis=1, keepdims=True)

    def spread(tiled, row):
        tile, at = divmod(row, SUBLANES)
        return jnp.broadcast_to(tiled[tile][at : at + 1], spread_shape)

    states = []
    for first in problems:
        original = [first[at * SUBLANES : (at + 1) * SUBLANES] for at in range(tiles)]
        states.append((original, list(original), [jnp.zeros(spread_shape, F32)] * tiles))
    def project(finished, found):
        weighted = tree_add([found[q] * finished[q] for q in found])
        return jnp.sum(weighted, axis=0, keepdims=True)

    currents = [spread(original, 0) for original, _, _ in states]
    known = [None for _ in states]
    for column in range(rank):
        tile, at = divmod(column, SUBLANES)
        before = range((column - 1) // SUBLANES + 1)
        for which, (original, residual, finished) in enumerate(states):
            current = currents[which]
            square = dots(current, current)
            inverse = lax.rsqrt(square + BASIS_EPS)
            unit = current * inverse
            if column + 1 < rank:
                ahead = spread(residual, column + 1)
                step = dots(spread(original, column + 1), current) * inverse
                own = dots(ahead, current) * inverse
                following = ahead - unit * (step + own - step * (square * inverse * inverse))
                if column:
                    cross = project(finished, {q: dots(finished[q], current) for q in before})
                    following = following - known[which] + (step * inverse) * cross
            finished[tile] = jnp.where(place == at, unit, finished[tile])
            if column + 1 < rank:
                for q in range((column + 1) // SUBLANES, tiles):
                    residual[q] = residual[q] - (dots(original[q], current) * inverse) * unit
                currents[which] = following
            if column + 2 < rank:
                far = spread(residual, column + 2)
                known[which] = project(
                    finished, {q: dots(finished[q], far) for q in range(tile + 1)}
                )
    return [jnp.concatenate(finished, axis=0) for _, _, finished in states]


def ortho_kernel(share, parts, stat_parts, *refs):
    lefts, stats = refs[:parts], refs[parts : parts + stat_parts]
    merged, ortho, *pieces, sums = refs[parts + stat_parts :]
    digit = lax.axis_index("dp") % 4
    rank = ortho.shape[0] // 2
    quarter = merged.shape[1] // len(pieces)
    sums[...] = tree_sum([stat[...] for stat in stats])
    total = tree_sum([left[...] for left in lefts]) * share
    finished = orthonormal([total[:rank], total[rank:]])
    ortho[:rank, :], ortho[rank:, :] = finished
    for step, piece in enumerate(pieces):
        block = jnp.bitwise_xor(digit, step)
        columns = pl.ds(pl.multiple_of(block * quarter, quarter), quarter)
        pair = stacked(jnp.where(block < len(pieces) - 1, finished[0], finished[1]))
        piece[:, :quarter] = folded(nn(pair, merged[:, columns].astype(BF16))).astype(BF16)
        stat_columns = pl.ds(pl.multiple_of(block * 2 * LANES, 2 * LANES), 2 * LANES)
        piece[:, quarter:] = stats_pieces(sums[:, stat_columns])


def reduce_kernel(*refs):
    pieces, total = refs[:-2], refs[-1]
    quarter = total.shape[1] - LANES
    summed = tree_sum([piece[...].astype(F32) for piece in pieces])
    total[:, :quarter] = summed[:, :quarter].astype(BF16)
    total[:, quarter:] = stats_pieces(stats_pair(summed[:, quarter:]))


def update_kernel(share, stat_share, parts, *refs):
    pieces = refs[:parts]
    ortho, merged = refs[parts : parts + 2]
    in_update, out_update, in_new_error, out_new_error = refs[parts + 2 : parts + 6]
    small_results = refs[parts + 6 : parts + 10]
    rights, updates, errors, sems = refs[parts + 10 : parts + 14]
    small = refs[parts + 14 : parts + 18]
    in_basis, out_basis, table, gain = small
    digit = lax.axis_index("dp") % 4
    rank = ortho.shape[0] // 2
    quarter = rights.shape[2] - LANES
    for step, piece in enumerate(pieces):
        rights[step] = piece[...].astype(F32)
    copies = []
    tiles = []
    for block in range(parts):
        here = rights[jnp.bitwise_xor(digit, block)]
        right = here[:, :quarter] * share
        tiles.append(stats_pair(here[:, quarter:]) * stat_share)
        is_in = block < parts - 1
        columns = slice(block * quarter, (block + 1) * quarter)
        own = ortho[:rank, :] if is_in else ortho[rank:, :]
        own_coarse, own_fine = halves(own)
        coarse, fine = halves(right)
        update = tn(
            jnp.concatenate([own_coarse, own_coarse, own_fine], axis=0),
            jnp.concatenate([coarse, fine, coarse], axis=0),
        )
        updates[block] = update
        errors[block] = merged[:, columns] - update
        if is_in:
            in_basis[:, columns] = right
            update_to, error_to = in_update.at[:, columns], in_new_error.at[:, columns]
        else:
            out_basis[...] = right
            update_to, error_to = out_update, out_new_error
        copies += fetch(
            [(updates.at[block], update_to), (errors.at[block], error_to)], sems.at[block]
        )
    stats = jnp.concatenate(tiles, axis=1)
    table[...] = stats[:, : table.shape[1]]
    padded = stats.shape[1] - 2 * LANES
    for at in range(gain.shape[1] // LANES):
        gain[:, at * LANES : (at + 1) * LANES] = stats[at : at + 1, padded : padded + LANES]
    copies += fetch(list(zip(small, small_results)), refs[parts + 18])
    for copy in copies:
        copy.wait()


def call(kernel, outs, scratch=(), flops=0, moved=0, vmem=16, **options):
    return pl.pallas_call(
        kernel,
        out_shape=outs,
        scratch_shapes=list(scratch),
        cost_estimate=pl.CostEstimate(flops=flops, bytes_accessed=moved, transcendentals=0),
        compiler_params=pltpu.CompilerParams(vmem_limit_bytes=vmem << 20),
        **options,
    )


def buffers(*arrays):
    return [pltpu.VMEM(array.shape, array.dtype) for array in arrays] + [
        pltpu.SemaphoreType.DMA((len(arrays),))
    ]


def in_hbm(*arrays):
    return [pltpu.with_memory_space_constraint(array, pltpu.HBM) for array in arrays]


def shape(dims, dtype):
    return jax.ShapeDtypeStruct(dims, dtype)


def exchange(value, axis, count, distance):
    return lax.ppermute(value, axis, [(at, at ^ distance) for at in range(count)])


def digits(count):
    groups, stride = [], 1
    while stride < count:
        size = 4 if count // stride % 4 == 0 else 2
        groups.append((stride, size))
        stride *= size
    return groups


def partners(value, axis, count, stride, size):
    return [value] + [exchange(value, axis, count, step * stride) for step in range(1, size)]


def sum_over(value, axis, count):
    for stride, size in digits(count):
        value = tree_sum(partners(value, axis, count, stride, size))
    return value


def shards(
    tokens,
    cotangent,
    region_ids,
    rel_bucket,
    norm_gain,
    in_weight,
    out_weight,
    bias_table,
    in_error,
    out_error,
    in_basis,
    out_basis,
):
    n_dp = lax.axis_size("dp")
    n_mp = lax.axis_size("mp")
    window_count, span, features = tokens.shape
    head_count, buckets = bias_table.shape
    rank = in_basis.shape[2]
    row_count = window_count * span
    row_block = in_weight.shape[0]
    wide = in_weight.shape[1]
    both = wide + features
    padded = -(-buckets // LANES) * LANES
    blocks = 2 if n_mp == 2 else 1
    token_rows = tokens.reshape(row_count, features)
    cot_rows = cotangent.reshape(row_count, features)
    gain = norm_gain.reshape(1, features)

    in_basis_t = jnp.swapaxes(in_basis[0], 0, 1)
    out_basis_t = jnp.swapaxes(out_basis[0], 0, 1)
    if blocks == 2:
        own = (in_weight, out_weight, in_basis_t, out_basis_t)
        arrived = [exchange(array, "mp", n_mp, 1) for array in own]
    else:
        own = (
            lax.all_gather(in_weight, "mp", axis=0, tiled=True),
            lax.all_gather(out_weight, "mp", axis=0, tiled=True),
            in_basis_t,
            out_basis_t,
        )
        arrived = []
    width = features // blocks

    operands = (
        rel_bucket,
        bias_table,
        token_rows,
        gain,
        own[0],
        cot_rows,
        region_ids,
        *own[1:],
        in_error[0],
        out_error[0],
    )
    normed, part, bias, index_t, table_pad, bucket, *kept = call(
        functools.partial(prepare_kernel, blocks, READY_HEADS),
        (
            shape((row_count, features), BF16),
            shape((row_count, wide), F32),
            shape((READY_HEADS, span, span), F32),
            shape((span, span), jnp.int32),
            shape((head_count, padded), F32),
            shape((span, span), jnp.int32),
        )
        + tuple(shape(array.shape, array.dtype) for array in operands[2:]),
        [pltpu.VMEM(bias_table.shape, F32), pltpu.SemaphoreType.DMA((12,))],
        flops=2 * row_count * width * wide,
        moved=4 << 20,
        in_specs=[HBM] * 12,
        out_specs=[VMEM] * 16,
    )(*in_hbm(*operands))
    token_rows, gain, w_in_own, cot_rows, region, *own, in_errors, out_errors = kept
    in_basis_t, out_basis_t = own[1:]

    left_shape = shape((2 * rank, width), F32)
    outputs = call(
        functools.partial(attend_kernel, blocks, 1.0 / n_mp),
        (shape((width, both), BF16),) * blocks
        + (left_shape,) * blocks
        + (shape((head_count, span // blocks, span), F32),) * blocks
        + (shape((row_count, wide), BF16), shape((SUBLANES, LANES), F32)),
        [
            pltpu.VMEM((row_count, wide), BF16),
            pltpu.VMEM((row_count, features), BF16),
            pltpu.VMEM((row_count, features), BF16),
            pltpu.VMEM((head_count, span, span), F32),
            pltpu.VMEM((1, features), F32),
            pltpu.VMEM((head_count, span, span), F32),
        ],
        flops=4 * row_count * features * both,
        moved=8 << 20,
        in_specs=[VMEM] * (13 + len(arrived)),
        out_specs=[VMEM] * (3 * blocks + 2),
    )(normed, part, bias, index_t, table_pad, bucket, gain, cot_rows, region, w_in_own, *own, *arrived)
    terms, lefts, score_parts = (
        outputs[at * blocks : (at + 1) * blocks] for at in range(3)
    )
    packed, gain_term = outputs[3 * blocks :]

    if blocks == 2:
        left_other = exchange(lefts[1], "mp", n_mp, 1)
        left = lefts[0]
    else:
        term_parts = [lax.psum_scatter(terms[0], "mp", scatter_dimension=0, tiled=True)]
        left = call(
            functools.partial(shard_kernel, 1.0 / n_mp),
            shape((2 * rank, row_block), F32),
            in_specs=[VMEM] * 3,
            out_specs=VMEM,
        )(term_parts[0], in_basis_t, out_basis_t)

    left = call(
        error_kernel,
        shape((2 * rank, row_block), F32),
        flops=8 * row_block * both * rank,
        moved=3 << 20,
        in_specs=[VMEM] * 5,
        out_specs=VMEM,
    )(left, in_errors, out_errors, in_basis_t, out_basis_t)
    if blocks == 2:
        left, term_sent, score_sent = call(
            join_kernel,
            tuple(shape(array.shape, array.dtype) for array in (left, terms[1], score_parts[1])),
            in_specs=[VMEM] * 2 + [ANY] * 2,
            out_specs=[VMEM] + [ANY] * 2,
            input_output_aliases={2: 1, 3: 2},
        )(left, left_other, terms[1], score_parts[1])
        score_parts = [score_parts[0], exchange(score_sent, "mp", n_mp, 1)]
        term_parts = [terms[0], exchange(term_sent, "mp", n_mp, 1)]

    stats = call(
        functools.partial(table_kernel, blocks),
        shape((head_count, padded + 2 * LANES), F32),
        flops=2 * row_count * features * wide,
        moved=4 << 20,
        in_specs=[VMEM] * (blocks + 2),
        out_specs=VMEM,
    )(*score_parts, gain_term, index_t)

    if blocks == 2:
        stats = [stats, exchange(stats, "mp", n_mp, 1)]
    else:
        stats = [sum_over(stats, "mp", n_mp)]

    groups = digits(n_dp)
    for group in groups[:0:-1]:
        left = call(
            functools.partial(add_kernel, group[1]),
            shape(left.shape, F32),
            in_specs=[VMEM] * (group[1] + 1),
            out_specs=VMEM,
        )(*partners(left, "dp", n_dp, *group), stats[-1])
    stride, parts = groups[0]
    lefts = partners(left, "dp", n_dp, stride, parts)
    merged = call(
        functools.partial(merge_kernel, 1.0 / n_mp, len(term_parts)),
        shape((row_block, both), F32),
        flops=4 * row_block * both,
        moved=6 << 20,
        in_specs=[VMEM] * (len(term_parts) + 2),
        out_specs=VMEM,
    )(*term_parts, in_errors, out_errors)

    quarter = both // parts
    piece = shape((rank, quarter + LANES), BF16)
    ortho, *pieces = call(
        functools.partial(ortho_kernel, 1.0 / n_dp, len(lefts), len(stats)),
        (shape((2 * rank, row_block), F32),) + (piece,) * parts,
        [pltpu.VMEM((head_count, padded + 2 * LANES), F32)],
        flops=12 * row_block * both * rank,
        moved=3 << 20,
        in_specs=[VMEM] * (len(lefts) + len(stats) + 1),
        out_specs=[VMEM] * (1 + parts),
    )(*lefts, *stats, merged)

    token_grad, flag = call(
        functools.partial(token_kernel, blocks),
        (shape((row_count, features), BF16), shape((SUBLANES, LANES), F32)),
        [
            pltpu.VMEM((row_count, features), F32),
            pltpu.VMEM((row_count, features), BF16),
            pltpu.SemaphoreType.DMA((1,)),
        ],
        flops=2 * row_count * features * wide,
        moved=4 << 20,
        in_specs=[VMEM] * (blocks + 5),
        out_specs=[HBM, VMEM],
    )(packed, w_in_own, *arrived[:1], token_rows, cot_rows, gain, ortho)

    def reduced(values):
        return call(
            reduce_kernel,
            piece,
            in_specs=[VMEM] * (len(values) + 1),
            out_specs=VMEM,
            moved=1 << 18,
        )(*values, flag)

    held = reduced(
        [pieces[0]]
        + [exchange(pieces[step], "dp", n_dp, step * stride) for step in range(1, parts)]
    )
    for group in groups[1:]:
        held = reduced(partners(held, "dp", n_dp, *group))
    pieces = partners(held, "dp", n_dp, stride, parts)

    small = (
        shape((rank, wide), F32),
        shape((rank, features), F32),
        shape((head_count, buckets), F32),
        shape((1, features), F32),
    )
    in_update, out_update, in_new_error, out_new_error, in_right, out_right, table, gain = call(
        functools.partial(update_kernel, 1.0 / n_dp, 1.0 / (n_dp * n_mp), parts),
        (
            shape((row_block, wide), F32),
            shape((row_block, features), F32),
            shape((row_block, wide), F32),
            shape((row_block, features), F32),
            *small,
        ),
        [
            pltpu.VMEM((parts, rank, quarter + LANES), F32),
            pltpu.VMEM((parts, row_block, quarter), F32),
            pltpu.VMEM((parts, row_block, quarter), F32),
            pltpu.SemaphoreType.DMA((parts, 2)),
        ]
        + buffers(*small),
        flops=12 * row_block * both * rank,
        moved=8 << 20,
        in_specs=[VMEM] * (parts + 2),
        out_specs=[HBM] * 8,
    )(*pieces, ortho, merged)

    return (
        token_grad.reshape(tokens.shape),
        gain.reshape(features),
        table,
        in_update,
        out_update,
        in_new_error[None],
        out_new_error[None],
        jnp.swapaxes(in_right, 0, 1)[None],
        jnp.swapaxes(out_right, 0, 1)[None],
    )


def solution(mesh):
    placed = (
        P(("dp", "mp"), None, None),
        P(("dp", "mp"), None, None),
        P(("dp", "mp"), None),
        P(),
        P(),
        P("mp", None),
        P("mp", None),
        P(),
        P("dp", "mp", None),
        P("dp", "mp", None),
        P("mp", None, None),
        P("mp", None, None),
    )
    return jax.shard_map(
        shards,
        mesh=mesh,
        in_specs=placed,
        out_specs=(
            P(("dp", "mp"), None, None),
            P(),
            P(),
            P("mp", None),
            P("mp", None),
            P("dp", "mp", None),
            P("dp", "mp", None),
            P("mp", None, None),
            P("mp", None, None),
        ),
        check_vma=False,
    )
```

```python
import functools

import jax
import jax.numpy as jnp
from jax import lax
from jax.experimental import pallas as pl
from jax.experimental.pallas import tpu as pltpu
from jax.sharding import PartitionSpec as P

NORM_EPS = 1e-05
BASIS_EPS = 1e-06
MASKED = -1e30
LANES = 128
SUBLANES = 8
READY_HEADS = 2
F32 = jnp.float32
BF16 = jnp.bfloat16

VMEM = pl.BlockSpec(memory_space=pltpu.VMEM)
HBM = pl.BlockSpec(memory_space=pltpu.HBM)
ANY = pl.BlockSpec(memory_space=pl.ANY)


def nn(a, b):
    return lax.dot_general(
        a, b, (((1,), (0,)), ((), ())), preferred_element_type=F32
    )


def nt(a, b):
    return lax.dot_general(
        a, b, (((1,), (1,)), ((), ())), preferred_element_type=F32
    )


def tn(a, b):
    return lax.dot_general(
        a, b, (((0,), (0,)), ((), ())), preferred_element_type=F32
    )


def block_columns(me, step, blocks, width):
    if blocks == 1:
        return pl.ds(0, width)
    index = me if step == 0 else 1 - me
    return pl.ds(pl.multiple_of(index * width, width), width)


def norm_forward(token_rows):
    tokens_wide = token_rows.astype(F32)
    mean_x = jnp.mean(tokens_wide, axis=-1, keepdims=True)
    centered = tokens_wide - mean_x
    variance = jnp.mean(centered * centered, axis=-1, keepdims=True)
    inv_sigma = lax.rsqrt(variance + NORM_EPS)
    return (centered * inv_sigma, inv_sigma)


def fetch(pairs, sems):
    copies = [
        pltpu.make_async_copy(source, target, sems.at[at])
        for at, (source, target) in enumerate(pairs)
    ]
    for copy in copies:
        copy.start()
    return copies


def halves(value):
    coarse = value.astype(BF16)
    return coarse, (value - coarse.astype(F32)).astype(BF16)


def stacked(value):
    return jnp.concatenate(halves(value), axis=0)


def folded(value):
    half = value.shape[0] // 2
    return value[:half] + value[half:]


def gather_bias(bias, heads, table_pad, index_t, index):
    span = index.shape[0]
    padded = table_pad.shape[1]
    even = span // LANES * LANES
    lookups = [(index_t[:, :even], False)] if even else []
    if even < span:
        lookups.append((index[even:, :], True))
    for places, flipped in lookups:
        rows, columns = places.shape
        for start in range(0, columns, LANES):
            stop = min(columns, start + LANES)
            part = places[:, start:stop]
            if stop - start < LANES:
                filler = jnp.zeros((rows, LANES - (stop - start)), jnp.int32)
                part = jnp.concatenate([part, filler], axis=1)
            high, low = part // LANES, part % LANES
            for head in heads:
                found = jnp.zeros((rows, LANES), F32)
                for level in range(padded // LANES):
                    row = table_pad[head : head + 1, level * LANES : (level + 1) * LANES]
                    row = jnp.broadcast_to(row, (rows, LANES))
                    picked = jnp.take_along_axis(row, low, axis=1, mode="promise_in_bounds")
                    found = jnp.where(high == level, picked, found)
                if flipped:
                    bias[head, start:stop, even:] = found[:, : stop - start].T
                else:
                    bias[head, :, start:stop] = found[:, : stop - start]


def prepare_kernel(blocks, ready, *refs):
    sources, rest = refs[:12], refs[12:]
    normed, part, bias, index_t, table_pad, bucket, *kept = rest[:16]
    table, sems = rest[16:]
    copies = fetch(list(zip(sources, [bucket, table] + kept)), sems)
    tokens, gain, w_own = kept[:3]
    me = lax.axis_index("mp")
    width = w_own.shape[0]
    span = bucket.shape[0]
    head_count, padded = table_pad.shape
    for copy in copies[:2]:
        copy.wait()
    table_pad[...] = jnp.zeros_like(table_pad)
    table_pad[:, : table.shape[1]] = table[...]
    index_t[...] = bucket[...].T
    gather_bias(bias, range(ready), table_pad, index_t, bucket)
    for copy in copies[2:5]:
        copy.wait()
    x_hat, _ = norm_forward(tokens[...])
    normed[...] = (x_hat * gain[...]).astype(BF16)
    part[...] = nn(normed[:, block_columns(me, 0, blocks, width)], w_own[...])
    for copy in copies[5:]:
        copy.wait()


def attend_kernel(blocks, share, *refs):
    normed, part, bias_ready, index_t, table_pad, bucket, cot, region = refs[:8]
    own, arrived = refs[8:12], refs[12 : 8 + 4 * blocks]
    rest = refs[8 + 4 * blocks :]
    terms, lefts, rest = rest[:blocks], rest[blocks : 2 * blocks], rest[2 * blocks :]
    score_sum, packed, proj, mixed_grad, mixed, bias = rest
    w_in, w_out, in_basis, out_basis = (
        [own[at]] + list(arrived[at : at + blocks - 1]) for at in range(4)
    )
    me = lax.axis_index("mp")
    window_count, span = region.shape
    features = normed.shape[1]
    ready, head_count = bias_ready.shape[0], bias.shape[0]
    head_size = features // head_count
    scale = head_size ** (-0.5)
    width = features // blocks
    if blocks == 1:
        proj[...] = part[...].astype(BF16)
    else:
        other = nn(normed[:, block_columns(me, 1, blocks, width)], w_in[1][...])
        proj[...] = (part[...] + other).astype(BF16)
    for step in range(blocks):
        mixed_grad[:, block_columns(me, step, blocks, width)] = nt(
            cot[...], w_out[step][...]
        ).astype(BF16)
    lane = lax.broadcasted_iota(jnp.int32, (span, LANES), 1)
    per_group = LANES // head_size
    for window in range(window_count):
        rows = pl.ds(window * span, span)
        ids_row = jnp.broadcast_to(region[window : window + 1, :], (span, span))
        allowed = ids_row == ids_row.T
        for group in range(features // LANES):
            start = group * LANES
            heads = slice(group * per_group, (group + 1) * per_group)
            if heads.stop <= ready:
                pair_bias = bias_ready[heads]
            else:
                if window == 0:
                    gather_bias(bias, range(heads.start, heads.stop), table_pad, index_t, bucket)
                pair_bias = bias[heads]
            q = proj[rows, start : start + LANES]
            k = proj[rows, features + start : features + start + LANES]
            v = proj[rows, 2 * features + start : 2 * features + start + LANES]
            g = mixed_grad[rows, start : start + LANES]
            pick = [lane // head_size == sub for sub in range(per_group)]
            k_split = jnp.concatenate([jnp.where(own, k, jnp.zeros_like(k)) for own in pick], 0)
            v_split = jnp.concatenate([jnp.where(own, v, jnp.zeros_like(v)) for own in pick], 0)
            scores = nt(k_split, q).reshape(per_group, span, span) * scale + pair_bias
            scores = jnp.where(allowed[None], scores, MASKED)
            top = jnp.max(scores, axis=1, keepdims=True)
            raised = jnp.exp(scores - top)
            prob = raised * (1.0 / jnp.sum(raised, axis=1, keepdims=True))
            prob_b = prob.astype(BF16)
            prob_grad = nt(v_split, g).reshape(per_group, span, span)
            inner = jnp.sum(prob * prob_grad, axis=1, keepdims=True)
            score_grad = prob * (prob_grad - inner)
            score_b = score_grad.astype(BF16)
            if window == 0:
                score_sum[heads] = score_grad
            else:
                score_sum[heads] += score_grad
            k_grads = nn(score_b.reshape(per_group * span, span), q)
            v_grads = nn(prob_b.reshape(per_group * span, span), g)

            def joined(parts):
                total = parts[0]
                for sub in range(1, per_group):
                    total = jnp.where(pick[sub], parts[sub], total)
                return total

            k_grad = joined([k_grads[at * span : (at + 1) * span] for at in range(per_group)])
            v_grad = joined([v_grads[at * span : (at + 1) * span] for at in range(per_group)])
            out = joined([tn(prob_b[at], v) for at in range(per_group)])
            q_grad = joined([tn(score_b[at], k) for at in range(per_group)])
            mixed[rows, start : start + LANES] = out.astype(BF16)
            packed[rows, start : start + LANES] = (q_grad * scale).astype(BF16)
            packed[rows, features + start : features + start + LANES] = (k_grad * scale).astype(
                BF16
            )
            packed[rows, 2 * features + start : 2 * features + start + LANES] = v_grad.astype(BF16)
    wide = 3 * features
    for step in range(blocks):
        columns = block_columns(me, step, blocks, width)
        terms[step][:, :wide] = tn(normed[:, columns], packed[...]).astype(BF16)
        terms[step][:, wide:] = tn(mixed[:, columns], cot[...]).astype(BF16)
        rank = in_basis[step].shape[0]
        for basis, at, place in (
            (in_basis[step], slice(None, wide), 0),
            (out_basis[step], slice(wide, None), rank),
        ):
            left = folded(nt(stacked(basis[...]), terms[step][:, at])) * share
            lefts[step][place : place + rank, :] = left


def token_kernel(blocks, packed, *refs):
    w_in, (tokens, cot, gain, _, result, flag, normed_grad, token_grad, sems) = (
        refs[:blocks],
        refs[blocks:],
    )
    me = lax.axis_index("mp")
    width = tokens.shape[1] // blocks
    for step in range(blocks):
        normed_grad[:, block_columns(me, step, blocks, width)] = nt(packed[...], w_in[step][...])
    x_hat, inv_sigma = norm_forward(tokens[...])
    hat_grad = normed_grad[...] * gain[...]
    token_delta = inv_sigma * (
        hat_grad
        - jnp.mean(hat_grad, axis=-1, keepdims=True)
        - x_hat * jnp.mean(hat_grad * x_hat, axis=-1, keepdims=True)
    )
    token_grad[...] = (cot[...].astype(F32) + token_delta).astype(BF16)
    flag[...] = jnp.zeros_like(flag)
    for copy in fetch([(token_grad, result)], sems):
        copy.wait()


def table_kernel(blocks, *refs):
    scores_of, terms = refs[:blocks], refs[blocks : 2 * blocks]
    w_in, rest = refs[2 * blocks : 3 * blocks], refs[3 * blocks :]
    gain, index_t, stats, gain_row = rest
    me = lax.axis_index("mp")
    features = gain.shape[1]
    for step in range(blocks):
        columns = block_columns(me, step, blocks, features // blocks)
        folds = tree_add(
            [
                terms[step][:, at : at + LANES].astype(F32)
                * w_in[step][:, at : at + LANES].astype(F32)
                for at in range(0, w_in[step].shape[1], LANES)
            ]
        )
        gain_row[:, columns] = jnp.sum(folds.T, axis=0, keepdims=True) / gain[:, columns]
    head_count, span, _ = scores_of[0].shape
    rows = span // blocks
    mine = block_columns(me, 0, blocks, rows)
    padded = stats.shape[1] - 2 * LANES
    levels = padded // LANES
    indices = index_t[mine, :]
    scores = tree_add([part[:, mine, :] for part in scores_of])
    sublane = lax.broadcasted_iota(jnp.int32, (LANES, span), 0)
    total = jnp.zeros((2 * levels * head_count, LANES), F32)
    for row in range(rows):
        index = indices[row : row + 1, :]
        high = jnp.broadcast_to(index // LANES, (head_count, span))
        low = jnp.broadcast_to(index % LANES, (LANES, span))
        one_hot = jnp.where(low == sublane, 1.0, 0.0).astype(BF16)
        values = scores[:, row, :]
        coarse = values.astype(BF16).astype(F32)
        fine = values - coarse
        picked = [
            jnp.where(high == level, piece, 0.0)
            for piece in (coarse, fine)
            for level in range(levels)
        ]
        total += nt(jnp.concatenate(picked, axis=0).astype(BF16), one_hot)
    total = folded(total)
    for level in range(levels):
        stats[:, level * LANES : (level + 1) * LANES] = total[
            level * head_count : (level + 1) * head_count
        ]
    stats[:, padded:] = jnp.zeros((head_count, 2 * LANES), F32)
    for piece in range(features // LANES):
        stats[piece : piece + 1, padded : padded + LANES] = gain_row[
            :, piece * LANES : (piece + 1) * LANES
        ]


def shard_kernel(share, shard, in_basis, out_basis, left):
    rank, split = in_basis.shape
    left[:rank, :] = folded(nt(stacked(in_basis[...]), shard[:, :split])) * share
    left[rank:, :] = folded(nt(stacked(out_basis[...]), shard[:, split:])) * share


def error_kernel(term_left, in_error, out_error, in_basis, out_basis, left):
    rank = in_basis.shape[0]
    for error, basis, at in ((in_error, in_basis, 0), (out_error, out_basis, rank)):
        coarse, fine = halves(error[...])
        pair = stacked(basis[...])
        left[at : at + rank, :] = term_left[at : at + rank, :] + folded(
            nt(pair, coarse) + nt(pair, fine)
        )


def merge_kernel(share, parts, *refs):
    shards, (in_error, out_error, merged) = refs[:parts], refs[parts:]
    split = in_error.shape[1]
    for columns, error in ((slice(None, split), in_error), (slice(split, None), out_error)):
        total = tree_add([shard[:, columns].astype(F32) for shard in shards])
        merged[:, columns] = total * share + error[...]


def tree_sum(values):
    while len(values) > 1:
        values = [values[at] + values[at + 1] for at in range(0, len(values), 2)]
    return values[0]


def tree_add(values):
    while len(values) > 1:
        odd = values[len(values) // 2 * 2 :]
        values = [values[at] + values[at + 1] for at in range(0, len(values) - 1, 2)] + odd
    return values[0]


def join_kernel(left_own, left_other, *refs):
    left = refs[len(refs) // 2]
    left[...] = left_own[...] + left_other[...]


def add_kernel(parts, *refs):
    refs[-1][...] = tree_sum([ref[...] for ref in refs[:parts]])


def stats_pieces(pair):
    pieces = []
    for at in range(2):
        tile = pair[:, at * LANES : (at + 1) * LANES]
        coarse, fine = halves(tile)
        pieces += [coarse.astype(F32), fine.astype(F32)]
    return jnp.concatenate(pieces, axis=0).astype(BF16)


def stats_pair(pieces):
    rows = pieces.shape[0] // 4
    return jnp.concatenate(
        [
            pieces[2 * at * rows : (2 * at + 1) * rows]
            + pieces[(2 * at + 1) * rows : (2 * at + 2) * rows]
            for at in range(2)
        ],
        axis=1,
    )


def orthonormal(problems):
    rank, rows = problems[0].shape
    tiles = rank // SUBLANES
    spread_shape = (SUBLANES, rows)
    place = lax.broadcasted_iota(jnp.int32, spread_shape, 0)

    def dots(rows_of, vector):
        return jnp.sum(rows_of * vector, axis=1, keepdims=True)

    def spread(tiled, row):
        tile, at = divmod(row, SUBLANES)
        return jnp.broadcast_to(tiled[tile][at : at + 1], spread_shape)

    states = []
    for first in problems:
        original = [first[at * SUBLANES : (at + 1) * SUBLANES] for at in range(tiles)]
        states.append((original, list(original), [jnp.zeros(spread_shape, F32)] * tiles))
    def project(finished, found):
        weighted = tree_add([found[q] * finished[q] for q in found])
        return jnp.sum(weighted, axis=0, keepdims=True)

    currents = [spread(original, 0) for original, _, _ in states]
    known = [None for _ in states]
    for column in range(rank):
        tile, at = divmod(column, SUBLANES)
        before = range((column - 1) // SUBLANES + 1)
        for which, (original, residual, finished) in enumerate(states):
            current = currents[which]
            square = dots(current, current)
            inverse = lax.rsqrt(square + BASIS_EPS)
            unit = current * inverse
            if column + 1 < rank:
                ahead = spread(residual, column + 1)
                step = dots(spread(original, column + 1), current) * inverse
                own = dots(ahead, current) * inverse
                following = ahead - unit * (step + own - step * (square * inverse * inverse))
                if column:
                    cross = project(finished, {q: dots(finished[q], current) for q in before})
                    following = following - known[which] + (step * inverse) * cross
            finished[tile] = jnp.where(place == at, unit, finished[tile])
            if column + 1 < rank:
                for q in range((column + 1) // SUBLANES, tiles):
                    residual[q] = residual[q] - (dots(original[q], current) * inverse) * unit
                currents[which] = following
            if column + 2 < rank:
                far = spread(residual, column + 2)
                known[which] = project(
                    finished, {q: dots(finished[q], far) for q in range(tile + 1)}
                )
    return [jnp.concatenate(finished, axis=0) for _, _, finished in states]


def ortho_kernel(share, parts, stat_parts, *refs):
    lefts, stats = refs[:parts], refs[parts : parts + stat_parts]
    merged, ortho, *pieces, sums = refs[parts + stat_parts :]
    digit = lax.axis_index("dp") % 4
    rank = ortho.shape[0] // 2
    quarter = merged.shape[1] // len(pieces)
    sums[...] = tree_sum([stat[...] for stat in stats])
    total = tree_sum([left[...] for left in lefts]) * share
    finished = orthonormal([total[:rank], total[rank:]])
    ortho[:rank, :], ortho[rank:, :] = finished
    for step, piece in enumerate(pieces):
        block = jnp.bitwise_xor(digit, step)
        columns = pl.ds(pl.multiple_of(block * quarter, quarter), quarter)
        pair = stacked(jnp.where(block < len(pieces) - 1, finished[0], finished[1]))
        piece[:, :quarter] = folded(nn(pair, merged[:, columns].astype(BF16))).astype(BF16)
        stat_columns = pl.ds(pl.multiple_of(block * 2 * LANES, 2 * LANES), 2 * LANES)
        piece[:, quarter:] = stats_pieces(sums[:, stat_columns])


def reduce_kernel(*refs):
    pieces, total = refs[:-2], refs[-1]
    quarter = total.shape[1] - LANES
    summed = tree_sum([piece[...].astype(F32) for piece in pieces])
    total[:, :quarter] = summed[:, :quarter].astype(BF16)
    total[:, quarter:] = stats_pieces(stats_pair(summed[:, quarter:]))


def update_blocks(share, steps, pieces, ortho, merged, results, updates, errors, sems, small):
    in_update, out_update, in_new_error, out_new_error = results
    rank = ortho.shape[0] // 2
    quarter = updates.shape[2]
    count = merged.shape[1] // quarter
    places = []
    for at, step in enumerate(steps):
        block = jnp.bitwise_xor(lax.axis_index("dp") % 4, step)
        columns = pl.ds(pl.multiple_of(block * quarter, quarter), quarter)
        right = pieces[step][:, :quarter].astype(F32) * share
        own_coarse, own_fine = halves(
            jnp.where(block < count - 1, ortho[:rank, :], ortho[rank:, :])
        )
        coarse, fine = halves(right)
        update = tn(
            jnp.concatenate([own_coarse, own_coarse, own_fine], axis=0),
            jnp.concatenate([coarse, fine, coarse], axis=0),
        )
        updates[at] = update
        errors[at] = merged[:, columns] - update
        places.append((block, columns))

        @pl.when(block < count - 1)
        def _():
            targets = in_update.at[:, columns], in_new_error.at[:, columns]
            fetch(list(zip((updates.at[at], errors.at[at]), targets)), sems.at[at])

        @pl.when(block == count - 1)
        def _():
            targets = out_update, out_new_error
            fetch(list(zip((updates.at[at], errors.at[at]), targets)), sems.at[at])

    small()
    for at, (block, columns) in enumerate(places):
        pltpu.make_async_copy(updates.at[at], out_update, sems.at[at, 0]).wait()
        pltpu.make_async_copy(errors.at[at], out_new_error, sems.at[at, 1]).wait()


def first_kernel(share, steps, *refs):
    count = len(steps)
    pieces = dict(zip(steps, refs[:count]))
    ortho, merged = refs[count : count + 2]
    results, (updates, errors, sems) = refs[count + 2 : count + 6], refs[count + 6 :]
    update_blocks(share, steps, pieces, ortho, merged, results, updates, errors, sems, lambda: None)


def last_kernel(share, stat_share, steps, parts, *refs):
    pieces, (ortho, merged) = refs[:parts], refs[parts : parts + 2]
    results, small_results = refs[parts + 6 : parts + 10], refs[parts + 10 : parts + 14]
    rights, *small = refs[parts + 14 : parts + 19]
    small_sems, updates, errors, sems = refs[parts + 19 :]
    in_basis, out_basis, table, gain = small
    quarter = rights.shape[2] - LANES
    copies = []

    def small_outputs():
        for step, piece in enumerate(pieces):
            rights[step] = piece[...].astype(F32)
        tiles = []
        for block in range(parts):
            here = rights[jnp.bitwise_xor(lax.axis_index("dp") % 4, block)]
            right = here[:, :quarter] * share
            tiles.append(stats_pair(here[:, quarter:]) * stat_share)
            if block < parts - 1:
                in_basis[:, block * quarter : (block + 1) * quarter] = right
            else:
                out_basis[...] = right
        stats = jnp.concatenate(tiles, axis=1)
        table[...] = stats[:, : table.shape[1]]
        padded = stats.shape[1] - 2 * LANES
        for at in range(gain.shape[1] // LANES):
            gain[:, at * LANES : (at + 1) * LANES] = stats[at : at + 1, padded : padded + LANES]
        copies.extend(fetch(list(zip(small, small_results)), small_sems))

    update_blocks(
        share, steps, pieces, ortho, merged, results, updates, errors, sems, small_outputs
    )
    for copy in copies:
        copy.wait()


def call(kernel, outs, scratch=(), flops=0, moved=0, vmem=16, **options):
    return pl.pallas_call(
        kernel,
        out_shape=outs,
        scratch_shapes=list(scratch),
        cost_estimate=pl.CostEstimate(flops=flops, bytes_accessed=moved, transcendentals=0),
        compiler_params=pltpu.CompilerParams(vmem_limit_bytes=vmem << 20),
        **options,
    )


def buffers(*arrays):
    return [pltpu.VMEM(array.shape, array.dtype) for array in arrays] + [
        pltpu.SemaphoreType.DMA((len(arrays),))
    ]


def in_hbm(*arrays):
    return [pltpu.with_memory_space_constraint(array, pltpu.HBM) for array in arrays]


def shape(dims, dtype):
    return jax.ShapeDtypeStruct(dims, dtype)


def exchange(value, axis, count, distance):
    return lax.ppermute(value, axis, [(at, at ^ distance) for at in range(count)])


def digits(count):
    groups, stride = [], 1
    while stride < count:
        size = 4 if count // stride % 4 == 0 else 2
        groups.append((stride, size))
        stride *= size
    return groups


def partners(value, axis, count, stride, size):
    return [value] + [exchange(value, axis, count, step * stride) for step in range(1, size)]


def sum_over(value, axis, count):
    for stride, size in digits(count):
        value = tree_sum(partners(value, axis, count, stride, size))
    return value


def shards(
    tokens,
    cotangent,
    region_ids,
    rel_bucket,
    norm_gain,
    in_weight,
    out_weight,
    bias_table,
    in_error,
    out_error,
    in_basis,
    out_basis,
):
    n_dp = lax.axis_size("dp")
    n_mp = lax.axis_size("mp")
    window_count, span, features = tokens.shape
    head_count, buckets = bias_table.shape
    rank = in_basis.shape[2]
    row_count = window_count * span
    row_block = in_weight.shape[0]
    wide = in_weight.shape[1]
    both = wide + features
    padded = -(-buckets // LANES) * LANES
    blocks = 2 if n_mp == 2 else 1
    token_rows = tokens.reshape(row_count, features)
    cot_rows = cotangent.reshape(row_count, features)
    gain = norm_gain.reshape(1, features)

    in_basis_t = jnp.swapaxes(in_basis[0], 0, 1)
    out_basis_t = jnp.swapaxes(out_basis[0], 0, 1)
    if blocks == 2:
        own = (in_weight, out_weight, in_basis_t, out_basis_t)
        arrived = [exchange(array, "mp", n_mp, 1) for array in own]
    else:
        own = (
            lax.all_gather(in_weight, "mp", axis=0, tiled=True),
            lax.all_gather(out_weight, "mp", axis=0, tiled=True),
            in_basis_t,
            out_basis_t,
        )
        arrived = []
    width = features // blocks

    operands = (
        rel_bucket,
        bias_table,
        token_rows,
        gain,
        own[0],
        cot_rows,
        region_ids,
        *own[1:],
        in_error[0],
        out_error[0],
    )
    normed, part, bias, index_t, table_pad, bucket, *kept = call(
        functools.partial(prepare_kernel, blocks, READY_HEADS),
        (
            shape((row_count, features), BF16),
            shape((row_count, wide), F32),
            shape((READY_HEADS, span, span), F32),
            shape((span, span), jnp.int32),
            shape((head_count, padded), F32),
            shape((span, span), jnp.int32),
        )
        + tuple(shape(array.shape, array.dtype) for array in operands[2:]),
        [pltpu.VMEM(bias_table.shape, F32), pltpu.SemaphoreType.DMA((12,))],
        flops=2 * row_count * width * wide,
        moved=4 << 20,
        in_specs=[HBM] * 12,
        out_specs=[VMEM] * 16,
    )(*in_hbm(*operands))
    token_rows, gain, w_in_own, cot_rows, region, *own, in_errors, out_errors = kept
    in_basis_t, out_basis_t = own[1:]

    left_shape = shape((2 * rank, width), F32)
    outputs = call(
        functools.partial(attend_kernel, blocks, 1.0 / n_mp),
        (shape((width, both), BF16),) * blocks
        + (left_shape,) * blocks
        + (shape((head_count, span, span), F32), shape((row_count, wide), BF16)),
        [
            pltpu.VMEM((row_count, wide), BF16),
            pltpu.VMEM((row_count, features), BF16),
            pltpu.VMEM((row_count, features), BF16),
            pltpu.VMEM((head_count, span, span), F32),
        ],
        flops=4 * row_count * features * both,
        moved=8 << 20,
        in_specs=[VMEM] * (12 + len(arrived)),
        out_specs=[VMEM] * (2 * blocks + 2),
    )(normed, part, bias, index_t, table_pad, bucket, cot_rows, region, w_in_own, *own, *arrived)
    *outputs, score_sum, packed = outputs
    terms, lefts = outputs[:blocks], outputs[blocks:]
    scores_of = [score_sum]

    if blocks == 2:
        left_other = exchange(lefts[1], "mp", n_mp, 1)
        left = lefts[0]
    else:
        term_parts = [lax.psum_scatter(terms[0], "mp", scatter_dimension=0, tiled=True)]
        left = call(
            functools.partial(shard_kernel, 1.0 / n_mp),
            shape((2 * rank, row_block), F32),
            in_specs=[VMEM] * 3,
            out_specs=VMEM,
        )(term_parts[0], in_basis_t, out_basis_t)

    left = call(
        error_kernel,
        shape((2 * rank, row_block), F32),
        flops=8 * row_block * both * rank,
        moved=3 << 20,
        in_specs=[VMEM] * 5,
        out_specs=VMEM,
    )(left, in_errors, out_errors, in_basis_t, out_basis_t)
    if blocks == 2:
        left, term_sent, score_sent = call(
            join_kernel,
            tuple(shape(array.shape, array.dtype) for array in (left, terms[1], score_sum)),
            in_specs=[VMEM] * 2 + [ANY] * 2,
            out_specs=[VMEM] + [ANY] * 2,
            input_output_aliases={2: 1, 3: 2},
        )(left, left_other, terms[1], score_sum)
        scores_of = [score_sent, exchange(score_sent, "mp", n_mp, 1)]
        terms = [terms[0], term_sent]
        term_parts = [terms[0], exchange(term_sent, "mp", n_mp, 1)]

    stats = call(
        functools.partial(table_kernel, blocks),
        shape((head_count, padded + 2 * LANES), F32),
        [pltpu.VMEM((1, features), F32)],
        flops=2 * row_count * features * wide,
        moved=4 << 20,
        in_specs=[VMEM] * (3 * blocks + 2),
        out_specs=VMEM,
    )(*scores_of, *terms, w_in_own, *arrived[:1], gain, index_t)
    if blocks == 2:
        stats = [stats, exchange(stats, "mp", n_mp, 1)]
    else:
        stats = [sum_over(stats, "mp", n_mp)]

    groups = digits(n_dp)
    for group in groups[:0:-1]:
        left = call(
            functools.partial(add_kernel, group[1]),
            shape(left.shape, F32),
            in_specs=[VMEM] * (group[1] + 1),
            out_specs=VMEM,
        )(*partners(left, "dp", n_dp, *group), stats[-1])
    stride, parts = groups[0]
    lefts = partners(left, "dp", n_dp, stride, parts)
    merged = call(
        functools.partial(merge_kernel, 1.0 / n_mp, len(term_parts)),
        shape((row_block, both), F32),
        flops=4 * row_block * both,
        moved=6 << 20,
        in_specs=[VMEM] * (len(term_parts) + 2),
        out_specs=VMEM,
    )(*term_parts, in_errors, out_errors)

    quarter = both // parts
    piece = shape((rank, quarter + LANES), BF16)
    ortho, *pieces = call(
        functools.partial(ortho_kernel, 1.0 / n_dp, len(lefts), len(stats)),
        (shape((2 * rank, row_block), F32),) + (piece,) * parts,
        [pltpu.VMEM((head_count, padded + 2 * LANES), F32)],
        flops=12 * row_block * both * rank,
        moved=3 << 20,
        in_specs=[VMEM] * (len(lefts) + len(stats) + 1),
        out_specs=[VMEM] * (1 + parts),
    )(*lefts, *stats, merged)

    token_grad, flag = call(
        functools.partial(token_kernel, blocks),
        (shape((row_count, features), BF16), shape((SUBLANES, LANES), F32)),
        [
            pltpu.VMEM((row_count, features), F32),
            pltpu.VMEM((row_count, features), BF16),
            pltpu.SemaphoreType.DMA((1,)),
        ],
        flops=2 * row_count * features * wide,
        moved=4 << 20,
        in_specs=[VMEM] * (blocks + 5),
        out_specs=[HBM, VMEM],
    )(packed, w_in_own, *arrived[:1], token_rows, cot_rows, gain, ortho)

    def reduced(values):
        return call(
            reduce_kernel,
            piece,
            in_specs=[VMEM] * (len(values) + 1),
            out_specs=VMEM,
            moved=1 << 18,
        )(*values, flag)

    held = reduced(
        [pieces[0]]
        + [exchange(pieces[step], "dp", n_dp, step * stride) for step in range(1, parts)]
    )
    for group in groups[1:]:
        held = reduced(partners(held, "dp", n_dp, *group))
    pieces = partners(held, "dp", n_dp, stride, parts)

    big = (
        shape((row_block, wide), F32),
        shape((row_block, features), F32),
        shape((row_block, wide), F32),
        shape((row_block, features), F32),
    )
    small = (
        shape((rank, wide), F32),
        shape((rank, features), F32),
        shape((head_count, buckets), F32),
        shape((1, features), F32),
    )
    early, late = (0, parts - 1), tuple(range(parts - 2, 0, -1))

    def staging(steps):
        return [pltpu.VMEM((len(steps), row_block, quarter), F32)] * 2 + [
            pltpu.SemaphoreType.DMA((len(steps), 2))
        ]

    results = call(
        functools.partial(first_kernel, 1.0 / n_dp, early),
        big,
        staging(early),
        flops=24 * row_block * quarter * rank,
        moved=1 << 20,
        in_specs=[VMEM] * (len(early) + 2),
        out_specs=[HBM] * 4,
    )(*(pieces[step] for step in early), ortho, merged)
    in_update, out_update, in_new_error, out_new_error, in_right, out_right, table, gain = call(
        functools.partial(last_kernel, 1.0 / n_dp, 1.0 / (n_dp * n_mp), late, parts),
        big + small,
        [pltpu.VMEM((parts, rank, quarter + LANES), F32)] + buffers(*small) + staging(late),
        flops=24 * row_block * quarter * rank,
        moved=1 << 20,
        in_specs=[VMEM] * (parts + 2) + [HBM] * 4,
        out_specs=[HBM] * 8,
        input_output_aliases={2 + parts + at: at for at in range(4)},
    )(*pieces, ortho, merged, *in_hbm(*results))

    return (
        token_grad.reshape(tokens.shape),
        gain.reshape(features),
        table,
        in_update,
        out_update,
        in_new_error[None],
        out_new_error[None],
        jnp.swapaxes(in_right, 0, 1)[None],
        jnp.swapaxes(out_right, 0, 1)[None],
    )


def solution(mesh):
    placed = (
        P(("dp", "mp"), None, None),
        P(("dp", "mp"), None, None),
        P(("dp", "mp"), None),
        P(),
        P(),
        P("mp", None),
        P("mp", None),
        P(),
        P("dp", "mp", None),
        P("dp", "mp", None),
        P("mp", None, None),
        P("mp", None, None),
    )
    return jax.shard_map(
        shards,
        mesh=mesh,
        in_specs=placed,
        out_specs=(
            P(("dp", "mp"), None, None),
            P(),
            P(),
            P("mp", None),
            P("mp", None),
            P("dp", "mp", None),
            P("dp", "mp", None),
            P("mp", None, None),
            P("mp", None, None),
        ),
        check_vma=False,
    )
```

```python
import functools

import jax
import jax.numpy as jnp
from jax import lax
from jax.experimental import pallas as pl
from jax.experimental.pallas import tpu as pltpu
from jax.sharding import PartitionSpec as P

NORM_EPS = 1e-05
BASIS_EPS = 1e-06
MASKED = -1e30
LANES = 128
SUBLANES = 8
READY_HEADS = 2
F32 = jnp.float32
BF16 = jnp.bfloat16

VMEM = pl.BlockSpec(memory_space=pltpu.VMEM)
HBM = pl.BlockSpec(memory_space=pltpu.HBM)
ANY = pl.BlockSpec(memory_space=pl.ANY)


def nn(a, b):
    return lax.dot_general(
        a, b, (((1,), (0,)), ((), ())), preferred_element_type=F32
    )


def nt(a, b):
    return lax.dot_general(
        a, b, (((1,), (1,)), ((), ())), preferred_element_type=F32
    )


def tn(a, b):
    return lax.dot_general(
        a, b, (((0,), (0,)), ((), ())), preferred_element_type=F32
    )


def block_columns(me, step, blocks, width):
    if blocks == 1:
        return pl.ds(0, width)
    index = me if step == 0 else 1 - me
    return pl.ds(pl.multiple_of(index * width, width), width)


def norm_forward(token_rows):
    tokens_wide = token_rows.astype(F32)
    mean_x = jnp.mean(tokens_wide, axis=-1, keepdims=True)
    centered = tokens_wide - mean_x
    variance = jnp.mean(centered * centered, axis=-1, keepdims=True)
    inv_sigma = lax.rsqrt(variance + NORM_EPS)
    return (centered * inv_sigma, inv_sigma)


def fetch(pairs, sems):
    copies = [
        pltpu.make_async_copy(source, target, sems.at[at])
        for at, (source, target) in enumerate(pairs)
    ]
    for copy in copies:
        copy.start()
    return copies


def halves(value):
    coarse = value.astype(BF16)
    return coarse, (value - coarse.astype(F32)).astype(BF16)


def stacked(value):
    return jnp.concatenate(halves(value), axis=0)


def folded(value):
    half = value.shape[0] // 2
    return value[:half] + value[half:]


def gather_bias(bias, heads, table_pad, index_t, index):
    span = index.shape[0]
    padded = table_pad.shape[1]
    even = span // LANES * LANES
    lookups = [(index_t[:, :even], False)] if even else []
    if even < span:
        lookups.append((index[even:, :], True))
    for places, flipped in lookups:
        rows, columns = places.shape
        for start in range(0, columns, LANES):
            stop = min(columns, start + LANES)
            part = places[:, start:stop]
            if stop - start < LANES:
                filler = jnp.zeros((rows, LANES - (stop - start)), jnp.int32)
                part = jnp.concatenate([part, filler], axis=1)
            high, low = part // LANES, part % LANES
            for head in heads:
                found = jnp.zeros((rows, LANES), F32)
                for level in range(padded // LANES):
                    row = table_pad[head : head + 1, level * LANES : (level + 1) * LANES]
                    row = jnp.broadcast_to(row, (rows, LANES))
                    picked = jnp.take_along_axis(row, low, axis=1, mode="promise_in_bounds")
                    found = jnp.where(high == level, picked, found)
                if flipped:
                    bias[head, start:stop, even:] = found[:, : stop - start].T
                else:
                    bias[head, :, start:stop] = found[:, : stop - start]


def prepare_kernel(blocks, ready, *refs):
    sources, rest = refs[:12], refs[12:]
    normed, normed_t, part, bias, index_t, table_pad, bucket, *kept = rest[:17]
    table, sems = rest[17:]
    copies = fetch(list(zip(sources, [bucket, table] + kept)), sems)
    tokens, gain, w_own = kept[:3]
    me = lax.axis_index("mp")
    width = w_own.shape[0]
    span = bucket.shape[0]
    head_count, padded = table_pad.shape
    for copy in copies[:2]:
        copy.wait()
    table_pad[...] = jnp.zeros_like(table_pad)
    table_pad[:, : table.shape[1]] = table[...]
    index_t[...] = bucket[...].T
    gather_bias(bias, range(ready), table_pad, index_t, bucket)
    for copy in copies[2:5]:
        copy.wait()
    x_hat, _ = norm_forward(tokens[...])
    normed[...] = (x_hat * gain[...]).astype(BF16)
    normed_t[...] = normed[...].T
    part[...] = nn(normed[:, block_columns(me, 0, blocks, width)], w_own[...])
    for copy in copies[5:]:
        copy.wait()


def attend_kernel(blocks, share, *refs):
    normed, normed_t, part, bias_ready, index_t, table_pad, bucket, cot, region = refs[:9]
    own, arrived = refs[9:13], refs[13 : 9 + 4 * blocks]
    rest = refs[9 + 4 * blocks :]
    terms, lefts, rest = rest[:blocks], rest[blocks : 2 * blocks], rest[2 * blocks :]
    score_sum, packed, proj, mixed_grad, mixed, bias = rest
    w_in, w_out, in_basis, out_basis = (
        [own[at]] + list(arrived[at : at + blocks - 1]) for at in range(4)
    )
    me = lax.axis_index("mp")
    window_count, span = region.shape
    features = normed.shape[1]
    ready, head_count = bias_ready.shape[0], bias.shape[0]
    head_size = features // head_count
    scale = head_size ** (-0.5)
    width = features // blocks
    if blocks == 1:
        proj[...] = part[...].astype(BF16)
    else:
        other = nn(normed[:, block_columns(me, 1, blocks, width)], w_in[1][...])
        proj[...] = (part[...] + other).astype(BF16)
    for step in range(blocks):
        mixed_grad[:, block_columns(me, step, blocks, width)] = nt(
            cot[...], w_out[step][...]
        ).astype(BF16)
    lane = lax.broadcasted_iota(jnp.int32, (span, LANES), 1)
    per_group = LANES // head_size
    allowed_in = []
    for window in range(window_count):
        ids_row = jnp.broadcast_to(region[window : window + 1, :], (span, span))
        allowed_in.append(ids_row == ids_row.T)
    wide = 3 * features
    rank = in_basis[0].shape[0]
    left_sums = [[] for _ in range(blocks)]
    span_columns = 2 * LANES
    for group in range(features // LANES):
        start = group * LANES
        heads = slice(group * per_group, (group + 1) * per_group)
        if heads.stop <= ready:
            pair_bias = bias_ready[heads]
        else:
            gather_bias(bias, range(heads.start, heads.stop), table_pad, index_t, bucket)
            pair_bias = bias[heads]
        for window in range(window_count):
            rows = pl.ds(window * span, span)
            allowed = allowed_in[window]
            q = proj[rows, start : start + LANES]
            k = proj[rows, features + start : features + start + LANES]
            v = proj[rows, 2 * features + start : 2 * features + start + LANES]
            g = mixed_grad[rows, start : start + LANES]
            pick = [lane // head_size == sub for sub in range(per_group)]
            k_split = jnp.concatenate([jnp.where(own, k, jnp.zeros_like(k)) for own in pick], 0)
            v_split = jnp.concatenate([jnp.where(own, v, jnp.zeros_like(v)) for own in pick], 0)
            scores = nt(k_split, q).reshape(per_group, span, span) * scale + pair_bias
            scores = jnp.where(allowed[None], scores, MASKED)
            top = jnp.max(scores, axis=1, keepdims=True)
            raised = jnp.exp(scores - top)
            prob = raised * (1.0 / jnp.sum(raised, axis=1, keepdims=True))
            prob_b = prob.astype(BF16)
            prob_grad = nt(v_split, g).reshape(per_group, span, span)
            inner = jnp.sum(prob * prob_grad, axis=1, keepdims=True)
            score_grad = prob * (prob_grad - inner)
            score_b = score_grad.astype(BF16)
            if window == 0:
                score_sum[heads] = score_grad
            else:
                score_sum[heads] += score_grad
            k_grads = nn(score_b.reshape(per_group * span, span), q)
            v_grads = nn(prob_b.reshape(per_group * span, span), g)

            def joined(parts):
                total = parts[0]
                for sub in range(1, per_group):
                    total = jnp.where(pick[sub], parts[sub], total)
                return total

            k_grad = joined([k_grads[at * span : (at + 1) * span] for at in range(per_group)])
            v_grad = joined([v_grads[at * span : (at + 1) * span] for at in range(per_group)])
            out = joined([tn(prob_b[at], v) for at in range(per_group)])
            q_grad = joined([tn(score_b[at], k) for at in range(per_group)])
            mixed[rows, start : start + LANES] = out.astype(BF16)
            packed[rows, start : start + LANES] = (q_grad * scale).astype(BF16)
            packed[rows, features + start : features + start + LANES] = (k_grad * scale).astype(
                BF16
            )
            packed[rows, 2 * features + start : 2 * features + start + LANES] = v_grad.astype(BF16)
        if (start + LANES) % span_columns:
            continue
        for third in range(3):
            first = third * features + start + LANES - span_columns
            columns = slice(first, first + span_columns)
            for step in range(blocks):
                rows = block_columns(me, step, blocks, width)
                term = nn(normed_t[rows, :], packed[:, columns]).astype(BF16)
                terms[step][:, columns] = term
                left_sums[step].append(nt(stacked(in_basis[step][:, columns]), term))
    for step in range(blocks):
        columns = block_columns(me, step, blocks, width)
        term = tn(mixed[:, columns], cot[...]).astype(BF16)
        terms[step][:, wide:] = term
        lefts[step][:rank, :] = folded(tree_add(left_sums[step])) * share
        lefts[step][rank:, :] = folded(nt(stacked(out_basis[step][...]), term)) * share


def token_kernel(blocks, packed, *refs):
    w_in, (tokens, cot, gain, _, result, flag, normed_grad, token_grad, sems) = (
        refs[:blocks],
        refs[blocks:],
    )
    me = lax.axis_index("mp")
    width = tokens.shape[1] // blocks
    for step in range(blocks):
        normed_grad[:, block_columns(me, step, blocks, width)] = nt(packed[...], w_in[step][...])
    x_hat, inv_sigma = norm_forward(tokens[...])
    hat_grad = normed_grad[...] * gain[...]
    token_delta = inv_sigma * (
        hat_grad
        - jnp.mean(hat_grad, axis=-1, keepdims=True)
        - x_hat * jnp.mean(hat_grad * x_hat, axis=-1, keepdims=True)
    )
    token_grad[...] = (cot[...].astype(F32) + token_delta).astype(BF16)
    flag[...] = jnp.zeros_like(flag)
    for copy in fetch([(token_grad, result)], sems):
        copy.wait()


def table_kernel(blocks, *refs):
    scores_of, terms = refs[:blocks], refs[blocks : 2 * blocks]
    w_in, rest = refs[2 * blocks : 3 * blocks], refs[3 * blocks :]
    gain, index_t, stats, gain_row = rest
    me = lax.axis_index("mp")
    features = gain.shape[1]
    for step in range(blocks):
        columns = block_columns(me, step, blocks, features // blocks)
        folds = tree_add(
            [
                terms[step][:, at : at + LANES].astype(F32)
                * w_in[step][:, at : at + LANES].astype(F32)
                for at in range(0, w_in[step].shape[1], LANES)
            ]
        )
        gain_row[:, columns] = jnp.sum(folds.T, axis=0, keepdims=True) / gain[:, columns]
    head_count, span, _ = scores_of[0].shape
    rows = span // blocks
    mine = block_columns(me, 0, blocks, rows)
    padded = stats.shape[1] - 2 * LANES
    levels = padded // LANES
    indices = index_t[mine, :]
    scores = tree_add([part[:, mine, :] for part in scores_of])
    sublane = lax.broadcasted_iota(jnp.int32, (LANES, span), 0)
    total = jnp.zeros((2 * levels * head_count, LANES), F32)
    for row in range(rows):
        index = indices[row : row + 1, :]
        high = jnp.broadcast_to(index // LANES, (head_count, span))
        low = jnp.broadcast_to(index % LANES, (LANES, span))
        one_hot = jnp.where(low == sublane, 1.0, 0.0).astype(BF16)
        values = scores[:, row, :]
        coarse = values.astype(BF16).astype(F32)
        fine = values - coarse
        picked = [
            jnp.where(high == level, piece, 0.0)
            for piece in (coarse, fine)
            for level in range(levels)
        ]
        total += nt(jnp.concatenate(picked, axis=0).astype(BF16), one_hot)
    total = folded(total)
    for level in range(levels):
        stats[:, level * LANES : (level + 1) * LANES] = total[
            level * head_count : (level + 1) * head_count
        ]
    stats[:, padded:] = jnp.zeros((head_count, 2 * LANES), F32)
    for piece in range(features // LANES):
        stats[piece : piece + 1, padded : padded + LANES] = gain_row[
            :, piece * LANES : (piece + 1) * LANES
        ]


def shard_kernel(share, shard, in_basis, out_basis, left):
    rank, split = in_basis.shape
    left[:rank, :] = folded(nt(stacked(in_basis[...]), shard[:, :split])) * share
    left[rank:, :] = folded(nt(stacked(out_basis[...]), shard[:, split:])) * share


def error_kernel(term_left, in_error, out_error, in_basis, out_basis, left):
    rank = in_basis.shape[0]
    for error, basis, at in ((in_error, in_basis, 0), (out_error, out_basis, rank)):
        coarse, fine = halves(error[...])
        pair = stacked(basis[...])
        left[at : at + rank, :] = term_left[at : at + rank, :] + folded(
            nt(pair, coarse) + nt(pair, fine)
        )


def merge_kernel(share, parts, *refs):
    shards, (in_error, out_error, merged) = refs[:parts], refs[parts:]
    split = in_error.shape[1]
    for columns, error in ((slice(None, split), in_error), (slice(split, None), out_error)):
        total = tree_add([shard[:, columns].astype(F32) for shard in shards])
        merged[:, columns] = total * share + error[...]


def tree_sum(values):
    while len(values) > 1:
        values = [values[at] + values[at + 1] for at in range(0, len(values), 2)]
    return values[0]


def tree_add(values):
    while len(values) > 1:
        odd = values[len(values) // 2 * 2 :]
        values = [values[at] + values[at + 1] for at in range(0, len(values) - 1, 2)] + odd
    return values[0]


def join_kernel(left_own, left_other, *refs):
    left = refs[len(refs) // 2]
    left[...] = left_own[...] + left_other[...]


def add_kernel(parts, *refs):
    refs[-1][...] = tree_sum([ref[...] for ref in refs[:parts]])


def stats_pieces(pair):
    pieces = []
    for at in range(2):
        tile = pair[:, at * LANES : (at + 1) * LANES]
        coarse, fine = halves(tile)
        pieces += [coarse.astype(F32), fine.astype(F32)]
    return jnp.concatenate(pieces, axis=0).astype(BF16)


def stats_pair(pieces):
    rows = pieces.shape[0] // 4
    return jnp.concatenate(
        [
            pieces[2 * at * rows : (2 * at + 1) * rows]
            + pieces[(2 * at + 1) * rows : (2 * at + 2) * rows]
            for at in range(2)
        ],
        axis=1,
    )


def orthonormal(problems):
    rank, rows = problems[0].shape
    tiles = rank // SUBLANES
    spread_shape = (SUBLANES, rows)
    place = lax.broadcasted_iota(jnp.int32, spread_shape, 0)

    def dots(rows_of, vector):
        return jnp.sum(rows_of * vector, axis=1, keepdims=True)

    def spread(tiled, row):
        tile, at = divmod(row, SUBLANES)
        return jnp.broadcast_to(tiled[tile][at : at + 1], spread_shape)

    states = []
    for first in problems:
        original = [first[at * SUBLANES : (at + 1) * SUBLANES] for at in range(tiles)]
        states.append((original, list(original), [jnp.zeros(spread_shape, F32)] * tiles))
    def project(finished, found):
        weighted = tree_add([found[q] * finished[q] for q in found])
        return jnp.sum(weighted, axis=0, keepdims=True)

    currents = [spread(original, 0) for original, _, _ in states]
    known = [None for _ in states]
    for column in range(rank):
        tile, at = divmod(column, SUBLANES)
        before = range((column - 1) // SUBLANES + 1)
        for which, (original, residual, finished) in enumerate(states):
            current = currents[which]
            square = dots(current, current)
            inverse = lax.rsqrt(square + BASIS_EPS)
            unit = current * inverse
            if column + 1 < rank:
                ahead = spread(residual, column + 1)
                step = dots(spread(original, column + 1), current) * inverse
                own = dots(ahead, current) * inverse
                following = ahead - unit * (step + own - step * (square * inverse * inverse))
                if column:
                    cross = project(finished, {q: dots(finished[q], current) for q in before})
                    following = following - known[which] + (step * inverse) * cross
            finished[tile] = jnp.where(place == at, unit, finished[tile])
            if column + 1 < rank:
                for q in range((column + 1) // SUBLANES, tiles):
                    residual[q] = residual[q] - (dots(original[q], current) * inverse) * unit
                currents[which] = following
            if column + 2 < rank:
                far = spread(residual, column + 2)
                known[which] = project(
                    finished, {q: dots(finished[q], far) for q in range(tile + 1)}
                )
    return [jnp.concatenate(finished, axis=0) for _, _, finished in states]


def ortho_kernel(share, parts, stat_parts, *refs):
    lefts, stats = refs[:parts], refs[parts : parts + stat_parts]
    merged, ortho, *pieces, sums = refs[parts + stat_parts :]
    digit = lax.axis_index("dp") % 4
    rank = ortho.shape[0] // 2
    quarter = merged.shape[1] // len(pieces)
    sums[...] = tree_sum([stat[...] for stat in stats])
    total = tree_sum([left[...] for left in lefts]) * share
    finished = orthonormal([total[:rank], total[rank:]])
    ortho[:rank, :], ortho[rank:, :] = finished
    for step, piece in enumerate(pieces):
        block = jnp.bitwise_xor(digit, step)
        columns = pl.ds(pl.multiple_of(block * quarter, quarter), quarter)
        pair = stacked(jnp.where(block < len(pieces) - 1, finished[0], finished[1]))
        piece[:, :quarter] = folded(nn(pair, merged[:, columns].astype(BF16))).astype(BF16)
        stat_columns = pl.ds(pl.multiple_of(block * 2 * LANES, 2 * LANES), 2 * LANES)
        piece[:, quarter:] = stats_pieces(sums[:, stat_columns])


def reduce_kernel(*refs):
    pieces, total = refs[:-2], refs[-1]
    quarter = total.shape[1] - LANES
    summed = tree_sum([piece[...].astype(F32) for piece in pieces])
    total[:, :quarter] = summed[:, :quarter].astype(BF16)
    total[:, quarter:] = stats_pieces(stats_pair(summed[:, quarter:]))


def update_blocks(share, steps, pieces, ortho, merged, results, updates, errors, sems, small):
    in_update, out_update, in_new_error, out_new_error = results
    rank = ortho.shape[0] // 2
    quarter = updates.shape[2]
    count = merged.shape[1] // quarter
    places = []
    for at, step in enumerate(steps):
        block = jnp.bitwise_xor(lax.axis_index("dp") % 4, step)
        columns = pl.ds(pl.multiple_of(block * quarter, quarter), quarter)
        right = pieces[step][:, :quarter].astype(F32) * share
        own_coarse, own_fine = halves(
            jnp.where(block < count - 1, ortho[:rank, :], ortho[rank:, :])
        )
        coarse, fine = halves(right)
        update = tn(
            jnp.concatenate([own_coarse, own_coarse, own_fine], axis=0),
            jnp.concatenate([coarse, fine, coarse], axis=0),
        )
        updates[at] = update
        errors[at] = merged[:, columns] - update
        places.append((block, columns))

        @pl.when(block < count - 1)
        def _():
            targets = in_update.at[:, columns], in_new_error.at[:, columns]
            fetch(list(zip((updates.at[at], errors.at[at]), targets)), sems.at[at])

        @pl.when(block == count - 1)
        def _():
            targets = out_update, out_new_error
            fetch(list(zip((updates.at[at], errors.at[at]), targets)), sems.at[at])

    small()
    for at, (block, columns) in enumerate(places):
        pltpu.make_async_copy(updates.at[at], out_update, sems.at[at, 0]).wait()
        pltpu.make_async_copy(errors.at[at], out_new_error, sems.at[at, 1]).wait()


def first_kernel(share, steps, *refs):
    count = len(steps)
    pieces = dict(zip(steps, refs[:count]))
    ortho, merged = refs[count : count + 2]
    results, (updates, errors, sems) = refs[count + 2 : count + 6], refs[count + 6 :]
    update_blocks(share, steps, pieces, ortho, merged, results, updates, errors, sems, lambda: None)


def last_kernel(share, stat_share, steps, parts, *refs):
    pieces, (ortho, merged) = refs[:parts], refs[parts : parts + 2]
    results, small_results = refs[parts + 6 : parts + 10], refs[parts + 10 : parts + 14]
    rights, *small = refs[parts + 14 : parts + 19]
    small_sems, updates, errors, sems = refs[parts + 19 :]
    in_basis, out_basis, table, gain = small
    quarter = rights.shape[2] - LANES
    copies = []

    def small_outputs():
        for step, piece in enumerate(pieces):
            rights[step] = piece[...].astype(F32)
        tiles = []
        for block in range(parts):
            here = rights[jnp.bitwise_xor(lax.axis_index("dp") % 4, block)]
            right = here[:, :quarter] * share
            tiles.append(stats_pair(here[:, quarter:]) * stat_share)
            if block < parts - 1:
                in_basis[:, block * quarter : (block + 1) * quarter] = right
            else:
                out_basis[...] = right
        stats = jnp.concatenate(tiles, axis=1)
        table[...] = stats[:, : table.shape[1]]
        padded = stats.shape[1] - 2 * LANES
        for at in range(gain.shape[1] // LANES):
            gain[:, at * LANES : (at + 1) * LANES] = stats[at : at + 1, padded : padded + LANES]
        copies.extend(fetch(list(zip(small, small_results)), small_sems))

    update_blocks(
        share, steps, pieces, ortho, merged, results, updates, errors, sems, small_outputs
    )
    for copy in copies:
        copy.wait()


def call(kernel, outs, scratch=(), flops=0, moved=0, vmem=16, **options):
    return pl.pallas_call(
        kernel,
        out_shape=outs,
        scratch_shapes=list(scratch),
        cost_estimate=pl.CostEstimate(flops=flops, bytes_accessed=moved, transcendentals=0),
        compiler_params=pltpu.CompilerParams(vmem_limit_bytes=vmem << 20),
        **options,
    )


def buffers(*arrays):
    return [pltpu.VMEM(array.shape, array.dtype) for array in arrays] + [
        pltpu.SemaphoreType.DMA((len(arrays),))
    ]


def in_hbm(*arrays):
    return [pltpu.with_memory_space_constraint(array, pltpu.HBM) for array in arrays]


def shape(dims, dtype):
    return jax.ShapeDtypeStruct(dims, dtype)


def exchange(value, axis, count, distance):
    return lax.ppermute(value, axis, [(at, at ^ distance) for at in range(count)])


def digits(count):
    groups, stride = [], 1
    while stride < count:
        size = 4 if count // stride % 4 == 0 else 2
        groups.append((stride, size))
        stride *= size
    return groups


def partners(value, axis, count, stride, size):
    return [value] + [exchange(value, axis, count, step * stride) for step in range(1, size)]


def sum_over(value, axis, count):
    for stride, size in digits(count):
        value = tree_sum(partners(value, axis, count, stride, size))
    return value


def shards(
    tokens,
    cotangent,
    region_ids,
    rel_bucket,
    norm_gain,
    in_weight,
    out_weight,
    bias_table,
    in_error,
    out_error,
    in_basis,
    out_basis,
):
    n_dp = lax.axis_size("dp")
    n_mp = lax.axis_size("mp")
    window_count, span, features = tokens.shape
    head_count, buckets = bias_table.shape
    rank = in_basis.shape[2]
    row_count = window_count * span
    row_block = in_weight.shape[0]
    wide = in_weight.shape[1]
    both = wide + features
    padded = -(-buckets // LANES) * LANES
    blocks = 2 if n_mp == 2 else 1
    token_rows = tokens.reshape(row_count, features)
    cot_rows = cotangent.reshape(row_count, features)
    gain = norm_gain.reshape(1, features)

    in_basis_t = jnp.swapaxes(in_basis[0], 0, 1)
    out_basis_t = jnp.swapaxes(out_basis[0], 0, 1)
    if blocks == 2:
        own = (in_weight, out_weight, in_basis_t, out_basis_t)
        arrived = [exchange(array, "mp", n_mp, 1) for array in own]
    else:
        own = (
            lax.all_gather(in_weight, "mp", axis=0, tiled=True),
            lax.all_gather(out_weight, "mp", axis=0, tiled=True),
            in_basis_t,
            out_basis_t,
        )
        arrived = []
    width = features // blocks

    operands = (
        rel_bucket,
        bias_table,
        token_rows,
        gain,
        own[0],
        cot_rows,
        region_ids,
        *own[1:],
        in_error[0],
        out_error[0],
    )
    normed, normed_t, part, bias, index_t, table_pad, bucket, *kept = call(
        functools.partial(prepare_kernel, blocks, READY_HEADS),
        (
            shape((row_count, features), BF16),
            shape((features, row_count), BF16),
            shape((row_count, wide), F32),
            shape((READY_HEADS, span, span), F32),
            shape((span, span), jnp.int32),
            shape((head_count, padded), F32),
            shape((span, span), jnp.int32),
        )
        + tuple(shape(array.shape, array.dtype) for array in operands[2:]),
        [pltpu.VMEM(bias_table.shape, F32), pltpu.SemaphoreType.DMA((12,))],
        flops=2 * row_count * width * wide,
        moved=4 << 20,
        in_specs=[HBM] * 12,
        out_specs=[VMEM] * 17,
    )(*in_hbm(*operands))
    token_rows, gain, w_in_own, cot_rows, region, *own, in_errors, out_errors = kept
    in_basis_t, out_basis_t = own[1:]

    left_shape = shape((2 * rank, width), F32)
    outputs = call(
        functools.partial(attend_kernel, blocks, 1.0 / n_mp),
        (shape((width, both), BF16),) * blocks
        + (left_shape,) * blocks
        + (shape((head_count, span, span), F32), shape((row_count, wide), BF16)),
        [
            pltpu.VMEM((row_count, wide), BF16),
            pltpu.VMEM((row_count, features), BF16),
            pltpu.VMEM((row_count, features), BF16),
            pltpu.VMEM((head_count, span, span), F32),
        ],
        flops=4 * row_count * features * both,
        moved=8 << 20,
        in_specs=[VMEM] * (13 + len(arrived)),
        out_specs=[VMEM] * (2 * blocks + 2),
    )(normed, normed_t, part, bias, index_t, table_pad, bucket, cot_rows, region, w_in_own, *own, *arrived)
    *outputs, score_sum, packed = outputs
    terms, lefts = outputs[:blocks], outputs[blocks:]
    scores_of = [score_sum]

    if blocks == 2:
        left_other = exchange(lefts[1], "mp", n_mp, 1)
        left = lefts[0]
    else:
        term_parts = [lax.psum_scatter(terms[0], "mp", scatter_dimension=0, tiled=True)]
        left = call(
            functools.partial(shard_kernel, 1.0 / n_mp),
            shape((2 * rank, row_block), F32),
            in_specs=[VMEM] * 3,
            out_specs=VMEM,
        )(term_parts[0], in_basis_t, out_basis_t)

    left = call(
        error_kernel,
        shape((2 * rank, row_block), F32),
        flops=8 * row_block * both * rank,
        moved=3 << 20,
        in_specs=[VMEM] * 5,
        out_specs=VMEM,
    )(left, in_errors, out_errors, in_basis_t, out_basis_t)
    if blocks == 2:
        left, term_sent, score_sent = call(
            join_kernel,
            tuple(shape(array.shape, array.dtype) for array in (left, terms[1], score_sum)),
            in_specs=[VMEM] * 2 + [ANY] * 2,
            out_specs=[VMEM] + [ANY] * 2,
            input_output_aliases={2: 1, 3: 2},
        )(left, left_other, terms[1], score_sum)
        scores_of = [score_sent, exchange(score_sent, "mp", n_mp, 1)]
        terms = [terms[0], term_sent]
        term_parts = [terms[0], exchange(term_sent, "mp", n_mp, 1)]

    stats = call(
        functools.partial(table_kernel, blocks),
        shape((head_count, padded + 2 * LANES), F32),
        [pltpu.VMEM((1, features), F32)],
        flops=2 * row_count * features * wide,
        moved=4 << 20,
        in_specs=[VMEM] * (3 * blocks + 2),
        out_specs=VMEM,
    )(*scores_of, *terms, w_in_own, *arrived[:1], gain, index_t)
    if blocks == 2:
        stats = [stats, exchange(stats, "mp", n_mp, 1)]
    else:
        stats = [sum_over(stats, "mp", n_mp)]

    groups = digits(n_dp)
    for group in groups[:0:-1]:
        left = call(
            functools.partial(add_kernel, group[1]),
            shape(left.shape, F32),
            in_specs=[VMEM] * (group[1] + 1),
            out_specs=VMEM,
        )(*partners(left, "dp", n_dp, *group), stats[-1])
    stride, parts = groups[0]
    lefts = partners(left, "dp", n_dp, stride, parts)
    merged = call(
        functools.partial(merge_kernel, 1.0 / n_mp, len(term_parts)),
        shape((row_block, both), F32),
        flops=4 * row_block * both,
        moved=6 << 20,
        in_specs=[VMEM] * (len(term_parts) + 2),
        out_specs=VMEM,
    )(*term_parts, in_errors, out_errors)

    quarter = both // parts
    piece = shape((rank, quarter + LANES), BF16)
    ortho, *pieces = call(
        functools.partial(ortho_kernel, 1.0 / n_dp, len(lefts), len(stats)),
        (shape((2 * rank, row_block), F32),) + (piece,) * parts,
        [pltpu.VMEM((head_count, padded + 2 * LANES), F32)],
        flops=12 * row_block * both * rank,
        moved=3 << 20,
        in_specs=[VMEM] * (len(lefts) + len(stats) + 1),
        out_specs=[VMEM] * (1 + parts),
    )(*lefts, *stats, merged)

    token_grad, flag = call(
        functools.partial(token_kernel, blocks),
        (shape((row_count, features), BF16), shape((SUBLANES, LANES), F32)),
        [
            pltpu.VMEM((row_count, features), F32),
            pltpu.VMEM((row_count, features), BF16),
            pltpu.SemaphoreType.DMA((1,)),
        ],
        flops=2 * row_count * features * wide,
        moved=4 << 20,
        in_specs=[VMEM] * (blocks + 5),
        out_specs=[HBM, VMEM],
    )(packed, w_in_own, *arrived[:1], token_rows, cot_rows, gain, ortho)

    def reduced(values):
        return call(
            reduce_kernel,
            piece,
            in_specs=[VMEM] * (len(values) + 1),
            out_specs=VMEM,
            moved=1 << 18,
        )(*values, flag)

    held = reduced(
        [pieces[0]]
        + [exchange(pieces[step], "dp", n_dp, step * stride) for step in range(1, parts)]
    )
    for group in groups[1:]:
        held = reduced(partners(held, "dp", n_dp, *group))
    pieces = partners(held, "dp", n_dp, stride, parts)

    big = (
        shape((row_block, wide), F32),
        shape((row_block, features), F32),
        shape((row_block, wide), F32),
        shape((row_block, features), F32),
    )
    small = (
        shape((rank, wide), F32),
        shape((rank, features), F32),
        shape((head_count, buckets), F32),
        shape((1, features), F32),
    )
    early, late = (0, parts - 1), tuple(range(parts - 2, 0, -1))

    def staging(steps):
        return [pltpu.VMEM((len(steps), row_block, quarter), F32)] * 2 + [
            pltpu.SemaphoreType.DMA((len(steps), 2))
        ]

    results = call(
        functools.partial(first_kernel, 1.0 / n_dp, early),
        big,
        staging(early),
        flops=24 * row_block * quarter * rank,
        moved=1 << 20,
        in_specs=[VMEM] * (len(early) + 2),
        out_specs=[HBM] * 4,
    )(*(pieces[step] for step in early), ortho, merged)
    in_update, out_update, in_new_error, out_new_error, in_right, out_right, table, gain = call(
        functools.partial(last_kernel, 1.0 / n_dp, 1.0 / (n_dp * n_mp), late, parts),
        big + small,
        [pltpu.VMEM((parts, rank, quarter + LANES), F32)] + buffers(*small) + staging(late),
        flops=24 * row_block * quarter * rank,
        moved=1 << 20,
        in_specs=[VMEM] * (parts + 2) + [HBM] * 4,
        out_specs=[HBM] * 8,
        input_output_aliases={2 + parts + at: at for at in range(4)},
    )(*pieces, ortho, merged, *in_hbm(*results))

    return (
        token_grad.reshape(tokens.shape),
        gain.reshape(features),
        table,
        in_update,
        out_update,
        in_new_error[None],
        out_new_error[None],
        jnp.swapaxes(in_right, 0, 1)[None],
        jnp.swapaxes(out_right, 0, 1)[None],
    )


def solution(mesh):
    placed = (
        P(("dp", "mp"), None, None),
        P(("dp", "mp"), None, None),
        P(("dp", "mp"), None),
        P(),
        P(),
        P("mp", None),
        P("mp", None),
        P(),
        P("dp", "mp", None),
        P("dp", "mp", None),
        P("mp", None, None),
        P("mp", None, None),
    )
    return jax.shard_map(
        shards,
        mesh=mesh,
        in_specs=placed,
        out_specs=(
            P(("dp", "mp"), None, None),
            P(),
            P(),
            P("mp", None),
            P("mp", None),
            P("dp", "mp", None),
            P("dp", "mp", None),
            P("mp", None, None),
            P("mp", None, None),
        ),
        check_vma=False,
    )
```

```python
import functools

import jax
import jax.numpy as jnp
from jax import lax
from jax.experimental import pallas as pl
from jax.experimental.pallas import tpu as pltpu
from jax.sharding import PartitionSpec as P

NORM_EPS = 1e-05
BASIS_EPS = 1e-06
MASKED = -1e30
LANES = 128
SUBLANES = 8
TILE_ROWS = 16
READY_HEADS = 2
F32 = jnp.float32
BF16 = jnp.bfloat16

VMEM = pl.BlockSpec(memory_space=pltpu.VMEM)
HBM = pl.BlockSpec(memory_space=pltpu.HBM)
ANY = pl.BlockSpec(memory_space=pl.ANY)


def nn(a, b):
    return lax.dot_general(
        a, b, (((1,), (0,)), ((), ())), preferred_element_type=F32
    )


def nt(a, b):
    return lax.dot_general(
        a, b, (((1,), (1,)), ((), ())), preferred_element_type=F32
    )


def tn(a, b):
    return lax.dot_general(
        a, b, (((0,), (0,)), ((), ())), preferred_element_type=F32
    )


def block_columns(me, step, blocks, width):
    if blocks == 1:
        return pl.ds(0, width)
    index = me if step == 0 else 1 - me
    return pl.ds(pl.multiple_of(index * width, width), width)


def norm_forward(token_rows):
    tokens_wide = token_rows.astype(F32)
    mean_x = jnp.mean(tokens_wide, axis=-1, keepdims=True)
    centered = tokens_wide - mean_x
    variance = jnp.mean(centered * centered, axis=-1, keepdims=True)
    inv_sigma = lax.rsqrt(variance + NORM_EPS)
    return (centered * inv_sigma, inv_sigma)


def fetch(pairs, sems):
    copies = [
        pltpu.make_async_copy(source, target, sems.at[at])
        for at, (source, target) in enumerate(pairs)
    ]
    for copy in copies:
        copy.start()
    return copies


def halves(value):
    coarse = value.astype(BF16)
    return coarse, (value - coarse.astype(F32)).astype(BF16)


def stacked(value):
    return jnp.concatenate(halves(value), axis=0)


def folded(value):
    half = value.shape[0] // 2
    return value[:half] + value[half:]


def gather_bias(bias, heads, table_pad, index_t, index):
    span = index.shape[0]
    padded = table_pad.shape[1]
    even = span // LANES * LANES
    lookups = [(index_t[:, :even], False)] if even else []
    if even < span:
        lookups.append((index[even:, :], True))
    for places, flipped in lookups:
        rows, columns = places.shape
        for start in range(0, columns, LANES):
            stop = min(columns, start + LANES)
            part = places[:, start:stop]
            if stop - start < LANES:
                filler = jnp.zeros((rows, LANES - (stop - start)), jnp.int32)
                part = jnp.concatenate([part, filler], axis=1)
            high, low = part // LANES, part % LANES
            for head in heads:
                found = jnp.zeros((rows, LANES), F32)
                for level in range(padded // LANES):
                    row = table_pad[head : head + 1, level * LANES : (level + 1) * LANES]
                    row = jnp.broadcast_to(row, (rows, LANES))
                    picked = jnp.take_along_axis(row, low, axis=1, mode="promise_in_bounds")
                    found = jnp.where(high == level, picked, found)
                if flipped:
                    bias[head, start:stop, even:] = found[:, : stop - start].T
                else:
                    bias[head, :, start:stop] = found[:, : stop - start]


def prepare_kernel(blocks, ready, *refs):
    sources, rest = refs[:12], refs[12:]
    normed, normed_t, part, bias, index_t, table_pad, bucket, *kept = rest[:17]
    table, sems = rest[17:]
    copies = fetch(list(zip(sources, [bucket, table] + kept)), sems)
    tokens, gain, w_own = kept[:3]
    me = lax.axis_index("mp")
    width = w_own.shape[0]
    span = bucket.shape[0]
    head_count, padded = table_pad.shape
    for copy in copies[:2]:
        copy.wait()
    table_pad[...] = jnp.zeros_like(table_pad)
    table_pad[:, : table.shape[1]] = table[...]
    index_t[...] = bucket[...].T
    gather_bias(bias, range(ready), table_pad, index_t, bucket)
    for copy in copies[2:5]:
        copy.wait()
    x_hat, _ = norm_forward(tokens[...])
    normed[...] = (x_hat * gain[...]).astype(BF16)
    normed_t[...] = normed[...].T
    part[...] = nn(normed[:, block_columns(me, 0, blocks, width)], w_own[...])
    for copy in copies[5:]:
        copy.wait()


def attend_kernel(blocks, share, *refs):
    normed, normed_t, part, bias_ready, index_t, table_pad, bucket, cot, region = refs[:9]
    own, arrived = refs[9:13], refs[13 : 9 + 4 * blocks]
    rest = refs[9 + 4 * blocks :]
    terms, lefts, rest = rest[:blocks], rest[blocks : 2 * blocks], rest[2 * blocks :]
    score_sum, packed, proj, mixed_grad, mixed, bias = rest
    w_in, w_out, in_basis, out_basis = (
        [own[at]] + list(arrived[at : at + blocks - 1]) for at in range(4)
    )
    me = lax.axis_index("mp")
    window_count, span = region.shape
    features = normed.shape[1]
    ready, head_count = bias_ready.shape[0], bias.shape[0]
    head_size = features // head_count
    scale = head_size ** (-0.5)
    width = features // blocks
    if blocks == 1:
        proj[...] = part[...].astype(BF16)
    else:
        other = nn(normed[:, block_columns(me, 1, blocks, width)], w_in[1][...])
        proj[...] = (part[...] + other).astype(BF16)
    for step in range(blocks):
        mixed_grad[:, block_columns(me, step, blocks, width)] = nt(
            cot[...], w_out[step][...]
        ).astype(BF16)
    lane = lax.broadcasted_iota(jnp.int32, (span, LANES), 1)
    per_group = LANES // head_size
    for window in range(window_count):
        rows = pl.ds(window * span, span)
        ids_row = jnp.broadcast_to(region[window : window + 1, :], (span, span))
        allowed = ids_row == ids_row.T
        for group in range(features // LANES):
            start = group * LANES
            heads = slice(group * per_group, (group + 1) * per_group)
            if heads.stop <= ready:
                pair_bias = bias_ready[heads]
            else:
                if window == 0:
                    gather_bias(bias, range(heads.start, heads.stop), table_pad, index_t, bucket)
                pair_bias = bias[heads]
            q = proj[rows, start : start + LANES] * jnp.asarray(scale, BF16)
            k = proj[rows, features + start : features + start + LANES]
            v = proj[rows, 2 * features + start : 2 * features + start + LANES]
            g = mixed_grad[rows, start : start + LANES]
            pick = [lane // head_size == sub for sub in range(per_group)]
            k_split = jnp.concatenate([jnp.where(own, k, jnp.zeros_like(k)) for own in pick], 0)
            v_split = jnp.concatenate([jnp.where(own, v, jnp.zeros_like(v)) for own in pick], 0)
            scores = nt(k_split, q).reshape(per_group, span, span) + pair_bias
            scores = jnp.where(allowed[None], scores, MASKED)
            top = jnp.max(scores, axis=1, keepdims=True)
            raised = jnp.exp(scores - top)
            prob = raised * (1.0 / jnp.sum(raised, axis=1, keepdims=True))
            prob_b = prob.astype(BF16)
            prob_grad = nt(v_split, g).reshape(per_group, span, span)
            inner = jnp.sum(prob * prob_grad, axis=1, keepdims=True)
            score_grad = prob * (prob_grad - inner)
            score_b = score_grad.astype(BF16)
            if window == 0:
                score_sum[heads] = score_grad
            else:
                score_sum[heads] += score_grad
            k_grads = nn(score_b.reshape(per_group * span, span), q)
            v_grads = nn(prob_b.reshape(per_group * span, span), g)

            def joined(parts):
                total = parts[0]
                for sub in range(1, per_group):
                    total = jnp.where(pick[sub], parts[sub], total)
                return total

            k_grad = joined([k_grads[at * span : (at + 1) * span] for at in range(per_group)])
            v_grad = joined([v_grads[at * span : (at + 1) * span] for at in range(per_group)])
            out = joined([tn(prob_b[at], v) for at in range(per_group)])
            q_grad = joined([tn(score_b[at], k) for at in range(per_group)])
            mixed[rows, start : start + LANES] = out.astype(BF16)
            packed[rows, start : start + LANES] = (q_grad * scale).astype(BF16)
            packed[rows, features + start : features + start + LANES] = k_grad.astype(BF16)
            packed[rows, 2 * features + start : 2 * features + start + LANES] = v_grad.astype(BF16)
    wide = 3 * features
    for step in range(blocks):
        columns = block_columns(me, step, blocks, width)
        terms[step][:, :wide] = nn(normed_t[columns, :], packed[...]).astype(BF16)
        terms[step][:, wide:] = tn(mixed[:, columns], cot[...]).astype(BF16)
        rank = in_basis[step].shape[0]
        for basis, at, place in (
            (in_basis[step], slice(None, wide), 0),
            (out_basis[step], slice(wide, None), rank),
        ):
            left = folded(nt(stacked(basis[...]), terms[step][:, at])) * share
            lefts[step][place : place + rank, :] = left


def token_kernel(blocks, packed, *refs):
    w_in, (tokens, cot, gain, _, result, flag, normed_grad, token_grad, sems) = (
        refs[:blocks],
        refs[blocks:],
    )
    me = lax.axis_index("mp")
    width = tokens.shape[1] // blocks
    for step in range(blocks):
        normed_grad[:, block_columns(me, step, blocks, width)] = nt(packed[...], w_in[step][...])
    x_hat, inv_sigma = norm_forward(tokens[...])
    hat_grad = normed_grad[...] * gain[...]
    token_delta = inv_sigma * (
        hat_grad
        - jnp.mean(hat_grad, axis=-1, keepdims=True)
        - x_hat * jnp.mean(hat_grad * x_hat, axis=-1, keepdims=True)
    )
    token_grad[...] = (cot[...].astype(F32) + token_delta).astype(BF16)
    flag[...] = jnp.zeros_like(flag)
    for copy in fetch([(token_grad, result)], sems):
        copy.wait()


def table_kernel(blocks, *refs):
    scores_of, terms = refs[:blocks], refs[blocks : 2 * blocks]
    w_in, rest = refs[2 * blocks : 3 * blocks], refs[3 * blocks :]
    gain, index_t, stats, gain_row = rest
    me = lax.axis_index("mp")
    features = gain.shape[1]
    for step in range(blocks):
        columns = block_columns(me, step, blocks, features // blocks)
        folds = tree_add(
            [
                terms[step][:, at : at + LANES].astype(F32)
                * w_in[step][:, at : at + LANES].astype(F32)
                for at in range(0, w_in[step].shape[1], LANES)
            ]
        )
        gain_row[:, columns] = jnp.sum(folds.T, axis=0, keepdims=True) / gain[:, columns]
    head_count, span, _ = scores_of[0].shape
    rows = span // blocks
    mine = block_columns(me, 0, blocks, rows)
    padded = stats.shape[1] - 2 * LANES
    levels = padded // LANES
    indices = index_t[mine, :]
    scores = tree_add([part[:, mine, :] for part in scores_of])
    sublane = lax.broadcasted_iota(jnp.int32, (LANES, span), 0)
    total = jnp.zeros((2 * levels * head_count, LANES), F32)
    for row in range(rows):
        index = indices[row : row + 1, :]
        high = jnp.broadcast_to(index // LANES, (head_count, span))
        low = jnp.broadcast_to(index % LANES, (LANES, span))
        one_hot = jnp.where(low == sublane, 1.0, 0.0).astype(BF16)
        values = scores[:, row, :]
        coarse = values.astype(BF16).astype(F32)
        fine = values - coarse
        picked = [
            jnp.where(high == level, piece, 0.0)
            for piece in (coarse, fine)
            for level in range(levels)
        ]
        total += nt(jnp.concatenate(picked, axis=0).astype(BF16), one_hot)
    total = folded(total)
    for level in range(levels):
        stats[:, level * LANES : (level + 1) * LANES] = total[
            level * head_count : (level + 1) * head_count
        ]
    stats[:, padded:] = jnp.zeros((head_count, 2 * LANES), F32)
    for piece in range(features // LANES):
        stats[piece : piece + 1, padded : padded + LANES] = gain_row[
            :, piece * LANES : (piece + 1) * LANES
        ]


def shard_kernel(share, shard, in_basis, out_basis, left):
    rank, split = in_basis.shape
    left[:rank, :] = folded(nt(stacked(in_basis[...]), shard[:, :split])) * share
    left[rank:, :] = folded(nt(stacked(out_basis[...]), shard[:, split:])) * share


def error_kernel(term_left, in_error, out_error, in_basis, out_basis, left):
    rank = in_basis.shape[0]
    for error, basis, at in ((in_error, in_basis, 0), (out_error, out_basis, rank)):
        coarse, fine = halves(error[...])
        pair = stacked(basis[...])
        left[at : at + rank, :] = term_left[at : at + rank, :] + folded(
            nt(pair, coarse) + nt(pair, fine)
        )


def merge_kernel(share, parts, *refs):
    shards, (in_error, out_error, merged) = refs[:parts], refs[parts:]
    split = in_error.shape[1]
    for columns, error in ((slice(None, split), in_error), (slice(split, None), out_error)):
        total = tree_add([shard[:, columns].astype(F32) for shard in shards])
        merged[:, columns] = total * share + error[...]


def tree_sum(values):
    while len(values) > 1:
        values = [values[at] + values[at + 1] for at in range(0, len(values), 2)]
    return values[0]


def tree_add(values):
    while len(values) > 1:
        odd = values[len(values) // 2 * 2 :]
        values = [values[at] + values[at + 1] for at in range(0, len(values) - 1, 2)] + odd
    return values[0]


def join_kernel(left_own, left_other, *refs):
    left = refs[len(refs) // 2]
    left[...] = left_own[...] + left_other[...]


def add_kernel(parts, *refs):
    refs[-1][...] = tree_sum([ref[...] for ref in refs[:parts]])


def store_tiles(piece, right, stats):
    rows, columns = right.shape
    place = 0
    for column in range(0, columns, LANES):
        for row in range(0, rows, TILE_ROWS):
            piece[place] = right[row : row + TILE_ROWS, column : column + LANES].astype(BF16)
            place += 1
    piece[place] = jnp.concatenate([stats[:, :LANES], stats[:, LANES:]], axis=0).astype(BF16)


def load_right(piece, rows):
    per_column = rows // TILE_ROWS
    tiles = [piece[at].astype(F32) for at in range(piece.shape[0] - 1)]
    return jnp.concatenate(
        [
            jnp.concatenate(tiles[at : at + per_column], axis=0)
            for at in range(0, len(tiles), per_column)
        ],
        axis=1,
    )


def load_stats(piece):
    tile = piece[piece.shape[0] - 1].astype(F32)
    return jnp.concatenate([tile[: TILE_ROWS // 2], tile[TILE_ROWS // 2 :]], axis=1)


def orthonormal(problems):
    rank, rows = problems[0].shape
    tiles = rank // SUBLANES
    spread_shape = (SUBLANES, rows)
    place = lax.broadcasted_iota(jnp.int32, spread_shape, 0)

    def dots(rows_of, vector):
        return jnp.sum(rows_of * vector, axis=1, keepdims=True)

    def spread(tiled, row):
        tile, at = divmod(row, SUBLANES)
        return jnp.broadcast_to(tiled[tile][at : at + 1], spread_shape)

    states = []
    for first in problems:
        original = [first[at * SUBLANES : (at + 1) * SUBLANES] for at in range(tiles)]
        states.append((original, list(original), [jnp.zeros(spread_shape, F32)] * tiles))
    def project(finished, found):
        weighted = tree_add([found[q] * finished[q] for q in found])
        return jnp.sum(weighted, axis=0, keepdims=True)

    currents = [spread(original, 0) for original, _, _ in states]
    known = [None for _ in states]
    for column in range(rank):
        tile, at = divmod(column, SUBLANES)
        before = range((column - 1) // SUBLANES + 1)
        for which, (original, residual, finished) in enumerate(states):
            current = currents[which]
            square = dots(current, current)
            inverse = lax.rsqrt(square + BASIS_EPS)
            unit = current * inverse
            if column + 1 < rank:
                ahead = spread(residual, column + 1)
                step = dots(spread(original, column + 1), current) * inverse
                own = dots(ahead, current) * inverse
                following = ahead - unit * (step + own - step * (square * inverse * inverse))
                if column:
                    cross = project(finished, {q: dots(finished[q], current) for q in before})
                    following = following - known[which] + (step * inverse) * cross
            finished[tile] = jnp.where(place == at, unit, finished[tile])
            if column + 1 < rank:
                for q in range((column + 1) // SUBLANES, tiles):
                    residual[q] = residual[q] - (dots(original[q], current) * inverse) * unit
                currents[which] = following
            if column + 2 < rank:
                far = spread(residual, column + 2)
                known[which] = project(
                    finished, {q: dots(finished[q], far) for q in range(tile + 1)}
                )
    return [jnp.concatenate(finished, axis=0) for _, _, finished in states]


def ortho_kernel(share, parts, stat_parts, *refs):
    lefts, stats = refs[:parts], refs[parts : parts + stat_parts]
    merged, ortho, *pieces, sums = refs[parts + stat_parts :]
    digit = lax.axis_index("dp") % 4
    rank = ortho.shape[0] // 2
    quarter = merged.shape[1] // len(pieces)
    sums[...] = tree_sum([stat[...] for stat in stats])
    total = tree_sum([left[...] for left in lefts]) * share
    finished = orthonormal([total[:rank], total[rank:]])
    ortho[:rank, :], ortho[rank:, :] = finished
    for step, piece in enumerate(pieces):
        block = jnp.bitwise_xor(digit, step)
        columns = pl.ds(pl.multiple_of(block * quarter, quarter), quarter)
        pair = stacked(jnp.where(block < len(pieces) - 1, finished[0], finished[1]))
        stat_columns = pl.ds(pl.multiple_of(block * 2 * LANES, 2 * LANES), 2 * LANES)
        right = folded(nn(pair, merged[:, columns].astype(BF16)))
        store_tiles(piece, right, sums[:, stat_columns])


def reduce_kernel(*refs):
    pieces, total = refs[:-2], refs[-1]
    total[...] = tree_sum([piece[...].astype(F32) for piece in pieces]).astype(BF16)


def update_blocks(share, steps, pieces, ortho, merged, results, updates, errors, sems, small):
    in_update, out_update, in_new_error, out_new_error = results
    rank = ortho.shape[0] // 2
    quarter = updates.shape[2]
    count = merged.shape[1] // quarter
    places = []
    for at, step in enumerate(steps):
        block = jnp.bitwise_xor(lax.axis_index("dp") % 4, step)
        columns = pl.ds(pl.multiple_of(block * quarter, quarter), quarter)
        right = load_right(pieces[step], rank) * share
        own_coarse, own_fine = halves(
            jnp.where(block < count - 1, ortho[:rank, :], ortho[rank:, :])
        )
        coarse, fine = halves(right)
        update = tn(
            jnp.concatenate([own_coarse, own_coarse, own_fine], axis=0),
            jnp.concatenate([coarse, fine, coarse], axis=0),
        )
        updates[at] = update
        errors[at] = merged[:, columns] - update
        places.append((block, columns))

        @pl.when(block < count - 1)
        def _():
            targets = in_update.at[:, columns], in_new_error.at[:, columns]
            fetch(list(zip((updates.at[at], errors.at[at]), targets)), sems.at[at])

        @pl.when(block == count - 1)
        def _():
            targets = out_update, out_new_error
            fetch(list(zip((updates.at[at], errors.at[at]), targets)), sems.at[at])

    small()
    for at, (block, columns) in enumerate(places):
        pltpu.make_async_copy(updates.at[at], out_update, sems.at[at, 0]).wait()
        pltpu.make_async_copy(errors.at[at], out_new_error, sems.at[at, 1]).wait()


def first_kernel(share, steps, *refs):
    count = len(steps)
    pieces = dict(zip(steps, refs[:count]))
    ortho, merged = refs[count : count + 2]
    results, (updates, errors, sems) = refs[count + 2 : count + 6], refs[count + 6 :]
    update_blocks(share, steps, pieces, ortho, merged, results, updates, errors, sems, lambda: None)


def last_kernel(share, stat_share, steps, parts, *refs):
    pieces, (ortho, merged) = refs[:parts], refs[parts : parts + 2]
    results, small_results = refs[parts + 6 : parts + 10], refs[parts + 10 : parts + 14]
    rights, stats_of, *small = refs[parts + 14 : parts + 20]
    small_sems, updates, errors, sems = refs[parts + 20 :]
    in_basis, out_basis, table, gain = small
    quarter = rights.shape[2]
    copies = []

    def small_outputs():
        for step, piece in enumerate(pieces):
            rights[step] = load_right(piece, rights.shape[1]) * share
            stats_of[step] = load_stats(piece) * stat_share
        tiles = []
        for block in range(parts):
            place = jnp.bitwise_xor(lax.axis_index("dp") % 4, block)
            right = rights[place]
            tiles.append(stats_of[place])
            if block < parts - 1:
                in_basis[:, block * quarter : (block + 1) * quarter] = right
            else:
                out_basis[...] = right
        stats = jnp.concatenate(tiles, axis=1)
        table[...] = stats[:, : table.shape[1]]
        padded = stats.shape[1] - 2 * LANES
        for at in range(gain.shape[1] // LANES):
            gain[:, at * LANES : (at + 1) * LANES] = stats[at : at + 1, padded : padded + LANES]
        copies.extend(fetch(list(zip(small, small_results)), small_sems))

    update_blocks(
        share, steps, pieces, ortho, merged, results, updates, errors, sems, small_outputs
    )
    for copy in copies:
        copy.wait()


def call(kernel, outs, scratch=(), flops=0, moved=0, vmem=16, **options):
    return pl.pallas_call(
        kernel,
        out_shape=outs,
        scratch_shapes=list(scratch),
        cost_estimate=pl.CostEstimate(flops=flops, bytes_accessed=moved, transcendentals=0),
        compiler_params=pltpu.CompilerParams(vmem_limit_bytes=vmem << 20),
        **options,
    )


def buffers(*arrays):
    return [pltpu.VMEM(array.shape, array.dtype) for array in arrays] + [
        pltpu.SemaphoreType.DMA((len(arrays),))
    ]


def in_hbm(*arrays):
    return [pltpu.with_memory_space_constraint(array, pltpu.HBM) for array in arrays]


def shape(dims, dtype):
    return jax.ShapeDtypeStruct(dims, dtype)


def exchange(value, axis, count, distance):
    return lax.ppermute(value, axis, [(at, at ^ distance) for at in range(count)])


def digits(count):
    groups, stride = [], 1
    while stride < count:
        size = 4 if count // stride % 4 == 0 else 2
        groups.append((stride, size))
        stride *= size
    return groups


def partners(value, axis, count, stride, size):
    return [value] + [exchange(value, axis, count, step * stride) for step in range(1, size)]


def sum_over(value, axis, count):
    for stride, size in digits(count):
        value = tree_sum(partners(value, axis, count, stride, size))
    return value


def shards(
    tokens,
    cotangent,
    region_ids,
    rel_bucket,
    norm_gain,
    in_weight,
    out_weight,
    bias_table,
    in_error,
    out_error,
    in_basis,
    out_basis,
):
    n_dp = lax.axis_size("dp")
    n_mp = lax.axis_size("mp")
    window_count, span, features = tokens.shape
    head_count, buckets = bias_table.shape
    rank = in_basis.shape[2]
    row_count = window_count * span
    row_block = in_weight.shape[0]
    wide = in_weight.shape[1]
    both = wide + features
    padded = -(-buckets // LANES) * LANES
    blocks = 2 if n_mp == 2 else 1
    token_rows = tokens.reshape(row_count, features)
    cot_rows = cotangent.reshape(row_count, features)
    gain = norm_gain.reshape(1, features)

    in_basis_t = jnp.swapaxes(in_basis[0], 0, 1)
    out_basis_t = jnp.swapaxes(out_basis[0], 0, 1)
    if blocks == 2:
        own = (in_weight, out_weight, in_basis_t, out_basis_t)
        arrived = [exchange(array, "mp", n_mp, 1) for array in own]
    else:
        own = (
            lax.all_gather(in_weight, "mp", axis=0, tiled=True),
            lax.all_gather(out_weight, "mp", axis=0, tiled=True),
            in_basis_t,
            out_basis_t,
        )
        arrived = []
    width = features // blocks

    operands = (
        rel_bucket,
        bias_table,
        token_rows,
        gain,
        own[0],
        cot_rows,
        region_ids,
        *own[1:],
        in_error[0],
        out_error[0],
    )
    normed, normed_t, part, bias, index_t, table_pad, bucket, *kept = call(
        functools.partial(prepare_kernel, blocks, READY_HEADS),
        (
            shape((row_count, features), BF16),
            shape((features, row_count), BF16),
            shape((row_count, wide), F32),
            shape((READY_HEADS, span, span), F32),
            shape((span, span), jnp.int32),
            shape((head_count, padded), F32),
            shape((span, span), jnp.int32),
        )
        + tuple(shape(array.shape, array.dtype) for array in operands[2:]),
        [pltpu.VMEM(bias_table.shape, F32), pltpu.SemaphoreType.DMA((12,))],
        flops=2 * row_count * width * wide,
        moved=4 << 20,
        in_specs=[HBM] * 12,
        out_specs=[VMEM] * 17,
    )(*in_hbm(*operands))
    token_rows, gain, w_in_own, cot_rows, region, *own, in_errors, out_errors = kept
    in_basis_t, out_basis_t = own[1:]

    left_shape = shape((2 * rank, width), F32)
    outputs = call(
        functools.partial(attend_kernel, blocks, 1.0 / n_mp),
        (shape((width, both), BF16),) * blocks
        + (left_shape,) * blocks
        + (shape((head_count, span, span), F32), shape((row_count, wide), BF16)),
        [
            pltpu.VMEM((row_count, wide), BF16),
            pltpu.VMEM((row_count, features), BF16),
            pltpu.VMEM((row_count, features), BF16),
            pltpu.VMEM((head_count, span, span), F32),
        ],
        flops=4 * row_count * features * both,
        moved=8 << 20,
        in_specs=[VMEM] * (13 + len(arrived)),
        out_specs=[VMEM] * (2 * blocks + 2),
    )(normed, normed_t, part, bias, index_t, table_pad, bucket, cot_rows, region, w_in_own, *own, *arrived)
    *outputs, score_sum, packed = outputs
    terms, lefts = outputs[:blocks], outputs[blocks:]
    scores_of = [score_sum]

    if blocks == 2:
        left_other = exchange(lefts[1], "mp", n_mp, 1)
        left = lefts[0]
    else:
        term_parts = [lax.psum_scatter(terms[0], "mp", scatter_dimension=0, tiled=True)]
        left = call(
            functools.partial(shard_kernel, 1.0 / n_mp),
            shape((2 * rank, row_block), F32),
            in_specs=[VMEM] * 3,
            out_specs=VMEM,
        )(term_parts[0], in_basis_t, out_basis_t)

    left = call(
        error_kernel,
        shape((2 * rank, row_block), F32),
        flops=8 * row_block * both * rank,
        moved=3 << 20,
        in_specs=[VMEM] * 5,
        out_specs=VMEM,
    )(left, in_errors, out_errors, in_basis_t, out_basis_t)
    if blocks == 2:
        left, term_sent, score_sent = call(
            join_kernel,
            tuple(shape(array.shape, array.dtype) for array in (left, terms[1], score_sum)),
            in_specs=[VMEM] * 2 + [ANY] * 2,
            out_specs=[VMEM] + [ANY] * 2,
            input_output_aliases={2: 1, 3: 2},
        )(left, left_other, terms[1], score_sum)
        scores_of = [score_sent, exchange(score_sent, "mp", n_mp, 1)]
        terms = [terms[0], term_sent]
        term_parts = [terms[0], exchange(term_sent, "mp", n_mp, 1)]

    stats = call(
        functools.partial(table_kernel, blocks),
        shape((head_count, padded + 2 * LANES), F32),
        [pltpu.VMEM((1, features), F32)],
        flops=2 * row_count * features * wide,
        moved=4 << 20,
        in_specs=[VMEM] * (3 * blocks + 2),
        out_specs=VMEM,
    )(*scores_of, *terms, w_in_own, *arrived[:1], gain, index_t)
    if blocks == 2:
        stats = [stats, exchange(stats, "mp", n_mp, 1)]
    else:
        stats = [sum_over(stats, "mp", n_mp)]

    groups = digits(n_dp)
    for group in groups[:0:-1]:
        left = call(
            functools.partial(add_kernel, group[1]),
            shape(left.shape, F32),
            in_specs=[VMEM] * (group[1] + 1),
            out_specs=VMEM,
        )(*partners(left, "dp", n_dp, *group), stats[-1])
    stride, parts = groups[0]
    lefts = partners(left, "dp", n_dp, stride, parts)
    merged = call(
        functools.partial(merge_kernel, 1.0 / n_mp, len(term_parts)),
        shape((row_block, both), F32),
        flops=4 * row_block * both,
        moved=6 << 20,
        in_specs=[VMEM] * (len(term_parts) + 2),
        out_specs=VMEM,
    )(*term_parts, in_errors, out_errors)

    quarter = both // parts
    tiles = quarter // LANES * (rank // TILE_ROWS) + 1
    piece = shape((tiles, TILE_ROWS, LANES), BF16)
    ortho, *pieces = call(
        functools.partial(ortho_kernel, 1.0 / n_dp, len(lefts), len(stats)),
        (shape((2 * rank, row_block), F32),) + (piece,) * parts,
        [pltpu.VMEM((head_count, padded + 2 * LANES), F32)],
        flops=12 * row_block * both * rank,
        moved=3 << 20,
        in_specs=[VMEM] * (len(lefts) + len(stats) + 1),
        out_specs=[VMEM] * (1 + parts),
    )(*lefts, *stats, merged)

    token_grad, flag = call(
        functools.partial(token_kernel, blocks),
        (shape((row_count, features), BF16), shape((SUBLANES, LANES), F32)),
        [
            pltpu.VMEM((row_count, features), F32),
            pltpu.VMEM((row_count, features), BF16),
            pltpu.SemaphoreType.DMA((1,)),
        ],
        flops=2 * row_count * features * wide,
        moved=4 << 20,
        in_specs=[VMEM] * (blocks + 5),
        out_specs=[HBM, VMEM],
    )(packed, w_in_own, *arrived[:1], token_rows, cot_rows, gain, ortho)

    def reduced(values):
        return call(
            reduce_kernel,
            piece,
            in_specs=[VMEM] * (len(values) + 1),
            out_specs=VMEM,
            moved=1 << 18,
        )(*values, flag)

    held = reduced(
        [pieces[0]]
        + [exchange(pieces[step], "dp", n_dp, step * stride) for step in range(1, parts)]
    )
    for group in groups[1:]:
        held = reduced(partners(held, "dp", n_dp, *group))
    pieces = partners(held, "dp", n_dp, stride, parts)

    big = (
        shape((row_block, wide), F32),
        shape((row_block, features), F32),
        shape((row_block, wide), F32),
        shape((row_block, features), F32),
    )
    small = (
        shape((rank, wide), F32),
        shape((rank, features), F32),
        shape((head_count, buckets), F32),
        shape((1, features), F32),
    )
    early, late = (0, parts - 1), tuple(range(parts - 2, 0, -1))

    def staging(steps):
        return [pltpu.VMEM((len(steps), row_block, quarter), F32)] * 2 + [
            pltpu.SemaphoreType.DMA((len(steps), 2))
        ]

    results = call(
        functools.partial(first_kernel, 1.0 / n_dp, early),
        big,
        staging(early),
        flops=24 * row_block * quarter * rank,
        moved=1 << 20,
        in_specs=[VMEM] * (len(early) + 2),
        out_specs=[HBM] * 4,
    )(*(pieces[step] for step in early), ortho, merged)
    in_update, out_update, in_new_error, out_new_error, in_right, out_right, table, gain = call(
        functools.partial(last_kernel, 1.0 / n_dp, 1.0 / (n_dp * n_mp), late, parts),
        big + small,
        [
            pltpu.VMEM((parts, rank, quarter), F32),
            pltpu.VMEM((parts, head_count, 2 * LANES), F32),
        ]
        + buffers(*small)
        + staging(late),
        flops=24 * row_block * quarter * rank,
        moved=1 << 20,
        in_specs=[VMEM] * (parts + 2) + [HBM] * 4,
        out_specs=[HBM] * 8,
        input_output_aliases={2 + parts + at: at for at in range(4)},
    )(*pieces, ortho, merged, *in_hbm(*results))

    return (
        token_grad.reshape(tokens.shape),
        gain.reshape(features),
        table,
        in_update,
        out_update,
        in_new_error[None],
        out_new_error[None],
        jnp.swapaxes(in_right, 0, 1)[None],
        jnp.swapaxes(out_right, 0, 1)[None],
    )


def solution(mesh):
    placed = (
        P(("dp", "mp"), None, None),
        P(("dp", "mp"), None, None),
        P(("dp", "mp"), None),
        P(),
        P(),
        P("mp", None),
        P("mp", None),
        P(),
        P("dp", "mp", None),
        P("dp", "mp", None),
        P("mp", None, None),
        P("mp", None, None),
    )
    return jax.shard_map(
        shards,
        mesh=mesh,
        in_specs=placed,
        out_specs=(
            P(("dp", "mp"), None, None),
            P(),
            P(),
            P("mp", None),
            P("mp", None),
            P("dp", "mp", None),
            P("dp", "mp", None),
            P("mp", None, None),
            P("mp", None, None),
        ),
        check_vma=False,
    )
```

```python
import functools

import jax
import jax.numpy as jnp
from jax import lax
from jax.experimental import pallas as pl
from jax.experimental.pallas import tpu as pltpu
from jax.sharding import PartitionSpec as P

NORM_EPS = 1e-05
BASIS_EPS = 1e-06
MASKED = -1e30
LANES = 128
SUBLANES = 8
TILE_ROWS = 16
READY_HEADS = 2
F32 = jnp.float32
BF16 = jnp.bfloat16

VMEM = pl.BlockSpec(memory_space=pltpu.VMEM)
HBM = pl.BlockSpec(memory_space=pltpu.HBM)
ANY = pl.BlockSpec(memory_space=pl.ANY)


def nn(a, b):
    return lax.dot_general(
        a, b, (((1,), (0,)), ((), ())), preferred_element_type=F32
    )


def nt(a, b):
    return lax.dot_general(
        a, b, (((1,), (1,)), ((), ())), preferred_element_type=F32
    )


def tn(a, b):
    return lax.dot_general(
        a, b, (((0,), (0,)), ((), ())), preferred_element_type=F32
    )


def block_columns(me, step, blocks, width):
    if blocks == 1:
        return pl.ds(0, width)
    index = me if step == 0 else 1 - me
    return pl.ds(pl.multiple_of(index * width, width), width)


def norm_forward(token_rows):
    tokens_wide = token_rows.astype(F32)
    mean_x = jnp.mean(tokens_wide, axis=-1, keepdims=True)
    centered = tokens_wide - mean_x
    variance = jnp.mean(centered * centered, axis=-1, keepdims=True)
    inv_sigma = lax.rsqrt(variance + NORM_EPS)
    return (centered * inv_sigma, inv_sigma)


def fetch(pairs, sems):
    copies = [
        pltpu.make_async_copy(source, target, sems.at[at])
        for at, (source, target) in enumerate(pairs)
    ]
    for copy in copies:
        copy.start()
    return copies


def halves(value):
    coarse = value.astype(BF16)
    return coarse, (value - coarse.astype(F32)).astype(BF16)


def stacked(value):
    return jnp.concatenate(halves(value), axis=0)


def folded(value):
    half = value.shape[0] // 2
    return value[:half] + value[half:]


def gather_bias(bias, heads, table_pad, index_t, index):
    span = index.shape[0]
    padded = table_pad.shape[1]
    even = span // LANES * LANES
    lookups = [(index_t[:, :even], False)] if even else []
    if even < span:
        lookups.append((index[even:, :], True))
    for places, flipped in lookups:
        rows, columns = places.shape
        for start in range(0, columns, LANES):
            stop = min(columns, start + LANES)
            part = places[:, start:stop]
            if stop - start < LANES:
                filler = jnp.zeros((rows, LANES - (stop - start)), jnp.int32)
                part = jnp.concatenate([part, filler], axis=1)
            high, low = part // LANES, part % LANES
            for head in heads:
                found = jnp.zeros((rows, LANES), F32)
                for level in range(padded // LANES):
                    row = table_pad[head : head + 1, level * LANES : (level + 1) * LANES]
                    row = jnp.broadcast_to(row, (rows, LANES))
                    picked = jnp.take_along_axis(row, low, axis=1, mode="promise_in_bounds")
                    found = jnp.where(high == level, picked, found)
                if flipped:
                    bias[head, start:stop, even:] = found[:, : stop - start].T
                else:
                    bias[head, :, start:stop] = found[:, : stop - start]


def prepare_kernel(blocks, ready, *refs):
    sources, rest = refs[:10], refs[10:]
    normed, normed_t, part, bias, index_t, table_pad, bucket, *kept = rest[:15]
    table, sems = rest[15:]
    copies = fetch(list(zip(sources, [bucket, table] + kept)), sems)
    tokens, gain, w_own = kept[:3]
    me = lax.axis_index("mp")
    width = w_own.shape[0]
    span = bucket.shape[0]
    head_count, padded = table_pad.shape
    for copy in copies[:2]:
        copy.wait()
    table_pad[...] = jnp.zeros_like(table_pad)
    table_pad[:, : table.shape[1]] = table[...]
    index_t[...] = bucket[...].T
    gather_bias(bias, range(ready), table_pad, index_t, bucket)
    for copy in copies[2:4]:
        copy.wait()
    x_hat, _ = norm_forward(tokens[...])
    normed[...] = (x_hat * gain[...]).astype(BF16)
    normed_t[...] = normed[...].T
    copies[4].wait()
    part[...] = nn(normed[:, block_columns(me, 0, blocks, width)], w_own[...])
    for copy in copies[5:]:
        copy.wait()


def attend_kernel(blocks, share, *refs):
    normed, normed_t, part, bias_ready, index_t, table_pad, bucket, cot, region = refs[:9]
    own, arrived = refs[9:13], refs[13 : 9 + 4 * blocks]
    sources, rest = refs[9 + 4 * blocks : 11 + 4 * blocks], refs[11 + 4 * blocks :]
    terms, lefts, rest = rest[:blocks], rest[blocks : 2 * blocks], rest[2 * blocks :]
    score_sum, packed, in_error, out_error, proj, mixed_grad, mixed, bias, sems = rest
    copies = fetch(list(zip(sources, (in_error, out_error))), sems)
    w_in, w_out, in_basis, out_basis = (
        [own[at]] + list(arrived[at : at + blocks - 1]) for at in range(4)
    )
    me = lax.axis_index("mp")
    window_count, span = region.shape
    features = normed.shape[1]
    ready, head_count = bias_ready.shape[0], bias.shape[0]
    head_size = features // head_count
    scale = head_size ** (-0.5)
    width = features // blocks
    if blocks == 1:
        proj[...] = part[...].astype(BF16)
    else:
        other = nn(normed[:, block_columns(me, 1, blocks, width)], w_in[1][...])
        proj[...] = (part[...] + other).astype(BF16)
    for step in range(blocks):
        mixed_grad[:, block_columns(me, step, blocks, width)] = nt(
            cot[...], w_out[step][...]
        ).astype(BF16)
    lane = lax.broadcasted_iota(jnp.int32, (span, LANES), 1)
    per_group = LANES // head_size
    for window in range(window_count):
        rows = pl.ds(window * span, span)
        ids_row = jnp.broadcast_to(region[window : window + 1, :], (span, span))
        allowed = ids_row == ids_row.T
        for group in range(features // LANES):
            start = group * LANES
            heads = slice(group * per_group, (group + 1) * per_group)
            if heads.stop <= ready:
                pair_bias = bias_ready[heads]
            else:
                if window == 0:
                    gather_bias(bias, range(heads.start, heads.stop), table_pad, index_t, bucket)
                pair_bias = bias[heads]
            q = proj[rows, start : start + LANES] * jnp.asarray(scale, BF16)
            k = proj[rows, features + start : features + start + LANES]
            v = proj[rows, 2 * features + start : 2 * features + start + LANES]
            g = mixed_grad[rows, start : start + LANES]
            pick = [lane // head_size == sub for sub in range(per_group)]
            k_split = jnp.concatenate([jnp.where(own, k, jnp.zeros_like(k)) for own in pick], 0)
            v_split = jnp.concatenate([jnp.where(own, v, jnp.zeros_like(v)) for own in pick], 0)
            scores = nt(k_split, q).reshape(per_group, span, span) + pair_bias
            scores = jnp.where(allowed[None], scores, MASKED)
            top = jnp.max(scores, axis=1, keepdims=True)
            raised = jnp.exp(scores - top)
            prob = raised * (1.0 / jnp.sum(raised, axis=1, keepdims=True))
            prob_b = prob.astype(BF16)
            prob_grad = nt(v_split, g).reshape(per_group, span, span)
            inner = jnp.sum(prob * prob_grad, axis=1, keepdims=True)
            score_grad = prob * (prob_grad - inner)
            score_b = score_grad.astype(BF16)
            if window == 0:
                score_sum[heads] = score_grad
            else:
                score_sum[heads] += score_grad
            k_grads = nn(score_b.reshape(per_group * span, span), q)
            v_grads = nn(prob_b.reshape(per_group * span, span), g)

            def joined(parts):
                total = parts[0]
                for sub in range(1, per_group):
                    total = jnp.where(pick[sub], parts[sub], total)
                return total

            k_grad = joined([k_grads[at * span : (at + 1) * span] for at in range(per_group)])
            v_grad = joined([v_grads[at * span : (at + 1) * span] for at in range(per_group)])
            out = joined([tn(prob_b[at], v) for at in range(per_group)])
            q_grad = joined([tn(score_b[at], k) for at in range(per_group)])
            mixed[rows, start : start + LANES] = out.astype(BF16)
            packed[rows, start : start + LANES] = (q_grad * scale).astype(BF16)
            packed[rows, features + start : features + start + LANES] = k_grad.astype(BF16)
            packed[rows, 2 * features + start : 2 * features + start + LANES] = v_grad.astype(BF16)
    wide = 3 * features
    for step in range(blocks):
        columns = block_columns(me, step, blocks, width)
        terms[step][:, :wide] = nn(normed_t[columns, :], packed[...]).astype(BF16)
        terms[step][:, wide:] = tn(mixed[:, columns], cot[...]).astype(BF16)
        rank = in_basis[step].shape[0]
        for basis, at, place in (
            (in_basis[step], slice(None, wide), 0),
            (out_basis[step], slice(wide, None), rank),
        ):
            left = folded(nt(stacked(basis[...]), terms[step][:, at])) * share
            lefts[step][place : place + rank, :] = left
    for copy in copies:
        copy.wait()


def token_kernel(blocks, packed, *refs):
    w_in, (tokens, cot, gain, _, result, flag, normed_grad, token_grad, sems) = (
        refs[:blocks],
        refs[blocks:],
    )
    me = lax.axis_index("mp")
    width = tokens.shape[1] // blocks
    for step in range(blocks):
        normed_grad[:, block_columns(me, step, blocks, width)] = nt(packed[...], w_in[step][...])
    x_hat, inv_sigma = norm_forward(tokens[...])
    hat_grad = normed_grad[...] * gain[...]
    token_delta = inv_sigma * (
        hat_grad
        - jnp.mean(hat_grad, axis=-1, keepdims=True)
        - x_hat * jnp.mean(hat_grad * x_hat, axis=-1, keepdims=True)
    )
    token_grad[...] = (cot[...].astype(F32) + token_delta).astype(BF16)
    flag[...] = jnp.zeros_like(flag)
    for copy in fetch([(token_grad, result)], sems):
        copy.wait()


def table_kernel(blocks, *refs):
    scores_of, terms = refs[:blocks], refs[blocks : 2 * blocks]
    w_in, rest = refs[2 * blocks : 3 * blocks], refs[3 * blocks :]
    gain, index_t, stats, gain_row = rest
    me = lax.axis_index("mp")
    features = gain.shape[1]
    for step in range(blocks):
        columns = block_columns(me, step, blocks, features // blocks)
        folds = tree_add(
            [
                terms[step][:, at : at + LANES].astype(F32)
                * w_in[step][:, at : at + LANES].astype(F32)
                for at in range(0, w_in[step].shape[1], LANES)
            ]
        )
        gain_row[:, columns] = jnp.sum(folds.T, axis=0, keepdims=True) / gain[:, columns]
    head_count, span, _ = scores_of[0].shape
    rows = span // blocks
    mine = block_columns(me, 0, blocks, rows)
    padded = stats.shape[1] - 2 * LANES
    levels = padded // LANES
    indices = index_t[mine, :]
    scores = tree_add([part[:, mine, :] for part in scores_of])
    sublane = lax.broadcasted_iota(jnp.int32, (LANES, span), 0)
    total = jnp.zeros((2 * levels * head_count, LANES), F32)
    for row in range(rows):
        index = indices[row : row + 1, :]
        high = jnp.broadcast_to(index // LANES, (head_count, span))
        low = jnp.broadcast_to(index % LANES, (LANES, span))
        one_hot = jnp.where(low == sublane, 1.0, 0.0).astype(BF16)
        values = scores[:, row, :]
        coarse = values.astype(BF16).astype(F32)
        fine = values - coarse
        picked = [
            jnp.where(high == level, piece, 0.0)
            for piece in (coarse, fine)
            for level in range(levels)
        ]
        total += nt(jnp.concatenate(picked, axis=0).astype(BF16), one_hot)
    total = folded(total)
    for level in range(levels):
        stats[:, level * LANES : (level + 1) * LANES] = total[
            level * head_count : (level + 1) * head_count
        ]
    stats[:, padded:] = jnp.zeros((head_count, 2 * LANES), F32)
    for piece in range(features // LANES):
        stats[piece : piece + 1, padded : padded + LANES] = gain_row[
            :, piece * LANES : (piece + 1) * LANES
        ]


def shard_kernel(share, shard, in_basis, out_basis, left):
    rank, split = in_basis.shape
    left[:rank, :] = folded(nt(stacked(in_basis[...]), shard[:, :split])) * share
    left[rank:, :] = folded(nt(stacked(out_basis[...]), shard[:, split:])) * share


def error_kernel(term_left, in_error, out_error, in_basis, out_basis, left):
    rank = in_basis.shape[0]
    for error, basis, at in ((in_error, in_basis, 0), (out_error, out_basis, rank)):
        coarse, fine = halves(error[...])
        pair = stacked(basis[...])
        left[at : at + rank, :] = term_left[at : at + rank, :] + folded(
            nt(pair, coarse) + nt(pair, fine)
        )


def merge_kernel(share, parts, *refs):
    shards, (in_error, out_error, merged) = refs[:parts], refs[parts:]
    split = in_error.shape[1]
    for columns, error in ((slice(None, split), in_error), (slice(split, None), out_error)):
        total = tree_add([shard[:, columns].astype(F32) for shard in shards])
        merged[:, columns] = total * share + error[...]


def tree_sum(values):
    while len(values) > 1:
        values = [values[at] + values[at + 1] for at in range(0, len(values), 2)]
    return values[0]


def tree_add(values):
    while len(values) > 1:
        odd = values[len(values) // 2 * 2 :]
        values = [values[at] + values[at + 1] for at in range(0, len(values) - 1, 2)] + odd
    return values[0]


def join_kernel(left_own, left_other, *refs):
    left = refs[len(refs) // 2]
    left[...] = left_own[...] + left_other[...]


def add_kernel(parts, *refs):
    refs[-1][...] = tree_sum([ref[...] for ref in refs[:parts]])


def store_tiles(piece, right, stats):
    rows, columns = right.shape
    place = 0
    for column in range(0, columns, LANES):
        for row in range(0, rows, TILE_ROWS):
            piece[place] = right[row : row + TILE_ROWS, column : column + LANES].astype(BF16)
            place += 1
    piece[place] = jnp.concatenate([stats[:, :LANES], stats[:, LANES:]], axis=0).astype(BF16)


def load_right(piece, rows):
    per_column = rows // TILE_ROWS
    tiles = [piece[at].astype(F32) for at in range(piece.shape[0] - 1)]
    return jnp.concatenate(
        [
            jnp.concatenate(tiles[at : at + per_column], axis=0)
            for at in range(0, len(tiles), per_column)
        ],
        axis=1,
    )


def load_stats(piece):
    tile = piece[piece.shape[0] - 1].astype(F32)
    return jnp.concatenate([tile[: TILE_ROWS // 2], tile[TILE_ROWS // 2 :]], axis=1)


def orthonormal(problems):
    rank, rows = problems[0].shape
    tiles = rank // SUBLANES
    spread_shape = (SUBLANES, rows)
    place = lax.broadcasted_iota(jnp.int32, spread_shape, 0)

    def dots(rows_of, vector):
        return jnp.sum(rows_of * vector, axis=1, keepdims=True)

    def spread(tiled, row):
        tile, at = divmod(row, SUBLANES)
        return jnp.broadcast_to(tiled[tile][at : at + 1], spread_shape)

    states = []
    for first in problems:
        original = [first[at * SUBLANES : (at + 1) * SUBLANES] for at in range(tiles)]
        states.append((original, list(original), [jnp.zeros(spread_shape, F32)] * tiles))
    def project(finished, found):
        weighted = tree_add([found[q] * finished[q] for q in found])
        return jnp.sum(weighted, axis=0, keepdims=True)

    currents = [spread(original, 0) for original, _, _ in states]
    known = [None for _ in states]
    for column in range(rank):
        tile, at = divmod(column, SUBLANES)
        before = range((column - 1) // SUBLANES + 1)
        for which, (original, residual, finished) in enumerate(states):
            current = currents[which]
            square = dots(current, current)
            inverse = lax.rsqrt(square + BASIS_EPS)
            unit = current * inverse
            if column + 1 < rank:
                ahead = spread(residual, column + 1)
                step = dots(spread(original, column + 1), current) * inverse
                own = dots(ahead, current) * inverse
                following = ahead - unit * (step + own - step * (square * inverse * inverse))
                if column:
                    cross = project(finished, {q: dots(finished[q], current) for q in before})
                    following = following - known[which] + (step * inverse) * cross
            finished[tile] = jnp.where(place == at, unit, finished[tile])
            if column + 1 < rank:
                for q in range((column + 1) // SUBLANES, tiles):
                    residual[q] = residual[q] - (dots(original[q], current) * inverse) * unit
                currents[which] = following
            if column + 2 < rank:
                far = spread(residual, column + 2)
                known[which] = project(
                    finished, {q: dots(finished[q], far) for q in range(tile + 1)}
                )
    return [jnp.concatenate(finished, axis=0) for _, _, finished in states]


def ortho_kernel(share, parts, stat_parts, *refs):
    lefts, stats = refs[:parts], refs[parts : parts + stat_parts]
    merged, ortho, *pieces, sums = refs[parts + stat_parts :]
    digit = lax.axis_index("dp") % 4
    rank = ortho.shape[0] // 2
    quarter = merged.shape[1] // len(pieces)
    sums[...] = tree_sum([stat[...] for stat in stats])
    total = tree_sum([left[...] for left in lefts]) * share
    finished = orthonormal([total[:rank], total[rank:]])
    ortho[:rank, :], ortho[rank:, :] = finished
    for step, piece in enumerate(pieces):
        block = jnp.bitwise_xor(digit, step)
        columns = pl.ds(pl.multiple_of(block * quarter, quarter), quarter)
        pair = stacked(jnp.where(block < len(pieces) - 1, finished[0], finished[1]))
        stat_columns = pl.ds(pl.multiple_of(block * 2 * LANES, 2 * LANES), 2 * LANES)
        right = folded(nn(pair, merged[:, columns].astype(BF16)))
        store_tiles(piece, right, sums[:, stat_columns])


def reduce_kernel(*refs):
    pieces, total = refs[:-2], refs[-1]
    total[...] = tree_sum([piece[...].astype(F32) for piece in pieces]).astype(BF16)


def update_blocks(share, steps, pieces, ortho, merged, results, updates, errors, sems, small):
    in_update, out_update, in_new_error, out_new_error = results
    rank = ortho.shape[0] // 2
    quarter = updates.shape[2]
    count = merged.shape[1] // quarter
    places = []
    for at, step in enumerate(steps):
        block = jnp.bitwise_xor(lax.axis_index("dp") % 4, step)
        columns = pl.ds(pl.multiple_of(block * quarter, quarter), quarter)
        right = load_right(pieces[step], rank) * share
        own_coarse, own_fine = halves(
            jnp.where(block < count - 1, ortho[:rank, :], ortho[rank:, :])
        )
        coarse, fine = halves(right)
        update = tn(
            jnp.concatenate([own_coarse, own_coarse, own_fine], axis=0),
            jnp.concatenate([coarse, fine, coarse], axis=0),
        )
        updates[at] = update
        errors[at] = merged[:, columns] - update
        places.append((block, columns))

        @pl.when(block < count - 1)
        def _():
            targets = in_update.at[:, columns], in_new_error.at[:, columns]
            fetch(list(zip((updates.at[at], errors.at[at]), targets)), sems.at[at])

        @pl.when(block == count - 1)
        def _():
            targets = out_update, out_new_error
            fetch(list(zip((updates.at[at], errors.at[at]), targets)), sems.at[at])

    small()
    for at, (block, columns) in enumerate(places):
        pltpu.make_async_copy(updates.at[at], out_update, sems.at[at, 0]).wait()
        pltpu.make_async_copy(errors.at[at], out_new_error, sems.at[at, 1]).wait()


def first_kernel(share, steps, *refs):
    count = len(steps)
    pieces = dict(zip(steps, refs[:count]))
    ortho, merged = refs[count : count + 2]
    results, (updates, errors, sems) = refs[count + 2 : count + 6], refs[count + 6 :]
    update_blocks(share, steps, pieces, ortho, merged, results, updates, errors, sems, lambda: None)


def last_kernel(share, stat_share, steps, parts, *refs):
    pieces, (ortho, merged) = refs[:parts], refs[parts : parts + 2]
    results, small_results = refs[parts + 6 : parts + 10], refs[parts + 10 : parts + 14]
    rights, stats_of, *small = refs[parts + 14 : parts + 20]
    small_sems, updates, errors, sems = refs[parts + 20 :]
    in_basis, out_basis, table, gain = small
    quarter = rights.shape[2]
    copies = []

    def small_outputs():
        for step, piece in enumerate(pieces):
            rights[step] = load_right(piece, rights.shape[1]) * share
            stats_of[step] = load_stats(piece) * stat_share
        tiles = []
        for block in range(parts):
            place = jnp.bitwise_xor(lax.axis_index("dp") % 4, block)
            right = rights[place]
            tiles.append(stats_of[place])
            if block < parts - 1:
                in_basis[:, block * quarter : (block + 1) * quarter] = right
            else:
                out_basis[...] = right
        stats = jnp.concatenate(tiles, axis=1)
        table[...] = stats[:, : table.shape[1]]
        padded = stats.shape[1] - 2 * LANES
        for at in range(gain.shape[1] // LANES):
            gain[:, at * LANES : (at + 1) * LANES] = stats[at : at + 1, padded : padded + LANES]
        copies.extend(fetch(list(zip(small, small_results)), small_sems))

    update_blocks(
        share, steps, pieces, ortho, merged, results, updates, errors, sems, small_outputs
    )
    for copy in copies:
        copy.wait()


def call(kernel, outs, scratch=(), flops=0, moved=0, vmem=16, **options):
    return pl.pallas_call(
        kernel,
        out_shape=outs,
        scratch_shapes=list(scratch),
        cost_estimate=pl.CostEstimate(flops=flops, bytes_accessed=moved, transcendentals=0),
        compiler_params=pltpu.CompilerParams(vmem_limit_bytes=vmem << 20),
        **options,
    )


def buffers(*arrays):
    return [pltpu.VMEM(array.shape, array.dtype) for array in arrays] + [
        pltpu.SemaphoreType.DMA((len(arrays),))
    ]


def in_hbm(*arrays):
    return [pltpu.with_memory_space_constraint(array, pltpu.HBM) for array in arrays]


def shape(dims, dtype):
    return jax.ShapeDtypeStruct(dims, dtype)


def exchange(value, axis, count, distance):
    return lax.ppermute(value, axis, [(at, at ^ distance) for at in range(count)])


def digits(count):
    groups, stride = [], 1
    while stride < count:
        size = 4 if count // stride % 4 == 0 else 2
        groups.append((stride, size))
        stride *= size
    return groups


def partners(value, axis, count, stride, size):
    return [value] + [exchange(value, axis, count, step * stride) for step in range(1, size)]


def sum_over(value, axis, count):
    for stride, size in digits(count):
        value = tree_sum(partners(value, axis, count, stride, size))
    return value


def shards(
    tokens,
    cotangent,
    region_ids,
    rel_bucket,
    norm_gain,
    in_weight,
    out_weight,
    bias_table,
    in_error,
    out_error,
    in_basis,
    out_basis,
):
    n_dp = lax.axis_size("dp")
    n_mp = lax.axis_size("mp")
    window_count, span, features = tokens.shape
    head_count, buckets = bias_table.shape
    rank = in_basis.shape[2]
    row_count = window_count * span
    row_block = in_weight.shape[0]
    wide = in_weight.shape[1]
    both = wide + features
    padded = -(-buckets // LANES) * LANES
    blocks = 2 if n_mp == 2 else 1
    token_rows = tokens.reshape(row_count, features)
    cot_rows = cotangent.reshape(row_count, features)
    gain = norm_gain.reshape(1, features)

    in_basis_t = jnp.swapaxes(in_basis[0], 0, 1)
    out_basis_t = jnp.swapaxes(out_basis[0], 0, 1)
    if blocks == 2:
        own = (in_weight, out_weight, in_basis_t, out_basis_t)
        arrived = [exchange(array, "mp", n_mp, 1) for array in own]
    else:
        own = (
            lax.all_gather(in_weight, "mp", axis=0, tiled=True),
            lax.all_gather(out_weight, "mp", axis=0, tiled=True),
            in_basis_t,
            out_basis_t,
        )
        arrived = []
    width = features // blocks

    operands = (
        rel_bucket,
        bias_table,
        token_rows,
        gain,
        own[0],
        cot_rows,
        region_ids,
        *own[1:],
    )
    normed, normed_t, part, bias, index_t, table_pad, bucket, *kept = call(
        functools.partial(prepare_kernel, blocks, READY_HEADS),
        (
            shape((row_count, features), BF16),
            shape((features, row_count), BF16),
            shape((row_count, wide), F32),
            shape((READY_HEADS, span, span), F32),
            shape((span, span), jnp.int32),
            shape((head_count, padded), F32),
            shape((span, span), jnp.int32),
        )
        + tuple(shape(array.shape, array.dtype) for array in operands[2:]),
        [pltpu.VMEM(bias_table.shape, F32), pltpu.SemaphoreType.DMA((10,))],
        flops=2 * row_count * width * wide,
        moved=4 << 20,
        in_specs=[HBM] * 10,
        out_specs=[VMEM] * 15,
    )(*in_hbm(*operands))
    token_rows, gain, w_in_own, cot_rows, region, *own = kept
    errors = (in_error[0], out_error[0])
    in_basis_t, out_basis_t = own[1:]

    left_shape = shape((2 * rank, width), F32)
    outputs = call(
        functools.partial(attend_kernel, blocks, 1.0 / n_mp),
        (shape((width, both), BF16),) * blocks
        + (left_shape,) * blocks
        + (shape((head_count, span, span), F32), shape((row_count, wide), BF16))
        + tuple(shape(array.shape, F32) for array in errors),
        [
            pltpu.VMEM((row_count, wide), BF16),
            pltpu.VMEM((row_count, features), BF16),
            pltpu.VMEM((row_count, features), BF16),
            pltpu.VMEM((head_count, span, span), F32),
            pltpu.SemaphoreType.DMA((2,)),
        ],
        flops=4 * row_count * features * both,
        moved=8 << 20,
        in_specs=[VMEM] * (13 + len(arrived)) + [HBM] * 2,
        out_specs=[VMEM] * (2 * blocks + 4),
    )(normed, normed_t, part, bias, index_t, table_pad, bucket, cot_rows, region, w_in_own, *own, *arrived, *in_hbm(*errors))
    *outputs, score_sum, packed, in_errors, out_errors = outputs
    terms, lefts = outputs[:blocks], outputs[blocks:]
    scores_of = [score_sum]

    if blocks == 2:
        left_other = exchange(lefts[1], "mp", n_mp, 1)
        left = lefts[0]
    else:
        term_parts = [lax.psum_scatter(terms[0], "mp", scatter_dimension=0, tiled=True)]
        left = call(
            functools.partial(shard_kernel, 1.0 / n_mp),
            shape((2 * rank, row_block), F32),
            in_specs=[VMEM] * 3,
            out_specs=VMEM,
        )(term_parts[0], in_basis_t, out_basis_t)

    left = call(
        error_kernel,
        shape((2 * rank, row_block), F32),
        flops=8 * row_block * both * rank,
        moved=3 << 20,
        in_specs=[VMEM] * 5,
        out_specs=VMEM,
    )(left, in_errors, out_errors, in_basis_t, out_basis_t)
    if blocks == 2:
        left, term_sent, score_sent = call(
            join_kernel,
            tuple(shape(array.shape, array.dtype) for array in (left, terms[1], score_sum)),
            in_specs=[VMEM] * 2 + [ANY] * 2,
            out_specs=[VMEM] + [ANY] * 2,
            input_output_aliases={2: 1, 3: 2},
        )(left, left_other, terms[1], score_sum)
        scores_of = [score_sent, exchange(score_sent, "mp", n_mp, 1)]
        terms = [terms[0], term_sent]
        term_parts = [terms[0], exchange(term_sent, "mp", n_mp, 1)]

    stats = call(
        functools.partial(table_kernel, blocks),
        shape((head_count, padded + 2 * LANES), F32),
        [pltpu.VMEM((1, features), F32)],
        flops=2 * row_count * features * wide,
        moved=4 << 20,
        in_specs=[VMEM] * (3 * blocks + 2),
        out_specs=VMEM,
    )(*scores_of, *terms, w_in_own, *arrived[:1], gain, index_t)
    if blocks == 2:
        stats = [stats, exchange(stats, "mp", n_mp, 1)]
    else:
        stats = [sum_over(stats, "mp", n_mp)]

    groups = digits(n_dp)
    for group in groups[:0:-1]:
        left = call(
            functools.partial(add_kernel, group[1]),
            shape(left.shape, F32),
            in_specs=[VMEM] * (group[1] + 1),
            out_specs=VMEM,
        )(*partners(left, "dp", n_dp, *group), stats[-1])
    stride, parts = groups[0]
    lefts = partners(left, "dp", n_dp, stride, parts)
    merged = call(
        functools.partial(merge_kernel, 1.0 / n_mp, len(term_parts)),
        shape((row_block, both), F32),
        flops=4 * row_block * both,
        moved=6 << 20,
        in_specs=[VMEM] * (len(term_parts) + 2),
        out_specs=VMEM,
    )(*term_parts, in_errors, out_errors)

    quarter = both // parts
    tiles = quarter // LANES * (rank // TILE_ROWS) + 1
    piece = shape((tiles, TILE_ROWS, LANES), BF16)
    ortho, *pieces = call(
        functools.partial(ortho_kernel, 1.0 / n_dp, len(lefts), len(stats)),
        (shape((2 * rank, row_block), F32),) + (piece,) * parts,
        [pltpu.VMEM((head_count, padded + 2 * LANES), F32)],
        flops=12 * row_block * both * rank,
        moved=3 << 20,
        in_specs=[VMEM] * (len(lefts) + len(stats) + 1),
        out_specs=[VMEM] * (1 + parts),
    )(*lefts, *stats, merged)

    token_grad, flag = call(
        functools.partial(token_kernel, blocks),
        (shape((row_count, features), BF16), shape((SUBLANES, LANES), F32)),
        [
            pltpu.VMEM((row_count, features), F32),
            pltpu.VMEM((row_count, features), BF16),
            pltpu.SemaphoreType.DMA((1,)),
        ],
        flops=2 * row_count * features * wide,
        moved=4 << 20,
        in_specs=[VMEM] * (blocks + 5),
        out_specs=[HBM, VMEM],
    )(packed, w_in_own, *arrived[:1], token_rows, cot_rows, gain, ortho)

    def reduced(values):
        return call(
            reduce_kernel,
            piece,
            in_specs=[VMEM] * (len(values) + 1),
            out_specs=VMEM,
            moved=1 << 18,
        )(*values, flag)

    held = reduced(
        [pieces[0]]
        + [exchange(pieces[step], "dp", n_dp, step * stride) for step in range(1, parts)]
    )
    for group in groups[1:]:
        held = reduced(partners(held, "dp", n_dp, *group))
    pieces = partners(held, "dp", n_dp, stride, parts)

    big = (
        shape((row_block, wide), F32),
        shape((row_block, features), F32),
        shape((row_block, wide), F32),
        shape((row_block, features), F32),
    )
    small = (
        shape((rank, wide), F32),
        shape((rank, features), F32),
        shape((head_count, buckets), F32),
        shape((1, features), F32),
    )
    early, late = (0, parts - 1), tuple(range(parts - 2, 0, -1))

    def staging(steps):
        return [pltpu.VMEM((len(steps), row_block, quarter), F32)] * 2 + [
            pltpu.SemaphoreType.DMA((len(steps), 2))
        ]

    results = call(
        functools.partial(first_kernel, 1.0 / n_dp, early),
        big,
        staging(early),
        flops=24 * row_block * quarter * rank,
        moved=1 << 20,
        in_specs=[VMEM] * (len(early) + 2),
        out_specs=[HBM] * 4,
    )(*(pieces[step] for step in early), ortho, merged)
    in_update, out_update, in_new_error, out_new_error, in_right, out_right, table, gain = call(
        functools.partial(last_kernel, 1.0 / n_dp, 1.0 / (n_dp * n_mp), late, parts),
        big + small,
        [
            pltpu.VMEM((parts, rank, quarter), F32),
            pltpu.VMEM((parts, head_count, 2 * LANES), F32),
        ]
        + buffers(*small)
        + staging(late),
        flops=24 * row_block * quarter * rank,
        moved=1 << 20,
        in_specs=[VMEM] * (parts + 2) + [HBM] * 4,
        out_specs=[HBM] * 8,
        input_output_aliases={2 + parts + at: at for at in range(4)},
    )(*pieces, ortho, merged, *in_hbm(*results))

    return (
        token_grad.reshape(tokens.shape),
        gain.reshape(features),
        table,
        in_update,
        out_update,
        in_new_error[None],
        out_new_error[None],
        jnp.swapaxes(in_right, 0, 1)[None],
        jnp.swapaxes(out_right, 0, 1)[None],
    )


def solution(mesh):
    placed = (
        P(("dp", "mp"), None, None),
        P(("dp", "mp"), None, None),
        P(("dp", "mp"), None),
        P(),
        P(),
        P("mp", None),
        P("mp", None),
        P(),
        P("dp", "mp", None),
        P("dp", "mp", None),
        P("mp", None, None),
        P("mp", None, None),
    )
    return jax.shard_map(
        shards,
        mesh=mesh,
        in_specs=placed,
        out_specs=(
            P(("dp", "mp"), None, None),
            P(),
            P(),
            P("mp", None),
            P("mp", None),
            P("dp", "mp", None),
            P("dp", "mp", None),
            P("mp", None, None),
            P("mp", None, None),
        ),
        check_vma=False,
    )
```

```python
import functools

import jax
import jax.numpy as jnp
from jax import lax
from jax.experimental import pallas as pl
from jax.experimental.pallas import tpu as pltpu
from jax.sharding import PartitionSpec as P

NORM_EPS = 1e-05
BASIS_EPS = 1e-06
MASKED = -1e30
LANES = 128
SUBLANES = 8
READY_HEADS = 2
F32 = jnp.float32
BF16 = jnp.bfloat16

VMEM = pl.BlockSpec(memory_space=pltpu.VMEM)
HBM = pl.BlockSpec(memory_space=pltpu.HBM)
ANY = pl.BlockSpec(memory_space=pl.ANY)


def nn(a, b):
    return lax.dot_general(
        a, b, (((1,), (0,)), ((), ())), preferred_element_type=F32
    )


def nt(a, b):
    return lax.dot_general(
        a, b, (((1,), (1,)), ((), ())), preferred_element_type=F32
    )


def tn(a, b):
    return lax.dot_general(
        a, b, (((0,), (0,)), ((), ())), preferred_element_type=F32
    )


def block_columns(me, step, blocks, width):
    if blocks == 1:
        return pl.ds(0, width)
    index = me if step == 0 else 1 - me
    return pl.ds(pl.multiple_of(index * width, width), width)


def norm_forward(token_rows):
    tokens_wide = token_rows.astype(F32)
    mean_x = jnp.mean(tokens_wide, axis=-1, keepdims=True)
    centered = tokens_wide - mean_x
    variance = jnp.mean(centered * centered, axis=-1, keepdims=True)
    inv_sigma = lax.rsqrt(variance + NORM_EPS)
    return (centered * inv_sigma, inv_sigma)


def fetch(pairs, sems):
    copies = [
        pltpu.make_async_copy(source, target, sems.at[at])
        for at, (source, target) in enumerate(pairs)
    ]
    for copy in copies:
        copy.start()
    return copies


def halves(value):
    coarse = value.astype(BF16)
    return coarse, (value - coarse.astype(F32)).astype(BF16)


def stacked(value):
    return jnp.concatenate(halves(value), axis=0)


def folded(value):
    half = value.shape[0] // 2
    return value[:half] + value[half:]


def gather_bias(bias, heads, table_pad, index_t, index):
    span = index.shape[0]
    padded = table_pad.shape[1]
    even = span // LANES * LANES
    lookups = [(index_t[:, :even], False)] if even else []
    if even < span:
        lookups.append((index[even:, :], True))
    for places, flipped in lookups:
        rows, columns = places.shape
        for start in range(0, columns, LANES):
            stop = min(columns, start + LANES)
            part = places[:, start:stop]
            if stop - start < LANES:
                filler = jnp.zeros((rows, LANES - (stop - start)), jnp.int32)
                part = jnp.concatenate([part, filler], axis=1)
            high, low = part // LANES, part % LANES
            for head in heads:
                found = jnp.zeros((rows, LANES), F32)
                for level in range(padded // LANES):
                    row = table_pad[head : head + 1, level * LANES : (level + 1) * LANES]
                    row = jnp.broadcast_to(row, (rows, LANES))
                    picked = jnp.take_along_axis(row, low, axis=1, mode="promise_in_bounds")
                    found = jnp.where(high == level, picked, found)
                if flipped:
                    bias[head, start:stop, even:] = found[:, : stop - start].T
                else:
                    bias[head, :, start:stop] = found[:, : stop - start]


def prepare_kernel(blocks, ready, *refs):
    sources, rest = refs[:12], refs[12:]
    normed, part, bias, index_t, table_pad, bucket, *kept = rest[:16]
    table, sems = rest[16:]
    copies = fetch(list(zip(sources, [bucket, table] + kept)), sems)
    tokens, gain, w_own = kept[:3]
    me = lax.axis_index("mp")
    width = w_own.shape[0]
    span = bucket.shape[0]
    head_count, padded = table_pad.shape
    for copy in copies[:2]:
        copy.wait()
    table_pad[...] = jnp.zeros_like(table_pad)
    table_pad[:, : table.shape[1]] = table[...]
    index_t[...] = bucket[...].T
    gather_bias(bias, range(ready), table_pad, index_t, bucket)
    for copy in copies[2:5]:
        copy.wait()
    x_hat, _ = norm_forward(tokens[...])
    normed[...] = (x_hat * gain[...]).astype(BF16)
    part[...] = nn(normed[:, block_columns(me, 0, blocks, width)], w_own[...])
    for copy in copies[5:]:
        copy.wait()


def attend_kernel(blocks, share, *refs):
    normed, part, bias_ready, index_t, table_pad, bucket, cot, region = refs[:8]
    own, arrived = refs[8:12], refs[12 : 8 + 4 * blocks]
    rest = refs[8 + 4 * blocks :]
    terms, lefts, rest = rest[:blocks], rest[blocks : 2 * blocks], rest[2 * blocks :]
    score_sum, packed, proj, mixed_grad, mixed, bias = rest
    w_in, w_out, in_basis, out_basis = (
        [own[at]] + list(arrived[at : at + blocks - 1]) for at in range(4)
    )
    me = lax.axis_index("mp")
    window_count, span = region.shape
    features = normed.shape[1]
    ready, head_count = bias_ready.shape[0], bias.shape[0]
    head_size = features // head_count
    scale = head_size ** (-0.5)
    width = features // blocks
    if blocks == 1:
        proj[...] = part[...].astype(BF16)
    else:
        other = nn(normed[:, block_columns(me, 1, blocks, width)], w_in[1][...])
        proj[...] = (part[...] + other).astype(BF16)
    for step in range(blocks):
        mixed_grad[:, block_columns(me, step, blocks, width)] = nt(
            cot[...], w_out[step][...]
        ).astype(BF16)
    lane = lax.broadcasted_iota(jnp.int32, (span, LANES), 1)
    per_group = LANES // head_size
    for window in range(window_count):
        rows = pl.ds(window * span, span)
        ids_row = jnp.broadcast_to(region[window : window + 1, :], (span, span))
        allowed = ids_row == ids_row.T
        for group in range(features // LANES):
            start = group * LANES
            heads = slice(group * per_group, (group + 1) * per_group)
            if heads.stop <= ready:
                pair_bias = bias_ready[heads]
            else:
                if window == 0:
                    gather_bias(bias, range(heads.start, heads.stop), table_pad, index_t, bucket)
                pair_bias = bias[heads]
            q = proj[rows, start : start + LANES]
            k = proj[rows, features + start : features + start + LANES]
            v = proj[rows, 2 * features + start : 2 * features + start + LANES]
            g = mixed_grad[rows, start : start + LANES]
            pick = [lane // head_size == sub for sub in range(per_group)]
            k_split = jnp.concatenate([jnp.where(own, k, jnp.zeros_like(k)) for own in pick], 0)
            v_split = jnp.concatenate([jnp.where(own, v, jnp.zeros_like(v)) for own in pick], 0)
            scores = nt(k_split, q).reshape(per_group, span, span) * scale + pair_bias
            scores = jnp.where(allowed[None], scores, MASKED)
            top = jnp.max(scores, axis=1, keepdims=True)
            raised = jnp.exp(scores - top)
            prob = raised * (1.0 / jnp.sum(raised, axis=1, keepdims=True))
            prob_b = prob.astype(BF16)
            prob_grad = nt(v_split, g).reshape(per_group, span, span)
            inner = jnp.sum(prob * prob_grad, axis=1, keepdims=True)
            score_grad = prob * (prob_grad - inner)
            score_b = score_grad.astype(BF16)
            if window == 0:
                score_sum[heads] = score_grad
            else:
                score_sum[heads] += score_grad
            k_grads = nn(score_b.reshape(per_group * span, span), q)
            v_grads = nn(prob_b.reshape(per_group * span, span), g)

            def joined(parts):
                total = parts[0]
                for sub in range(1, per_group):
                    total = jnp.where(pick[sub], parts[sub], total)
                return total

            k_grad = joined([k_grads[at * span : (at + 1) * span] for at in range(per_group)])
            v_grad = joined([v_grads[at * span : (at + 1) * span] for at in range(per_group)])
            out = joined([tn(prob_b[at], v) for at in range(per_group)])
            q_grad = joined([tn(score_b[at], k) for at in range(per_group)])
            mixed[rows, start : start + LANES] = out.astype(BF16)
            packed[rows, start : start + LANES] = (q_grad * scale).astype(BF16)
            packed[rows, features + start : features + start + LANES] = (k_grad * scale).astype(
                BF16
            )
            packed[rows, 2 * features + start : 2 * features + start + LANES] = v_grad.astype(BF16)
    wide = 3 * features
    for step in range(blocks):
        columns = block_columns(me, step, blocks, width)
        terms[step][:, :wide] = tn(normed[:, columns], packed[...]).astype(BF16)
        terms[step][:, wide:] = tn(mixed[:, columns], cot[...]).astype(BF16)
        rank = in_basis[step].shape[0]
        for basis, at, place in (
            (in_basis[step], slice(None, wide), 0),
            (out_basis[step], slice(wide, None), rank),
        ):
            left = folded(nt(stacked(basis[...]), terms[step][:, at])) * share
            lefts[step][place : place + rank, :] = left


def token_kernel(blocks, packed, *refs):
    w_in, (tokens, cot, gain, _, result, flag, normed_grad, token_grad, sems) = (
        refs[:blocks],
        refs[blocks:],
    )
    me = lax.axis_index("mp")
    width = tokens.shape[1] // blocks
    for step in range(blocks):
        normed_grad[:, block_columns(me, step, blocks, width)] = nt(packed[...], w_in[step][...])
    x_hat, inv_sigma = norm_forward(tokens[...])
    hat_grad = normed_grad[...] * gain[...]
    token_delta = inv_sigma * (
        hat_grad
        - jnp.mean(hat_grad, axis=-1, keepdims=True)
        - x_hat * jnp.mean(hat_grad * x_hat, axis=-1, keepdims=True)
    )
    token_grad[...] = (cot[...].astype(F32) + token_delta).astype(BF16)
    flag[...] = jnp.zeros_like(flag)
    for copy in fetch([(token_grad, result)], sems):
        copy.wait()


def table_kernel(blocks, *refs):
    scores_of, terms = refs[:blocks], refs[blocks : 2 * blocks]
    w_in, rest = refs[2 * blocks : 3 * blocks], refs[3 * blocks :]
    gain, index_t, stats, gain_row = rest
    me = lax.axis_index("mp")
    features = gain.shape[1]
    for step in range(blocks):
        columns = block_columns(me, step, blocks, features // blocks)
        folds = tree_add(
            [
                terms[step][:, at : at + LANES].astype(F32)
                * w_in[step][:, at : at + LANES].astype(F32)
                for at in range(0, w_in[step].shape[1], LANES)
            ]
        )
        gain_row[:, columns] = jnp.sum(folds.T, axis=0, keepdims=True) / gain[:, columns]
    head_count, span, _ = scores_of[0].shape
    rows = span // blocks
    mine = block_columns(me, 0, blocks, rows)
    padded = stats.shape[1] - 2 * LANES
    levels = padded // LANES
    indices = index_t[mine, :]
    scores = tree_add([part[:, mine, :] for part in scores_of])
    sublane = lax.broadcasted_iota(jnp.int32, (LANES, span), 0)
    total = jnp.zeros((2 * levels * head_count, LANES), F32)
    for row in range(rows):
        index = indices[row : row + 1, :]
        high = jnp.broadcast_to(index // LANES, (head_count, span))
        low = jnp.broadcast_to(index % LANES, (LANES, span))
        one_hot = jnp.where(low == sublane, 1.0, 0.0).astype(BF16)
        values = scores[:, row, :]
        coarse = values.astype(BF16).astype(F32)
        fine = values - coarse
        picked = [
            jnp.where(high == level, piece, 0.0)
            for piece in (coarse, fine)
            for level in range(levels)
        ]
        total += nt(jnp.concatenate(picked, axis=0).astype(BF16), one_hot)
    total = folded(total)
    for level in range(levels):
        stats[:, level * LANES : (level + 1) * LANES] = total[
            level * head_count : (level + 1) * head_count
        ]
    stats[:, padded:] = jnp.zeros((head_count, 2 * LANES), F32)
    for piece in range(features // LANES):
        stats[piece : piece + 1, padded : padded + LANES] = gain_row[
            :, piece * LANES : (piece + 1) * LANES
        ]


def shard_kernel(share, shard, in_basis, out_basis, left):
    rank, split = in_basis.shape
    left[:rank, :] = folded(nt(stacked(in_basis[...]), shard[:, :split])) * share
    left[rank:, :] = folded(nt(stacked(out_basis[...]), shard[:, split:])) * share


def error_kernel(term_left, in_error, out_error, in_basis, out_basis, left):
    rank = in_basis.shape[0]
    for error, basis, at in ((in_error, in_basis, 0), (out_error, out_basis, rank)):
        coarse, fine = halves(error[...])
        pair = stacked(basis[...])
        left[at : at + rank, :] = term_left[at : at + rank, :] + folded(
            nt(pair, coarse) + nt(pair, fine)
        )


def merge_kernel(share, parts, *refs):
    shards, (in_error, out_error, merged) = refs[:parts], refs[parts:]
    split = in_error.shape[1]
    for columns, error in ((slice(None, split), in_error), (slice(split, None), out_error)):
        total = tree_add([shard[:, columns].astype(F32) for shard in shards])
        merged[:, columns] = total * share + error[...]


def tree_sum(values):
    while len(values) > 1:
        values = [values[at] + values[at + 1] for at in range(0, len(values), 2)]
    return values[0]


def tree_add(values):
    while len(values) > 1:
        odd = values[len(values) // 2 * 2 :]
        values = [values[at] + values[at + 1] for at in range(0, len(values) - 1, 2)] + odd
    return values[0]


def join_kernel(left_own, left_other, *refs):
    left = refs[len(refs) // 2]
    left[...] = left_own[...] + left_other[...]


def add_kernel(parts, *refs):
    refs[-1][...] = tree_sum([ref[...] for ref in refs[:parts]])


def stats_pieces(pair):
    pieces = []
    for at in range(2):
        tile = pair[:, at * LANES : (at + 1) * LANES]
        coarse, fine = halves(tile)
        pieces += [coarse.astype(F32), fine.astype(F32)]
    return jnp.concatenate(pieces, axis=0).astype(BF16)


def stats_pair(pieces):
    rows = pieces.shape[0] // 4
    return jnp.concatenate(
        [
            pieces[2 * at * rows : (2 * at + 1) * rows]
            + pieces[(2 * at + 1) * rows : (2 * at + 2) * rows]
            for at in range(2)
        ],
        axis=1,
    )


def orthonormal(problems):
    rank, rows = problems[0].shape
    tiles = rank // SUBLANES
    spread_shape = (SUBLANES, rows)
    place = lax.broadcasted_iota(jnp.int32, spread_shape, 0)

    def dots(rows_of, vector):
        return jnp.sum(rows_of * vector, axis=1, keepdims=True)

    def spread(tiled, row):
        tile, at = divmod(row, SUBLANES)
        return jnp.broadcast_to(tiled[tile][at : at + 1], spread_shape)

    states = []
    for first in problems:
        original = [first[at * SUBLANES : (at + 1) * SUBLANES] for at in range(tiles)]
        states.append((original, list(original), [jnp.zeros(spread_shape, F32)] * tiles))
    def project(finished, found):
        weighted = tree_add([found[q] * finished[q] for q in found])
        return jnp.sum(weighted, axis=0, keepdims=True)

    currents = [spread(original, 0) for original, _, _ in states]
    known = [None for _ in states]
    for column in range(rank):
        tile, at = divmod(column, SUBLANES)
        before = range((column - 1) // SUBLANES + 1)
        for which, (original, residual, finished) in enumerate(states):
            current = currents[which]
            square = dots(current, current)
            inverse = lax.rsqrt(square + BASIS_EPS)
            unit = current * inverse
            if column + 1 < rank:
                ahead = spread(residual, column + 1)
                next_tile, next_at = divmod(column + 1, SUBLANES)
                found = {q: dots(original[q], current) * inverse for q in range(next_tile, tiles)}
                step = found[next_tile][next_at : next_at + 1]
                own = dots(ahead, current) * inverse
                following = ahead - unit * (step + own - step * (square * inverse * inverse))
                if column:
                    cross = project(finished, {q: dots(finished[q], current) for q in before})
                    following = following - known[which] + (step * inverse) * cross
            finished[tile] = jnp.where(place == at, unit, finished[tile])
            if column + 1 < rank:
                for q in found:
                    residual[q] = residual[q] - found[q] * unit
                currents[which] = following
            if column + 2 < rank:
                far = spread(residual, column + 2)
                known[which] = project(
                    finished, {q: dots(finished[q], far) for q in range(tile + 1)}
                )
    return [jnp.concatenate(finished, axis=0) for _, _, finished in states]


def ortho_kernel(share, parts, stat_parts, *refs):
    lefts, stats = refs[:parts], refs[parts : parts + stat_parts]
    merged, ortho, *pieces, sums = refs[parts + stat_parts :]
    digit = lax.axis_index("dp") % 4
    rank = ortho.shape[0] // 2
    quarter = merged.shape[1] // len(pieces)
    sums[...] = tree_sum([stat[...] for stat in stats])
    total = tree_sum([left[...] for left in lefts]) * share
    finished = orthonormal([total[:rank], total[rank:]])
    ortho[:rank, :], ortho[rank:, :] = finished
    for step, piece in enumerate(pieces):
        block = jnp.bitwise_xor(digit, step)
        columns = pl.ds(pl.multiple_of(block * quarter, quarter), quarter)
        pair = stacked(jnp.where(block < len(pieces) - 1, finished[0], finished[1]))
        piece[:, :quarter] = folded(nn(pair, merged[:, columns].astype(BF16))).astype(BF16)
        stat_columns = pl.ds(pl.multiple_of(block * 2 * LANES, 2 * LANES), 2 * LANES)
        piece[:, quarter:] = stats_pieces(sums[:, stat_columns])


def reduce_kernel(*refs):
    pieces, total = refs[:-2], refs[-1]
    quarter = total.shape[1] - LANES
    summed = tree_sum([piece[...].astype(F32) for piece in pieces])
    total[:, :quarter] = summed[:, :quarter].astype(BF16)
    total[:, quarter:] = stats_pieces(stats_pair(summed[:, quarter:]))


def update_blocks(share, steps, pieces, ortho, merged, results, updates, errors, sems, small):
    in_update, out_update, in_new_error, out_new_error = results
    rank = ortho.shape[0] // 2
    quarter = updates.shape[2]
    count = merged.shape[1] // quarter
    places = []
    for at, step in enumerate(steps):
        block = jnp.bitwise_xor(lax.axis_index("dp") % 4, step)
        columns = pl.ds(pl.multiple_of(block * quarter, quarter), quarter)
        right = pieces[step][:, :quarter].astype(F32) * share
        own_coarse, own_fine = halves(
            jnp.where(block < count - 1, ortho[:rank, :], ortho[rank:, :])
        )
        coarse, fine = halves(right)
        update = tn(
            jnp.concatenate([own_coarse, own_coarse, own_fine], axis=0),
            jnp.concatenate([coarse, fine, coarse], axis=0),
        )
        updates[at] = update
        errors[at] = merged[:, columns] - update
        places.append((block, columns))

        @pl.when(block < count - 1)
        def _():
            targets = in_update.at[:, columns], in_new_error.at[:, columns]
            fetch(list(zip((updates.at[at], errors.at[at]), targets)), sems.at[at])

        @pl.when(block == count - 1)
        def _():
            targets = out_update, out_new_error
            fetch(list(zip((updates.at[at], errors.at[at]), targets)), sems.at[at])

    small()
    for at, (block, columns) in enumerate(places):
        pltpu.make_async_copy(updates.at[at], out_update, sems.at[at, 0]).wait()
        pltpu.make_async_copy(errors.at[at], out_new_error, sems.at[at, 1]).wait()


def first_kernel(share, steps, *refs):
    count = len(steps)
    pieces = dict(zip(steps, refs[:count]))
    ortho, merged = refs[count : count + 2]
    results, (updates, errors, sems) = refs[count + 2 : count + 6], refs[count + 6 :]
    update_blocks(share, steps, pieces, ortho, merged, results, updates, errors, sems, lambda: None)


def last_kernel(share, stat_share, steps, parts, *refs):
    pieces, (ortho, merged) = refs[:parts], refs[parts : parts + 2]
    results, small_results = refs[parts + 6 : parts + 10], refs[parts + 10 : parts + 14]
    rights, *small = refs[parts + 14 : parts + 19]
    small_sems, updates, errors, sems = refs[parts + 19 :]
    in_basis, out_basis, table, gain = small
    quarter = rights.shape[2] - LANES
    copies = []

    def small_outputs():
        for step, piece in enumerate(pieces):
            rights[step] = piece[...].astype(F32)
        tiles = []
        for block in range(parts):
            here = rights[jnp.bitwise_xor(lax.axis_index("dp") % 4, block)]
            right = here[:, :quarter] * share
            tiles.append(stats_pair(here[:, quarter:]) * stat_share)
            if block < parts - 1:
                in_basis[:, block * quarter : (block + 1) * quarter] = right
            else:
                out_basis[...] = right
        stats = jnp.concatenate(tiles, axis=1)
        table[...] = stats[:, : table.shape[1]]
        padded = stats.shape[1] - 2 * LANES
        for at in range(gain.shape[1] // LANES):
            gain[:, at * LANES : (at + 1) * LANES] = stats[at : at + 1, padded : padded + LANES]
        copies.extend(fetch(list(zip(small, small_results)), small_sems))

    update_blocks(
        share, steps, pieces, ortho, merged, results, updates, errors, sems, small_outputs
    )
    for copy in copies:
        copy.wait()


def call(kernel, outs, scratch=(), flops=0, moved=0, vmem=16, **options):
    return pl.pallas_call(
        kernel,
        out_shape=outs,
        scratch_shapes=list(scratch),
        cost_estimate=pl.CostEstimate(flops=flops, bytes_accessed=moved, transcendentals=0),
        compiler_params=pltpu.CompilerParams(vmem_limit_bytes=vmem << 20),
        **options,
    )


def buffers(*arrays):
    return [pltpu.VMEM(array.shape, array.dtype) for array in arrays] + [
        pltpu.SemaphoreType.DMA((len(arrays),))
    ]


def in_hbm(*arrays):
    return [pltpu.with_memory_space_constraint(array, pltpu.HBM) for array in arrays]


def shape(dims, dtype):
    return jax.ShapeDtypeStruct(dims, dtype)


def exchange(value, axis, count, distance):
    return lax.ppermute(value, axis, [(at, at ^ distance) for at in range(count)])


def digits(count):
    groups, stride = [], 1
    while stride < count:
        size = 4 if count // stride % 4 == 0 else 2
        groups.append((stride, size))
        stride *= size
    return groups


def partners(value, axis, count, stride, size):
    return [value] + [exchange(value, axis, count, step * stride) for step in range(1, size)]


def sum_over(value, axis, count):
    for stride, size in digits(count):
        value = tree_sum(partners(value, axis, count, stride, size))
    return value


def shards(
    tokens,
    cotangent,
    region_ids,
    rel_bucket,
    norm_gain,
    in_weight,
    out_weight,
    bias_table,
    in_error,
    out_error,
    in_basis,
    out_basis,
):
    n_dp = lax.axis_size("dp")
    n_mp = lax.axis_size("mp")
    window_count, span, features = tokens.shape
    head_count, buckets = bias_table.shape
    rank = in_basis.shape[2]
    row_count = window_count * span
    row_block = in_weight.shape[0]
    wide = in_weight.shape[1]
    both = wide + features
    padded = -(-buckets // LANES) * LANES
    blocks = 2 if n_mp == 2 else 1
    token_rows = tokens.reshape(row_count, features)
    cot_rows = cotangent.reshape(row_count, features)
    gain = norm_gain.reshape(1, features)

    in_basis_t = jnp.swapaxes(in_basis[0], 0, 1)
    out_basis_t = jnp.swapaxes(out_basis[0], 0, 1)
    if blocks == 2:
        own = (in_weight, out_weight, in_basis_t, out_basis_t)
        arrived = [exchange(array, "mp", n_mp, 1) for array in own]
    else:
        own = (
            lax.all_gather(in_weight, "mp", axis=0, tiled=True),
            lax.all_gather(out_weight, "mp", axis=0, tiled=True),
            in_basis_t,
            out_basis_t,
        )
        arrived = []
    width = features // blocks

    operands = (
        rel_bucket,
        bias_table,
        token_rows,
        gain,
        own[0],
        cot_rows,
        region_ids,
        *own[1:],
        in_error[0],
        out_error[0],
    )
    normed, part, bias, index_t, table_pad, bucket, *kept = call(
        functools.partial(prepare_kernel, blocks, READY_HEADS),
        (
            shape((row_count, features), BF16),
            shape((row_count, wide), F32),
            shape((READY_HEADS, span, span), F32),
            shape((span, span), jnp.int32),
            shape((head_count, padded), F32),
            shape((span, span), jnp.int32),
        )
        + tuple(shape(array.shape, array.dtype) for array in operands[2:]),
        [pltpu.VMEM(bias_table.shape, F32), pltpu.SemaphoreType.DMA((12,))],
        flops=2 * row_count * width * wide,
        moved=4 << 20,
        in_specs=[HBM] * 12,
        out_specs=[VMEM] * 16,
    )(*in_hbm(*operands))
    token_rows, gain, w_in_own, cot_rows, region, *own, in_errors, out_errors = kept
    in_basis_t, out_basis_t = own[1:]

    left_shape = shape((2 * rank, width), F32)
    outputs = call(
        functools.partial(attend_kernel, blocks, 1.0 / n_mp),
        (shape((width, both), BF16),) * blocks
        + (left_shape,) * blocks
        + (shape((head_count, span, span), F32), shape((row_count, wide), BF16)),
        [
            pltpu.VMEM((row_count, wide), BF16),
            pltpu.VMEM((row_count, features), BF16),
            pltpu.VMEM((row_count, features), BF16),
            pltpu.VMEM((head_count, span, span), F32),
        ],
        flops=4 * row_count * features * both,
        moved=8 << 20,
        in_specs=[VMEM] * (12 + len(arrived)),
        out_specs=[VMEM] * (2 * blocks + 2),
    )(normed, part, bias, index_t, table_pad, bucket, cot_rows, region, w_in_own, *own, *arrived)
    *outputs, score_sum, packed = outputs
    terms, lefts = outputs[:blocks], outputs[blocks:]
    scores_of = [score_sum]

    if blocks == 2:
        left_other = exchange(lefts[1], "mp", n_mp, 1)
        left = lefts[0]
    else:
        term_parts = [lax.psum_scatter(terms[0], "mp", scatter_dimension=0, tiled=True)]
        left = call(
            functools.partial(shard_kernel, 1.0 / n_mp),
            shape((2 * rank, row_block), F32),
            in_specs=[VMEM] * 3,
            out_specs=VMEM,
        )(term_parts[0], in_basis_t, out_basis_t)

    left = call(
        error_kernel,
        shape((2 * rank, row_block), F32),
        flops=8 * row_block * both * rank,
        moved=3 << 20,
        in_specs=[VMEM] * 5,
        out_specs=VMEM,
    )(left, in_errors, out_errors, in_basis_t, out_basis_t)
    if blocks == 2:
        left, term_sent, score_sent = call(
            join_kernel,
            tuple(shape(array.shape, array.dtype) for array in (left, terms[1], score_sum)),
            in_specs=[VMEM] * 2 + [ANY] * 2,
            out_specs=[VMEM] + [ANY] * 2,
            input_output_aliases={2: 1, 3: 2},
        )(left, left_other, terms[1], score_sum)
        scores_of = [score_sent, exchange(score_sent, "mp", n_mp, 1)]
        terms = [terms[0], term_sent]
        term_parts = [terms[0], exchange(term_sent, "mp", n_mp, 1)]

    stats = call(
        functools.partial(table_kernel, blocks),
        shape((head_count, padded + 2 * LANES), F32),
        [pltpu.VMEM((1, features), F32)],
        flops=2 * row_count * features * wide,
        moved=4 << 20,
        in_specs=[VMEM] * (3 * blocks + 2),
        out_specs=VMEM,
    )(*scores_of, *terms, w_in_own, *arrived[:1], gain, index_t)
    if blocks == 2:
        stats = [stats, exchange(stats, "mp", n_mp, 1)]
    else:
        stats = [sum_over(stats, "mp", n_mp)]

    groups = digits(n_dp)
    for group in groups[:0:-1]:
        left = call(
            functools.partial(add_kernel, group[1]),
            shape(left.shape, F32),
            in_specs=[VMEM] * (group[1] + 1),
            out_specs=VMEM,
        )(*partners(left, "dp", n_dp, *group), stats[-1])
    stride, parts = groups[0]
    lefts = partners(left, "dp", n_dp, stride, parts)
    merged = call(
        functools.partial(merge_kernel, 1.0 / n_mp, len(term_parts)),
        shape((row_block, both), F32),
        flops=4 * row_block * both,
        moved=6 << 20,
        in_specs=[VMEM] * (len(term_parts) + 2),
        out_specs=VMEM,
    )(*term_parts, in_errors, out_errors)

    quarter = both // parts
    piece = shape((rank, quarter + LANES), BF16)
    ortho, *pieces = call(
        functools.partial(ortho_kernel, 1.0 / n_dp, len(lefts), len(stats)),
        (shape((2 * rank, row_block), F32),) + (piece,) * parts,
        [pltpu.VMEM((head_count, padded + 2 * LANES), F32)],
        flops=12 * row_block * both * rank,
        moved=3 << 20,
        in_specs=[VMEM] * (len(lefts) + len(stats) + 1),
        out_specs=[VMEM] * (1 + parts),
    )(*lefts, *stats, merged)

    token_grad, flag = call(
        functools.partial(token_kernel, blocks),
        (shape((row_count, features), BF16), shape((SUBLANES, LANES), F32)),
        [
            pltpu.VMEM((row_count, features), F32),
            pltpu.VMEM((row_count, features), BF16),
            pltpu.SemaphoreType.DMA((1,)),
        ],
        flops=2 * row_count * features * wide,
        moved=4 << 20,
        in_specs=[VMEM] * (blocks + 5),
        out_specs=[HBM, VMEM],
    )(packed, w_in_own, *arrived[:1], token_rows, cot_rows, gain, ortho)

    def reduced(values):
        return call(
            reduce_kernel,
            piece,
            in_specs=[VMEM] * (len(values) + 1),
            out_specs=VMEM,
            moved=1 << 18,
        )(*values, flag)

    held = reduced(
        [pieces[0]]
        + [exchange(pieces[step], "dp", n_dp, step * stride) for step in range(1, parts)]
    )
    for group in groups[1:]:
        held = reduced(partners(held, "dp", n_dp, *group))
    pieces = partners(held, "dp", n_dp, stride, parts)

    big = (
        shape((row_block, wide), F32),
        shape((row_block, features), F32),
        shape((row_block, wide), F32),
        shape((row_block, features), F32),
    )
    small = (
        shape((rank, wide), F32),
        shape((rank, features), F32),
        shape((head_count, buckets), F32),
        shape((1, features), F32),
    )
    early, late = (0, parts - 1), tuple(range(parts - 2, 0, -1))

    def staging(steps):
        return [pltpu.VMEM((len(steps), row_block, quarter), F32)] * 2 + [
            pltpu.SemaphoreType.DMA((len(steps), 2))
        ]

    results = call(
        functools.partial(first_kernel, 1.0 / n_dp, early),
        big,
        staging(early),
        flops=24 * row_block * quarter * rank,
        moved=1 << 20,
        in_specs=[VMEM] * (len(early) + 2),
        out_specs=[HBM] * 4,
    )(*(pieces[step] for step in early), ortho, merged)
    in_update, out_update, in_new_error, out_new_error, in_right, out_right, table, gain = call(
        functools.partial(last_kernel, 1.0 / n_dp, 1.0 / (n_dp * n_mp), late, parts),
        big + small,
        [pltpu.VMEM((parts, rank, quarter + LANES), F32)] + buffers(*small) + staging(late),
        flops=24 * row_block * quarter * rank,
        moved=1 << 20,
        in_specs=[VMEM] * (parts + 2) + [HBM] * 4,
        out_specs=[HBM] * 8,
        input_output_aliases={2 + parts + at: at for at in range(4)},
    )(*pieces, ortho, merged, *in_hbm(*results))

    return (
        token_grad.reshape(tokens.shape),
        gain.reshape(features),
        table,
        in_update,
        out_update,
        in_new_error[None],
        out_new_error[None],
        jnp.swapaxes(in_right, 0, 1)[None],
        jnp.swapaxes(out_right, 0, 1)[None],
    )


def solution(mesh):
    placed = (
        P(("dp", "mp"), None, None),
        P(("dp", "mp"), None, None),
        P(("dp", "mp"), None),
        P(),
        P(),
        P("mp", None),
        P("mp", None),
        P(),
        P("dp", "mp", None),
        P("dp", "mp", None),
        P("mp", None, None),
        P("mp", None, None),
    )
    return jax.shard_map(
        shards,
        mesh=mesh,
        in_specs=placed,
        out_specs=(
            P(("dp", "mp"), None, None),
            P(),
            P(),
            P("mp", None),
            P("mp", None),
            P("dp", "mp", None),
            P("dp", "mp", None),
            P("mp", None, None),
            P("mp", None, None),
        ),
        check_vma=False,
    )
```
